128 devices in a mesh: lat: 32 (over y, x, core), lev: 4 (over z).
Axes of the slice: x: 4, y: 4, z: 4, core: 2. Of those that a mesh axis runs over, the one named last changes fastest.
Arguments:
- control: float32 [4, 32, 768, 1536], P(None, 'lev', 'lat'), may hold values from -0.3 to 0.3
- obs_values: float32 [262144, 128], P(('lat', 'lev')), may hold values from -12 to 20
- obs_owner: int32 [262144, 1], P(('lat', 'lev')), may hold values from 0 to 127; in each aligned block of 2048 rows (0 to 2047, 2048 to 4095, ...) at most 32 rows name the same one
- obs_column: int32 [262144], P(('lat', 'lev')), may hold values from 0 to 9215
- sigma: float32 [4, 32, 768], replicated, may hold values from 0.5 to 2
- len_lon: float32 [4, 32], P(None, 'lev'), may hold values from 1.5 to 300
- len_lat: float32 [4, 32], P(None, 'lev'), may hold values from 1.5 to 150
- len_lev: float32 [4, 768], replicated, may hold values from 0.7 to 8
Outputs:
- gradient: float32 [4, 32, 768, 1536], P(None, 'lev', 'lat')
The draws below stay inside these ranges and needn't reach their ends.
Inputs may be any that keep to these rules, and one draw needn't show every extreme that they name: `obs_owner`: the rows of one device name one owner at most 32 times; in every draw some device names some owner exactly 32 times.
All inputs are finite; a program needn't handle non-finite values.
Results may differ from the reference program's by a relative error of at most 0.0003.
Values sent between devices are 32-bit elements; how exact they have to be, the bound alone decides.
No kernel may reach another device: no remote copies, remote signals or barrier semaphores. Data moves between devices by JAX's collectives and lax.ppermute only.
A program may use at most 128 MiB of HBM per device.

```python
import math
import jax
import jax.numpy as jnp
import numpy as np
from jax import lax

F = 4
NLEV = 32
NLAT = 768
NLON = 1536
BLK = 128
OBS_DEV = 2048
ROW = 128
CAP = 32
COLS_OWN = 9216
OBS_TOTAL = 262144
N_LAT = 32
N_LEV = 4
DEVICES = 128


def draw_obs_values(key, part):
    key = jax.random.fold_in(key, 11)
    key_level, key_sign, key_noise = jax.random.split(key, 3)
    level = jax.random.uniform(key_level, (1, ROW), jnp.float32, 1.0, 3.0)
    signs = jnp.where(jax.random.bernoulli(key_sign, 0.5, (1, ROW)), 1.0, -1.0).astype(jnp.float32)
    noise = jnp.clip(3.0 * jax.random.normal(key_noise, (OBS_TOTAL, ROW), jnp.float32), -9.0, 9.0)
    return (level * signs + noise).astype(jnp.float32)


def set_ends(drawn, own_key, low, largest):
    longest = drawn.shape.index(max(drawn.shape))
    spots = []
    for shift in (0, 1):
        where = [jax.random.randint(jax.random.fold_in(own_key, axis), (), 0, length) for axis, length in enumerate(drawn.shape)]
        where[longest] = (where[longest] + shift) % drawn.shape[longest]
        spots.append(tuple(where))
    return drawn.at[spots[0]].set(low).at[spots[1]].set(largest)


def shard_levels(stream_key, extent, pieces, smallest, high):
    def one(position, blocks):
        draws = jax.random.uniform(jax.random.fold_in(jax.random.fold_in(stream_key, 6), position), (blocks,), jnp.float32, smallest / len(pieces), high / len(pieces))
        return jnp.repeat(jnp.exp(draws), extent[position] // blocks).reshape((-1,) + (1,) * (len(extent) - position - 1))

    factor_of = one(*pieces[0])
    for cut in pieces[1:]:
        factor_of = factor_of * one(*cut)
    return factor_of


def deal_out(stream_key, own, number, rows, number_of, top, most, lean):
    sequence = jax.random.permutation(stream_key, number_of)
    crowded, usual = portions_of(number_of, rows * top, most, lean, True), portions_of(number_of, rows * top, most, lean, False)
    places = jnp.arange(number_of)

    def named(tallies, rotation):
        used = int((tallies > 0).sum())
        fixed = max(1, used // 4)
        shifted = fixed + (places - fixed + rotation * (used - fixed)) % max(1, number_of - fixed)
        return jnp.zeros((number_of,), jnp.int32).at[sequence[jnp.where(places < fixed, places, shifted)]].set(jnp.asarray(tallies, jnp.int32))

    tallies = jnp.where(number % 4 == 0, named(crowded, number // 4), named(usual, number - number // 4 - 1))
    mixed = jax.random.permutation(jax.random.fold_in(own, 3), number_of)
    donor, receiver = mixed[0:number_of // 2 * 2:2], mixed[1:number_of // 2 * 2:2]
    margin = jnp.minimum(tallies[donor] - 1, most - tallies[receiver]) // 2
    margin = jnp.where((donor == sequence[0]) | (receiver == sequence[0]) | (tallies[receiver] == 0), 0, jnp.maximum(margin, 0))
    shifted = jax.random.randint(jax.random.fold_in(own, 4), (number_of // 2,), 0, 1 << 20) % (margin + 1)
    tallies = tallies.at[donor].add(-shifted).at[receiver].add(shifted)
    members = jnp.searchsorted(jnp.cumsum(tallies), jnp.arange(rows * top), side="right").astype(jnp.int32)
    listing = members.reshape(top, rows).T
    listing = listing[jax.random.permutation(jax.random.fold_in(own, 1), rows)]
    rotation = jax.random.randint(jax.random.fold_in(own, 2), (rows, 1), 0, top)
    return jnp.take_along_axis(listing, (jnp.arange(top)[None, :] + rotation) % top, axis=1)


def portions_of(amount, total, reach, slope, full):
    weights = [(1 << 20) // math.isqrt(rank ** slope) + 1 for rank in range(1, amount + 1)]
    largest = reach if full else min(reach, max(-(-total // amount), total * weights[0] // sum(weights)))
    least = 1 if total - largest >= amount - 1 else 0
    holding, spare = [largest] + [least] * (amount - 1), total - largest - least * (amount - 1)
    while spare > 0:
        free = [i for i in range(1, amount) if holding[i] < largest] or [i for i in range(1, amount) if holding[i] < reach]
        pool, budget = sum([weights[i] for i in free]), spare
        for i in free:
            extra = min(reach - holding[i], max(1, budget * weights[i] // pool), spare)
            holding[i] = holding[i] + extra
            spare = spare - extra
    return np.array(holding)


def gaussian(key, extent, scale, limit, pieces=(), held_as=jnp.bfloat16):
    level = shard_levels(key, extent, pieces, -0.22, 0.18) if pieces else 1.0
    drawn = jax.random.normal(key, extent, jnp.float32) * scale * level
    return jnp.minimum(jnp.maximum(drawn, -limit), limit).astype(held_as)


def setup_inputs(seed: int = 0) -> dict:
    streams_of = jax.random.split(jax.random.key(seed), 9)
    control = gaussian(streams_of[0], (F, NLEV, NLAT, NLON), 0.05, 0.3, ((1, 4), (2, 32)), jnp.float32)
    obs_values = draw_obs_values(jax.random.fold_in(streams_of[8], 71), 0)
    obs_owner_keys = jax.random.split(jax.random.fold_in(streams_of[2], 1), OBS_TOTAL // OBS_DEV)
    obs_owner_turns = jax.random.permutation(jax.random.fold_in(streams_of[2], 3), OBS_TOTAL // OBS_DEV)
    obs_owner = jax.vmap(lambda own, number: deal_out(jax.random.fold_in(streams_of[2], 2), own, number, OBS_DEV, DEVICES, 1, CAP, 2))(obs_owner_keys, obs_owner_turns).reshape((OBS_TOTAL, 1))
    obs_column = set_ends(jax.random.randint(streams_of[3], (OBS_TOTAL,), 0, COLS_OWN), jax.random.fold_in(streams_of[3], 1), 0, COLS_OWN - 1).astype(jnp.int32)
    sigma = jnp.clip(jnp.exp(jax.random.uniform(streams_of[4], (F, NLEV, NLAT), jnp.float32, math.log(0.5), math.log(2.0))), 0.5, 2.0)
    len_lon = jnp.clip(jnp.exp(math.log(300.0) - 5.2983174 * jax.random.uniform(streams_of[5], (F, NLEV), jnp.float32) ** shard_levels(streams_of[5], (F, NLEV), ((1, 4),), -0.2, 0.2)), 1.5, 300.0)
    len_lat = jnp.clip(jnp.exp(math.log(150.0) - 4.6051702 * jax.random.uniform(streams_of[6], (F, NLEV), jnp.float32) ** shard_levels(streams_of[6], (F, NLEV), ((1, 4),), -0.2, 0.2)), 1.5, 150.0)
    len_lev = jnp.clip(jnp.exp(jax.random.uniform(streams_of[7], (F, NLAT), jnp.float32, math.log(0.7), math.log(8.0))), 0.7, 8.0)
    return {"control": control, "obs_values": obs_values, "obs_owner": obs_owner, "obs_column": obs_column, "sigma": sigma, "len_lon": len_lon, "len_lat": len_lat, "len_lev": len_lev}


precise_mode = lax.Precision.HIGHEST


def tri_matrix(scale, size):
    index_range = jnp.arange(size, dtype=jnp.int32)
    offset = (index_range[:, None] - index_range[None, :]).astype(jnp.float32)
    length = scale[..., None, None]
    decay = jnp.exp(-1.0 / length)
    return jnp.where(offset >= 0, (1.0 - decay) * jnp.exp(-jnp.maximum(offset, 0.0) / length), 0.0)


def carry_matrix(scale, blocks, periodic):
    index_range = jnp.arange(blocks, dtype=jnp.int32)
    offset = index_range[:, None] - 1 - index_range[None, :]
    length = scale[..., None, None]
    if periodic:
        spans = (offset % blocks).astype(jnp.float32) * BLK
        return jnp.exp(-spans / length) / (1.0 - jnp.exp(-(blocks * BLK) / length))
    spans = jnp.maximum(offset, 0).astype(jnp.float32) * BLK
    return jnp.where(offset >= 0, jnp.exp(-spans / length), 0.0)


def one_sweep(field, scale, axis, periodic, backward):
    shape = field.shape
    blocks = shape[axis] // BLK
    within = tri_matrix(scale, BLK)
    across = carry_matrix(scale, blocks, periodic)
    steps_in = (jnp.arange(BLK, dtype=jnp.int32) + 1).astype(jnp.float32)
    ramp = jnp.exp(-steps_in / scale[..., None])
    edge = BLK - 1
    if backward:
        within = jnp.swapaxes(within, 2, 3)
        across = jnp.swapaxes(across, 2, 3)
        ramp = ramp[..., ::-1]
        edge = 0
    if axis == 3:
        blocked = field.reshape(shape[0], shape[1], shape[2], blocks, BLK)
        local = jnp.einsum("flpbk,flik->flpbi", blocked, within, precision=precise_mode)
        carry = jnp.einsum("flpc,flbc->flpb", local[..., edge], across, precision=precise_mode)
        result = local + carry[..., None] * ramp[:, :, None, None, :]
    else:
        blocked = field.reshape(shape[0], shape[1], blocks, BLK, shape[3])
        local = jnp.einsum("flbkq,flik->flbiq", blocked, within, precision=precise_mode)
        carry = jnp.einsum("flcq,flbc->flbq", local[:, :, :, edge, :], across, precision=precise_mode)
        result = local + carry[:, :, :, None, :] * ramp[:, :, None, :, None]
    return result.reshape(shape)


def smooth(field, scale, axis, periodic):
    return one_sweep(one_sweep(field, scale, axis, periodic, False), scale, axis, periodic, True)


def level_filter(field, scale):
    lower = tri_matrix(scale, field.shape[1])
    once = jnp.einsum("fkao,faik->fiao", field, lower, precision=precise_mode)
    return jnp.einsum("fkao,faki->fiao", once, lower, precision=precise_mode)


def reference(control, obs_values, obs_owner, obs_column, sigma, len_lon, len_lat, len_lev):
    lat_own = NLAT // N_LEV
    lon_own = NLON // N_LAT
    owner = obs_owner[:, 0]
    latitude = ((owner % N_LEV) * lat_own + obs_column // lon_own).astype(jnp.int32)
    longitude = ((owner // N_LEV) * lon_own + obs_column % lon_own).astype(jnp.int32)
    profiles = jnp.transpose(obs_values.reshape(-1, F, NLEV), (1, 2, 0))

    def per_field(inputs):
        values, weights, scale_lon, scale_lat, scale_lev = inputs
        grid = jnp.zeros((NLEV, NLAT, NLON), values.dtype).at[:, latitude, longitude].add(values)
        grid = (grid * weights[:, :, None])[None]
        grid = level_filter(grid, scale_lev[None])
        grid = smooth(grid, scale_lat[None], 2, False)
        grid = smooth(grid, scale_lon[None], 3, True)
        return grid[0]

    return control + lax.map(per_field, (profiles, sigma, len_lon, len_lat, len_lev))
```

```python
import functools

import jax
import jax.numpy as jnp
from jax import lax
from jax.experimental import pallas as pl
from jax.experimental.pallas import tpu as pltpu
from jax.sharding import PartitionSpec as P

F = 4
NLEV = 32
NLAT = 768
NLON = 1536
BANDS = 32
LEVS = 4
BAND = NLAT // BANDS
LEVQ = NLEV // LEVS
PROF = F * LEVQ
GROUP = 128 // PROF
ROWS = 32
CAP = (ROWS - 1) * GROUP
COUNT_LANE = 124
MOST_LANE = 125
STEP = 64
SEGV = 3
TILES = BAND // GROUP
PLANE = NLON
PAD = 8
GRID_ROWS = BAND * PLANE + PAD
VMEM_LIMIT = 60 * 1024 * 1024


def third(x):
    return (x * 21846) >> 16


def blocks_of(shape):
    return lax.broadcasted_iota(jnp.int32, shape, len(shape) - 1) // PROF


def send_kernel(turn, vals, owner, column, sigma, len_lev, out, xs, ax, table, decay, places, place_s, sem):
    rows = vals.shape[0]
    turn_no = turn[0]
    zeros = jnp.zeros((64, 128), jnp.float32)

    def clear(i, _):
        at = pl.ds(pl.multiple_of(i * 64, 64), 64)
        xs[at, :] = zeros
        ax[at, :] = zeros
        return 0

    d = owner[...]
    c = column[...]
    c48 = third(c >> 4)
    lat = (d & 3) * 192 + c48
    lon = (d >> 2) * 48 + (c - c48 * 48)
    band = third(lat >> 3)
    seg = lon >> 6
    grid_row = ((seg >> 3) * STEP + (lon & (STEP - 1))) * 8 + (seg & 7)
    address = (lat - band * BAND) * PLANE + grid_row + PAD

    width = 256
    r0 = lax.broadcasted_iota(jnp.int32, (width, width), 0)
    r1 = lax.broadcasted_iota(jnp.int32, (width, width), 1)
    earlier = jnp.where(r0 < r1, 1.0, 0.0).astype(jnp.bfloat16)
    band_id = lax.broadcasted_iota(jnp.int32, (BANDS, width), 0)
    place_id = lax.broadcasted_iota(jnp.int32, (128, width), 0)
    base = jnp.zeros((BANDS, 1), jnp.float32)
    found = jnp.zeros((2 * BANDS, 128), jnp.float32)
    for k in range(rows // width):
        cut = slice(k * width, (k + 1) * width)
        hot = jnp.where(band[:, cut] == band_id, 1.0, 0.0)
        before = jnp.dot(hot.astype(jnp.bfloat16), earlier, preferred_element_type=jnp.float32) + base
        rank = jnp.sum(hot * before, axis=0, keepdims=True).astype(jnp.int32) - turn_no * CAP
        base = base + jnp.sum(hot, axis=1, keepdims=True)
        valid = (rank >= 0) & (rank < CAP)
        slot = jnp.where(valid, (rank & 3) * (BANDS * ROWS) + band[:, cut] * ROWS + (rank >> 2), ROWS - 1)
        for g in range(width // 128):
            row = k * (width // 128) + g
            places[row : row + 1, :] = slot[:, g * 128 : (g + 1) * 128]
            places[row + 16 : row + 17, :] = lat[:, cut][:, g * 128 : (g + 1) * 128]
        a = address[:, cut]
        high = hot * (a >> 8).astype(jnp.float32)
        low = hot * (a & 255).astype(jnp.float32)
        both = jnp.concatenate([high, low], axis=0).astype(jnp.bfloat16)
        at_place = jnp.where(rank == place_id, 1.0, 0.0).astype(jnp.bfloat16)
        found = found + lax.dot_general(
            both, at_place, (((1,), (1,)), ((), ())), preferred_element_type=jnp.float32
        )
    copy = pltpu.make_async_copy(places, place_s, sem)
    copy.start()
    lax.fori_loop(0, xs.shape[0] // 64, clear, 0)
    headers = found[:BANDS] * 256.0 + found[BANDS:]
    lane = lax.broadcasted_iota(jnp.int32, (BANDS, 128), 1)
    left = jnp.clip(base - (turn_no * CAP).astype(jnp.float32), 0.0, float(CAP))
    most = jnp.max(base, axis=0, keepdims=True)
    headers = jnp.where(lane < CAP, headers, jnp.where(lane == COUNT_LANE, left, jnp.where(lane == MOST_LANE, most, 0.0)))

    fade = jnp.exp(-1.0 / len_lev[...])
    wide = jnp.concatenate([jnp.broadcast_to(fade[f : f + 1], (NLEV, NLAT)) for f in range(F)], axis=0)
    gain = sigma[...] * ((1.0 - wide) * (1.0 - wide))
    table[...] = jnp.transpose(gain)
    decay[...] = jnp.transpose(wide)
    copy.wait()

    def place(g, _):
        first = pl.multiple_of(g * 128, 128)
        for u in range(128):
            s = place_s[g, u]
            t = place_s[g + 16, u]
            xs[pl.ds(s, 1), :] = vals[pl.ds(first + u, 1), :] * table[pl.ds(t, 1), :]
            ax[pl.ds(s, 1), :] = decay[pl.ds(t, 1), :]
        return 0

    lax.fori_loop(0, rows // 128, place, 0)

    level = lax.broadcasted_iota(jnp.int32, (128, 128), 1) & (NLEV - 1)
    pi = lax.broadcasted_iota(jnp.int32, (256, 512), 0)
    pj = lax.broadcasted_iota(jnp.int32, (256, 512), 1)
    f_in, l_in, k_in = (pi >> 5) & 3, (pi >> 3) & 3, pi & 7
    aim = l_in * 128 + (pi >> 7) * 32 + f_in * 8 + k_in
    move = [jnp.where(pj == aim + 64 * half, 1.0, 0.0).astype(jnp.bfloat16) for half in (0, 1)]

    def smooth_levels(x, a):
        powers = [a]
        for _ in range(4):
            powers.append(powers[-1] * powers[-1])
        y = x
        for n, p in enumerate(powers):
            s = 1 << n
            y = y + jnp.where(level >= s, p, 0.0) * pltpu.roll(y, s, 1)
        for n, p in enumerate(powers):
            s = 1 << n
            y = y + jnp.where(level < NLEV - s, p, 0.0) * pltpu.roll(y, 128 - s, 1)
        return y

    def finish(i, _):
        total = jnp.zeros((128, 512), jnp.float32)
        for half in (0, 1):
            parts = []
            for q in (2 * half, 2 * half + 1):
                at = pl.ds(pl.multiple_of(q * (BANDS * ROWS) + i * 128, 128), 128)
                parts.append(smooth_levels(xs[at, :], ax[at, :]))
            x = jnp.concatenate(parts, axis=1)
            hi = x.astype(jnp.bfloat16)
            lo = (x - hi.astype(jnp.float32)).astype(jnp.bfloat16)
            total = total + jnp.dot(hi, move[half], preferred_element_type=jnp.float32)
            total = total + jnp.dot(lo, move[half], preferred_element_type=jnp.float32)
        for b in range(4):
            for l in range(LEVS):
                out[i * 4 + b, l] = total[b * ROWS : (b + 1) * ROWS, l * 128 : (l + 1) * 128]
        return 0

    lax.fori_loop(0, BANDS * ROWS // 128, finish, 0)
    for b in range(BANDS):
        for l in range(LEVS):
            out[b, l, ROWS - 1 : ROWS, :] = headers[b : b + 1]


def make_messages(turn, vals, owner, column, sigma, len_lev):
    slots = GROUP * BANDS * ROWS
    vmem = pl.BlockSpec(memory_space=pltpu.VMEM)
    return pl.pallas_call(
        send_kernel,
        out_shape=jax.ShapeDtypeStruct((BANDS, LEVS, ROWS, 128), jnp.float32),
        in_specs=[pl.BlockSpec(memory_space=pltpu.SMEM)] + [vmem] * 5,
        out_specs=vmem,
        scratch_shapes=[
            pltpu.VMEM((slots, 128), jnp.float32),
            pltpu.VMEM((slots, 128), jnp.float32),
            pltpu.VMEM((NLAT, 128), jnp.float32),
            pltpu.VMEM((NLAT, 128), jnp.float32),
            pltpu.VMEM((32, 128), jnp.int32),
            pltpu.SMEM((32, 128), jnp.int32),
            pltpu.SemaphoreType.DMA,
        ],
        compiler_params=pltpu.CompilerParams(vmem_limit_bytes=VMEM_LIMIT),
        name="make_messages",
    )(turn, vals, owner, column, sigma, len_lev)


def shift_down(x, by, sub):
    return jnp.where(sub >= by, pltpu.roll(x, by, 0), 0.0)


def shift_up(x, by, sub):
    return jnp.where(sub < 8 - by, pltpu.roll(x, 8 - by, 0), 0.0)


def grid_kernel(recv, lon_len, lat_len, ends, local, most, ga, gb, ramp, carry, ids_v, ids_s, sem):
    heads = recv[:, ROWS - 1, :]
    most[...] = jnp.max(heads, axis=0, keepdims=True)
    ids_v[...] = heads.astype(jnp.int32)
    copy = pltpu.make_async_copy(ids_v, ids_s, sem)
    copy.start()

    zeros = jnp.zeros((64, 128), jnp.float32)

    def clear(i, _):
        at = pl.ds(pl.multiple_of(i * 64, 64), 64)
        ga[at, :] = zeros
        gb[at, :] = zeros
        return 0

    lax.fori_loop(0, GRID_ROWS // 64, clear, 0)
    ga[GRID_ROWS - PAD :, :] = zeros[:PAD]
    gb[GRID_ROWS - PAD :, :] = zeros[:PAD]
    copy.wait()

    lane_block = blocks_of((1, 128))
    masks = [lane_block == q for q in range(GROUP)]
    sources = recv.shape[0]
    half = sources // 2

    def add_source(s, _):
        pair = ((s, ga), (s + half, gb))
        n = jnp.maximum(ids_s[s, COUNT_LANE], ids_s[s + half, COUNT_LANE])

        def add_rows(lo, hi):
            for j in range(lo, hi):
                where = [[ids_s[x, GROUP * j + q] for q in range(GROUP)] for x, _ in pair]
                held = [[g[pl.ds(where[i][q], 1), :] for q in range(GROUP)] for i, (_, g) in enumerate(pair)]
                for i, (x, g) in enumerate(pair):
                    row = recv[x, j : j + 1, :]
                    for q in range(GROUP):
                        pltpu.store(g.at[pl.ds(where[i][q], 1), :], held[i][q] + row, mask=masks[q])

        add_rows(0, 12)
        for lo in range(12, ROWS - 1, 4):

            @pl.when(n > GROUP * lo)
            def _():
                add_rows(lo, min(lo + 4, ROWS - 1))

        return 0

    lax.fori_loop(0, half, add_source, 0)

    il = 1.0 / lon_len[...]
    fade = jnp.broadcast_to(jnp.exp(-il), (8, 128))
    stepno = (lax.broadcasted_iota(jnp.int32, (STEP, 128), 0) + 1).astype(jnp.float32)
    ramp[...] = jnp.exp(-stepno * il)
    sub = lax.broadcasted_iota(jnp.int32, (8, 128), 0)
    subf = sub.astype(jnp.float32)
    blk = blocks_of((8, 128))
    even = (blk & 1) == 0
    lower = blk < 2
    seg_fade = [jnp.broadcast_to(jnp.exp(-il * float(STEP * m)), (8, 128)) for m in (1, 2, 4)]
    fade8 = jnp.exp(-il * float(STEP * 8))
    fade16 = jnp.exp(-il * float(STEP * 16))
    whole = 1.0 / (1.0 - jnp.exp(-il * float(NLON)))
    up_to = jnp.exp(-il * STEP * subf)
    down_to = jnp.exp(-il * STEP * (7.0 - subf))

    def at_row(lat, sv, t):
        return pl.ds(pl.multiple_of(lat * PLANE + sv * (STEP * 8) + t * 8 + PAD, 8), 8)

    def forward(t, state):
        new = []
        for i in range(TILES):
            for sv in range(SEGV):
                g = [ga[at_row(4 * i + j, sv, t), :] + gb[at_row(4 * i + j, sv, t), :] for j in range(4)]
                u = [
                    jnp.where(even, g[j], g[j + 1]) + pltpu.roll(jnp.where(even, g[j + 1], g[j]), 32, 1)
                    for j in (0, 2)
                ]
                x = jnp.where(lower, u[0], u[1]) + pltpu.roll(jnp.where(lower, u[1], u[0]), 64, 1)
                y = fade * state[i * SEGV + sv] + x
                ga[at_row(4 * i, sv, t), :] = y
                new.append(y)
        return tuple(new)

    blank = tuple(jnp.zeros((8, 128), jnp.float32) for _ in range(TILES * SEGV))
    state = lax.fori_loop(0, STEP, forward, blank)
    for i in range(TILES):
        run, tail = [], []
        for sv in range(SEGV):
            x = state[i * SEGV + sv]
            for m, by in enumerate((1, 2, 4)):
                x = x + seg_fade[m] * shift_down(x, by, sub)
            run.append(x)
            tail.append(x[7:8])
        for sv in range(SEGV):
            c = (tail[sv - 1] + fade8 * tail[sv - 2] + fade16 * tail[sv - 3]) * whole
            carry[i * SEGV + sv] = shift_down(run[sv], 1, sub) + up_to * c

    def backward(n, state):
        t = STEP - 1 - n
        r = jnp.broadcast_to(ramp[pl.ds(t, 1), :], (8, 128))
        new = []
        for i in range(TILES):
            for sv in range(SEGV):
                at = at_row(4 * i, sv, t)
                y = fade * state[i * SEGV + sv] + (ga[at, :] + r * carry[i * SEGV + sv])
                ga[at, :] = y
                new.append(y)
        return tuple(new)

    state = lax.fori_loop(0, STEP, backward, blank)
    for i in range(TILES):
        run, tail = [], []
        for sv in range(SEGV):
            x = state[i * SEGV + sv]
            for m, by in enumerate((1, 2, 4)):
                x = x + seg_fade[m] * shift_up(x, by, sub)
            run.append(x)
            tail.append(x[0:1])
        for sv in range(SEGV):
            c = (tail[(sv + 1) % 3] + fade8 * tail[(sv + 2) % 3] + fade16 * tail[sv]) * whole
            carry[i * SEGV + sv] = shift_up(run[sv], 1, sub) + down_to * c

    im = 1.0 / lat_len[...]
    one = jnp.exp(-im)
    a_lon = jnp.exp(-il)
    gain = (1.0 - a_lon) * (1.0 - a_lon) * ((1.0 - one) / (1.0 + one))

    def power(n):
        return jnp.broadcast_to(jnp.exp(-im * n.astype(jnp.float32)), (8, 128))

    near = [None] + [power(jnp.where(lane_block >= s, s, 4 - s)) for s in (1, 2, 3)]
    to_end = [power(3 - ((lane_block - s) & 3)) for s in range(4)]
    to_start = [power((lane_block - s) & 3) for s in range(4)]
    from_start = power(lane_block + 1)
    from_end = power(4 - lane_block)
    four = jnp.broadcast_to(jnp.exp(-im * 4.0), (8, 128))

    def across(p, _):
        for sv in range(SEGV):
            packed = []
            for h in (0, 1):
                t = p + h * (STEP // 2)
                r = jnp.broadcast_to(ramp[pl.ds(STEP - 1 - t, 1), :], (8, 128))
                res, up, down = [], [], []
                for i in range(TILES):
                    w = (ga[at_row(4 * i, sv, t), :] + r * carry[i * SEGV + sv]) * gain
                    rolled = [w] + [pltpu.roll(w, PROF * s, 1) for s in (1, 2, 3)]
                    res.append(w + near[1] * rolled[1] + near[2] * rolled[2] + near[3] * rolled[3])
                    up.append(sum(to_end[s] * rolled[s] for s in range(4)))
                    down.append(sum(to_start[s] * rolled[s] for s in range(4)))
                c = up[0]
                for i in range(1, TILES):
                    res[i] = res[i] + from_start * c
                    c = four * c + up[i]
                packed.append(c)
                c = down[TILES - 1]
                for i in range(TILES - 2, -1, -1):
                    res[i] = res[i] + from_end * c
                    c = four * c + down[i]
                packed.append(c)
                for i in range(TILES):
                    at = pl.ds(pl.multiple_of(i * PLANE + sv * (STEP * 8) + t * 8, 8), 8)
                    local[at, :] = res[i]
            at = pl.ds(pl.multiple_of(sv * (STEP * 4) + p * 8, 8), 8)
            ends[at, :] = jnp.where(lower, jnp.where(even, packed[0], packed[1]), jnp.where(even, packed[2], packed[3]))
        return 0

    lax.fori_loop(0, STEP // 2, across, 0)


def to_grid(recv, lon_len, lat_len):
    vmem = pl.BlockSpec(memory_space=pltpu.VMEM)
    return pl.pallas_call(
        grid_kernel,
        out_shape=(
            jax.ShapeDtypeStruct((NLON // 2, 128), jnp.float32),
            jax.ShapeDtypeStruct((TILES * PLANE, 128), jnp.float32),
            jax.ShapeDtypeStruct((1, 128), jnp.float32),
        ),
        in_specs=[vmem] * 3,
        out_specs=(vmem,) * 3,
        scratch_shapes=[
            pltpu.VMEM((GRID_ROWS, 128), jnp.float32),
            pltpu.VMEM((GRID_ROWS, 128), jnp.float32),
            pltpu.VMEM((STEP, 128), jnp.float32),
            pltpu.VMEM((TILES * SEGV, 8, 128), jnp.float32),
            pltpu.VMEM((128, 128), jnp.int32),
            pltpu.SMEM((128, 128), jnp.int32),
            pltpu.SemaphoreType.DMA,
        ],
        compiler_params=pltpu.CompilerParams(vmem_limit_bytes=VMEM_LIMIT),
        cost_estimate=pl.CostEstimate(flops=100_000_000, bytes_accessed=8_000_000, transcendentals=0),
        name="to_grid",
    )(recv, lon_len, lat_len)


def bands_kernel(ends, lat_len, out):
    im = 1.0 / lat_len[...]
    shape = ends.shape[1:]
    hop = jnp.broadcast_to(jnp.exp(-im * float(BAND)), shape)
    is_up = (blocks_of(shape) & 1) == 1
    acc = jnp.zeros(shape, jnp.float32)
    south = []
    for b in range(BANDS):
        south.append(acc)
        acc = hop * acc + ends[b]
    total = pltpu.roll(acc, PROF, 1)
    acc = jnp.zeros(shape, jnp.float32)
    for b in range(BANDS - 1, -1, -1):
        edge = jnp.exp(-im * float(BAND * (BANDS - 1 - b) + 1))
        out[b] = jnp.where(is_up, acc - edge * total, south[b])
        acc = hop * acc + ends[b]


def join_bands(ends, lat_len):
    vmem = pl.BlockSpec(memory_space=pltpu.VMEM)
    return pl.pallas_call(
        bands_kernel,
        out_shape=jax.ShapeDtypeStruct(ends.shape, jnp.float32),
        in_specs=[vmem] * 2,
        out_specs=vmem,
        compiler_params=pltpu.CompilerParams(vmem_limit_bytes=VMEM_LIMIT),
        name="join_bands",
    )(ends, lat_len)


def turn_kernel(local, control, out, flipped):
    m = pl.program_id(0)
    sv = m >> 2
    sub = (m & 3) * 2
    for i in range(TILES):
        base = i * PLANE + sv * (STEP * 8) + sub
        x = jnp.concatenate(
            [local[pl.ds(base, STEP, stride=8), :], local[pl.ds(base + 1, STEP, stride=8), :]], axis=0
        )
        flipped[i * 128 : (i + 1) * 128, :] = jnp.transpose(x)
    for v in range(PROF):
        for g in range(BAND // 8):
            x = flipped[pl.ds(v + 8 * PROF * g, 8, stride=PROF), :]
            out[v // LEVQ, v % LEVQ, 8 * g : 8 * g + 8, :] = control[v // LEVQ, v % LEVQ, 8 * g : 8 * g + 8, :] + x


def add_control(local, control):
    block = pl.BlockSpec((F, LEVQ, BAND, 128), lambda m: (0, 0, 0, m))
    return pl.pallas_call(
        turn_kernel,
        grid=(NLON // 128,),
        out_shape=jax.ShapeDtypeStruct(control.shape, jnp.float32),
        in_specs=[pl.BlockSpec((TILES * PLANE, 128), lambda m: (0, 0)), block],
        out_specs=block,
        scratch_shapes=[pltpu.VMEM((BAND * PROF, 128), jnp.float32)],
        compiler_params=pltpu.CompilerParams(vmem_limit_bytes=VMEM_LIMIT),
        cost_estimate=pl.CostEstimate(flops=20_000_000, bytes_accessed=15_000_000, transcendentals=0),
        name="add_control",
    )(local, control)


def last_kernel(lat_len, parts, joined, out, from_start, from_end, flipped):
    m = pl.program_id(0)

    @pl.when(m == 0)
    def _():
        lat = lax.broadcasted_iota(jnp.int32, (BAND, 128), 0).astype(jnp.float32)
        for v in range(PROF):
            scale = lat_len[v // LEVQ, v % LEVQ]
            from_start[v] = jnp.exp(-(lat + 1.0) / scale)
            from_end[v] = jnp.exp(-(float(BAND) - lat) / scale)

    sv = m >> 2
    sub = (m & 3) * 2
    pieces = []
    for s in (0, 1):
        x = joined[pl.ds(sv * (STEP * 4) + sub + s, STEP // 2, stride=8), :]
        pieces += [x, pltpu.roll(x, 64, 1)]
    flipped[...] = jnp.transpose(jnp.concatenate(pieces, axis=0))
    for v in range(PROF):
        south = flipped[v : v + 1, :]
        north = flipped[PROF + v : PROF + v + 1, :]
        out[v // LEVQ, v % LEVQ] = parts[v // LEVQ, v % LEVQ] + (from_start[v] * south + from_end[v] * north)


def add_bands(lat_len, parts, joined):
    block = pl.BlockSpec((F, LEVQ, BAND, 128), lambda m: (0, 0, 0, m))
    return pl.pallas_call(
        last_kernel,
        grid=(NLON // 128,),
        out_shape=jax.ShapeDtypeStruct(parts.shape, jnp.float32),
        in_specs=[
            pl.BlockSpec(memory_space=pltpu.SMEM),
            block,
            pl.BlockSpec((NLON // 2, 128), lambda m: (0, 0)),
        ],
        out_specs=block,
        scratch_shapes=[
            pltpu.VMEM((PROF, BAND, 128), jnp.float32),
            pltpu.VMEM((PROF, BAND, 128), jnp.float32),
            pltpu.VMEM((128, 128), jnp.float32),
        ],
        compiler_params=pltpu.CompilerParams(vmem_limit_bytes=VMEM_LIMIT),
        name="add_bands",
    )(lat_len, parts, joined)


def per_device(control, obs_values, obs_owner, obs_column, sigma, len_lon, len_lat, len_lev):
    owner = obs_owner.reshape(1, -1)
    column = obs_column.reshape(1, -1)
    sigma = sigma.reshape(F * NLEV, NLAT)
    lon_len = jnp.tile(len_lon.reshape(1, PROF), (1, GROUP))
    lat_len = jnp.tile(len_lat.reshape(1, PROF), (1, GROUP))

    def one_turn(turn):
        messages = make_messages(turn.reshape(1), obs_values, owner, column, sigma, len_lev)
        messages = messages.reshape(BANDS * LEVS, ROWS, 128)
        arrived = lax.all_to_all(messages, ("lat", "lev"), split_axis=0, concat_axis=0, tiled=True)
        ends, local, most = to_grid(arrived, lon_len, lat_len)
        return ends, local, most[0, MOST_LANE].astype(jnp.int32)

    ends, local, most = one_turn(jnp.int32(0))

    def more(state):
        return state[0] * CAP < most

    def next_turn(state):
        turn, ends, local = state
        more_ends, more_local, _ = one_turn(turn)
        return turn + 1, ends + more_ends, local + more_local

    _, ends, local = lax.while_loop(more, next_turn, (jnp.int32(1), ends, local))

    ends = ends.reshape(BANDS, -1, 128)
    ends = lax.all_to_all(ends, "lat", split_axis=0, concat_axis=0, tiled=True)
    joined = join_bands(ends, lat_len)
    joined = lax.all_to_all(joined, "lat", split_axis=0, concat_axis=0, tiled=True)
    parts = add_control(local, control)
    return add_bands(len_lat, parts, joined.reshape(NLON // 2, 128))


def solution(mesh):
    placed = (
        P(None, "lev", "lat", None),
        P(("lat", "lev"), None),
        P(("lat", "lev"), None),
        P(("lat", "lev")),
        P(),
        P(None, "lev"),
        P(None, "lev"),
        P(),
    )
    return jax.shard_map(
        per_device,
        mesh=mesh,
        in_specs=placed,
        out_specs=P(None, "lev", "lat", None),
        check_vma=False,
    )
```

```python
import jax
import jax.numpy as jnp
from jax import lax
from jax.experimental import pallas as pl
from jax.experimental.pallas import tpu as pltpu
from jax.sharding import PartitionSpec as P

F = 4
NLEV = 32
NLAT = 768
NLON = 1536
BANDS = 32
LEVS = 4
BAND = NLAT // BANDS
LEVQ = NLEV // LEVS
PROF = F * LEVQ
GROUP = 128 // PROF
ROWS = 32
CAP = (ROWS - 1) * GROUP
COUNT_LANE = 124
MOST_LANE = 125
STEP = 64
SEGV = 3
TILES = BAND // GROUP
PLANE = NLON
VMEM_LIMIT = 60 * 1024 * 1024
PAD = 8
REGION = BAND // 2 * PLANE
GRID_ROWS = REGION + PAD
HALF_CAP = CAP // 2
SWAP_LANE = 126
SAME_LANE = 127
BATCH = 2
SHARE = 2
WIDE = 4
PARTS = 3
PAIRS = BAND // 2


def third(x):
    return (x * 21846) >> 16


def blocks_of(shape):
    return lax.broadcasted_iota(jnp.int32, shape, len(shape) - 1) // PROF


def in_lanes(lengths):
    value = lax.broadcasted_iota(jnp.int32, (1, 128), 1) & (PROF - 1)
    x = jnp.ones((1, 128), jnp.float32)
    for v in range(PROF):
        x = jnp.where(value == v, lengths[v // LEVQ, v % LEVQ], x)
    return x


def in_rows(lengths, first):
    row = lax.broadcasted_iota(jnp.int32, (8, 128), 0)
    x = jnp.ones((8, 128), jnp.float32)
    for v in range(8):
        x = jnp.where(row == v, lengths[(first + v) // LEVQ, (first + v) % LEVQ], x)
    return x


def send_kernel(turn, vals, owner, column, sigma, len_lev, out, picks, work, lines, xs, places, sem, *place_s):
    rows = vals.shape[0]
    tiles = rows // 128
    turn_no = turn[0]

    d = owner[...]
    c = column[...]
    c48 = third(c >> 4)
    lat = (d & 3) * 192 + c48
    lon = (d >> 2) * 48 + (c - c48 * 48)
    band = third(lat >> 3)
    seg = lon >> 6
    grid_row = ((seg >> 3) * STEP + (lon & (STEP - 1))) * 8 + (seg & 7)
    odd = lat & 1
    address = ((lat - band * BAND) >> 1) * PLANE + grid_row + PAD

    width = 256
    r0 = lax.broadcasted_iota(jnp.int32, (width, width), 0)
    r1 = lax.broadcasted_iota(jnp.int32, (width, width), 1)
    earlier = jnp.where(r0 < r1, 1.0, 0.0).astype(jnp.bfloat16)
    band_id = lax.broadcasted_iota(jnp.int32, (BANDS, width), 0)
    place_id = lax.broadcasted_iota(jnp.int32, (128, width), 0)
    base = jnp.zeros((BANDS, 1), jnp.float32)
    half_base = jnp.zeros((2 * BANDS, 1), jnp.float32)
    found = jnp.zeros((2 * BANDS, 128), jnp.float32)
    for k in range(rows // width):
        cut = slice(k * width, (k + 1) * width)
        hot = jnp.where(band[:, cut] == band_id, 1.0, 0.0)
        before = jnp.dot(hot.astype(jnp.bfloat16), earlier, preferred_element_type=jnp.float32) + base
        rank = jnp.sum(hot * before, axis=0, keepdims=True).astype(jnp.int32) - turn_no * CAP
        base = base + jnp.sum(hot, axis=1, keepdims=True)
        now = (rank >= 0) & (rank < CAP)
        parity = odd[:, cut]
        hot = jnp.where(now, hot, 0.0)
        sides = jnp.concatenate([jnp.where(parity == 0, hot, 0.0), jnp.where(parity == 1, hot, 0.0)], axis=0)
        before = jnp.dot(sides.astype(jnp.bfloat16), earlier, preferred_element_type=jnp.float32) + half_base
        rank = jnp.sum(sides * before, axis=0, keepdims=True).astype(jnp.int32)
        half_base = half_base + jnp.sum(sides, axis=1, keepdims=True)
        swapped = rank >= HALF_CAP
        pos = jnp.where(swapped, CAP - 1 - rank, rank)
        q = 2 * (pos & 1) + jnp.where(swapped, 1 - parity, parity)
        row = pos >> 1
        slot = jnp.where(now, q * (BANDS * ROWS) + band[:, cut] * ROWS + row, ROWS - 1)
        for g in range(width // 128):
            n = k * (width // 128) + g
            places[n : n + 1, :] = slot[:, g * 128 : (g + 1) * 128]
            places[tiles + n : tiles + n + 1, :] = lat[:, cut][:, g * 128 : (g + 1) * 128]
        a = address[:, cut] + jnp.where(swapped, REGION, 0)
        high = hot * (a >> 8).astype(jnp.float32)
        low = hot * (a & 255).astype(jnp.float32)
        both = jnp.concatenate([high, low], axis=0).astype(jnp.bfloat16)
        at_place = jnp.where(row * GROUP + q == place_id, 1.0, 0.0).astype(jnp.bfloat16)
        found = found + lax.dot_general(
            both, at_place, (((1,), (1,)), ((), ())), preferred_element_type=jnp.float32
        )
    copies = [
        pltpu.make_async_copy(places.at[pl.ds(n, 1), :], place_s[n], sem.at[n]) for n in range(tiles)
    ]
    for copy in copies:
        copy.start()
    headers = found[:BANDS] * 256.0 + found[BANDS:]
    lane = lax.broadcasted_iota(jnp.int32, (BANDS, 128), 1)
    most_side = jnp.maximum(half_base[:BANDS], half_base[BANDS:])
    left = jnp.minimum(2.0 * most_side, float(CAP))
    swaps = jnp.where(most_side > float(HALF_CAP), 1.0, 0.0)
    most = jnp.max(base, axis=0, keepdims=True)
    headers = jnp.where(lane < CAP, headers, 0.0)
    headers = jnp.where(lane == COUNT_LANE, left, headers)
    headers = jnp.where(lane == MOST_LANE, most, headers)
    headers = jnp.where(lane == SWAP_LANE, swaps, headers)

    sig = sigma[...]
    sig_hi = sig.astype(jnp.bfloat16)
    picks[0:128, :] = sig_hi
    picks[128:256, :] = (sig - sig_hi.astype(jnp.float32)).astype(jnp.bfloat16)
    fade = jnp.exp(-1.0 / len_lev[...])
    fade = jnp.concatenate([fade, fade], axis=0)
    f_hi = fade.astype(jnp.bfloat16).astype(jnp.float32)
    f_mid = (fade - f_hi).astype(jnp.bfloat16).astype(jnp.float32)
    f_lo = fade - f_hi - f_mid
    picks[256:288, :] = jnp.concatenate([f_hi, f_mid, f_lo, jnp.zeros_like(fade)], axis=0).astype(jnp.bfloat16)
    lat_id = lax.broadcasted_iota(jnp.int32, (NLAT, width), 0)

    def smooth_levels(k, _):
        which = jnp.concatenate([places[pl.ds(tiles + 2 * k + g, 1), :] for g in (0, 1)], axis=1)
        at_lat = jnp.where(lat_id == which, 1.0, 0.0).astype(jnp.bfloat16)
        got = jnp.dot(picks[...], at_lat, preferred_element_type=jnp.float32)
        for g in (0, 1):
            lanes = slice(g * 128, (g + 1) * 128)
            at = pl.ds(pl.multiple_of(k * width + g * 128, 128), 128)
            side = work.at[g]
            side[0:128, :] = jnp.transpose(vals[at, :]) * (got[0:128, lanes] + got[128:256, lanes])
            a = got[256:260, lanes] + got[264:268, lanes] + got[272:276, lanes]
            y = [side[pl.ds(0, F, stride=NLEV), :]]
            for n in range(1, NLEV):
                y.append(a * y[-1] + side[pl.ds(n, F, stride=NLEV), :])
            gain = (1.0 - a) * (1.0 - a)
            w = y[-1]
            for n in range(NLEV - 1, -1, -1):
                if n < NLEV - 1:
                    w = a * w + y[n]
                side[pl.ds(128 + n // LEVQ * PROF + n % LEVQ, F, stride=LEVQ), :] = w * gain
            lines[at, :] = jnp.transpose(side[128:, :])
        return 0

    lax.fori_loop(0, rows // width, smooth_levels, 0)

    zeros = jnp.zeros((128, 128), jnp.float32)

    def clear(i, _):
        xs[pl.ds(pl.multiple_of(i * 128, 128), 128), :] = zeros
        return 0

    lax.fori_loop(0, xs.shape[0] // 128, clear, 0)
    for copy in copies:
        copy.wait()

    def place(n, _):
        for u in range(4):
            r = n * 4 + u
            to = [place_s[g][0, r] for g in range(tiles)]
            for g in range(tiles):
                xs[pl.ds(to[g], 1), :] = lines[pl.ds(g * 128 + r, 1), :]
        return 0

    lax.fori_loop(0, 128 // 4, place, 0)

    blk = blocks_of((ROWS, 128))
    even = (blk & 1) == 0
    lower = blk < 2

    def finish(n, _):
        done = []
        for b in (2 * n, 2 * n + 1):
            x = [xs[pl.ds(pl.multiple_of(q * (BANDS * ROWS) + b * ROWS, ROWS), ROWS), :] for q in range(GROUP)]
            first = [jnp.where(lower, x[q], pltpu.roll(x[q + 2], 64, 1)) for q in (0, 1)]
            last = [jnp.where(lower, pltpu.roll(x[q], 64, 1), x[q + 2]) for q in (0, 1)]
            for l, (u, w) in ((0, first), (2, last)):
                done.append((b, l, jnp.where(even, u, pltpu.roll(w, 32, 1))))
                done.append((b, l + 1, jnp.where(even, pltpu.roll(u, 96, 1), w)))
        for b, l, x in done:
            out[b, l] = x
        return 0

    lax.fori_loop(0, BANDS // 2, finish, 0)
    for b in range(BANDS):
        for l in range(LEVS):
            out[b, l, ROWS - 1 : ROWS, :] = headers[b : b + 1]


def make_messages(turn, vals, owner, column, sigma, len_lev):
    rows = vals.shape[0]
    vmem = pl.BlockSpec(memory_space=pltpu.VMEM)
    return pl.pallas_call(
        send_kernel,
        out_shape=jax.ShapeDtypeStruct((BANDS, LEVS, ROWS, 128), jnp.float32),
        in_specs=[pl.BlockSpec(memory_space=pltpu.SMEM)] + [vmem] * 5,
        out_specs=vmem,
        scratch_shapes=[
            pltpu.VMEM((288, NLAT), jnp.bfloat16),
            pltpu.VMEM((2, 256, 128), jnp.float32),
            pltpu.VMEM((rows, 128), jnp.float32),
            pltpu.VMEM((GROUP * BANDS * ROWS, 128), jnp.float32),
            pltpu.VMEM((rows // 64, 128), jnp.int32),
            pltpu.SemaphoreType.DMA((rows // 128,)),
        ]
        + [pltpu.SMEM((1, 128), jnp.int32)] * (rows // 128),
        compiler_params=pltpu.CompilerParams(vmem_limit_bytes=VMEM_LIMIT),
        name="make_messages",
    )(turn, vals, owner, column, sigma, len_lev)


def fold_lanes(a, b, first, by):
    return jnp.where(first, a, b) + pltpu.roll(jnp.where(first, b, a), by, 1)


def shift_down(x, by, sub):
    return jnp.where(sub >= by, pltpu.roll(x, by, 0), 0.0)


def shift_up(x, by, sub):
    return jnp.where(sub < 8 - by, pltpu.roll(x, 8 - by, 0), 0.0)


def grid_kernel(recv, lat_len, ends, pairs, most, ga, gb, ups, downs, ids_v, sem, out_sem, *ids_s):
    heads = recv[:, ROWS - 1, :]
    lane = lax.broadcasted_iota(jnp.int32, (128, 128), 1)
    heads = jnp.where(lane == MOST_LANE, jnp.max(heads, axis=0, keepdims=True), heads)
    ids = jnp.transpose(heads).astype(jnp.int32)
    same = jnp.zeros((8, 128), jnp.bool_)
    for m in range(0, 128, 16):
        a, b = ids[m : m + 8], ids[m + 8 : m + 16]
        turned = pltpu.roll(b, 4, 0)
        same = same | ((a >= PAD) & ((a == pltpu.roll(a, 4, 0)) | (a == b) | (a == turned)))
        same = same | ((b >= PAD) & (b == turned))
    same = jnp.max(jnp.where(same, 1, 0), axis=0, keepdims=True)
    ids_v[...] = ids
    ids_v[SAME_LANE : SAME_LANE + 1, :] = same
    copies = [
        pltpu.make_async_copy(ids_v.at[pl.ds(GROUP * j, GROUP), :], ids_s[j], sem.at[j]) for j in range(ROWS)
    ]
    for copy in copies:
        copy.start()
    zeros = jnp.zeros((256, 128), jnp.float32)

    def clear(i, _):
        at = pl.ds(pl.multiple_of(PAD + i * 256, 8), 256)
        ga[at, :] = zeros
        gb[at, :] = zeros
        return 0

    lax.fori_loop(0, REGION // 256, clear, 0)
    ga[:PAD, :] = zeros[:PAD]
    gb[:PAD, :] = zeros[:PAD]
    for copy in copies:
        copy.wait()
    tail = ids_s[ROWS - 1]
    most[0] = tail[MOST_LANE - CAP, 0]

    lane_block = blocks_of((1, 128))
    masks = [lane_block == q for q in range(GROUP)]
    half = recv.shape[0] // 2

    def add_source(s, _):
        pair = ((s, ga), (s + half, gb))
        n = jnp.maximum(tail[COUNT_LANE - CAP, s], tail[COUNT_LANE - CAP, s + half])
        swaps = tail[SWAP_LANE - CAP, s] + tail[SWAP_LANE - CAP, s + half]
        sames = tail[SAME_LANE - CAP, s] + tail[SAME_LANE - CAP, s + half]

        def add_rows(lo, hi, batch):
            items = [(range(j, min(j + batch, hi)), x, g) for j in range(lo, hi, batch) for x, g in pair]

            def read(item):
                js, x, g = item
                at = [[pl.ds(ids_s[j][q, x], 1) for q in range(GROUP)] for j in js]
                return at, [[g[a, :] for a in some] for some in at], [recv[x, j : j + 1, :] for j in js]

            ahead = read(items[0])
            for k, (_, _, g) in enumerate(items):
                at, held, row = ahead
                if k + 1 < len(items):
                    ahead = read(items[k + 1])
                for m in range(len(row)):
                    for q in range(GROUP):
                        pltpu.store(g.at[at[m][q], :], held[m][q] + row[m], mask=masks[q])

        def add_message(batch):
            add_rows(0, 12, batch)
            for lo in range(12, ROWS - 1, 4):

                @pl.when(n > GROUP * lo)
                def _():
                    add_rows(lo, min(lo + 4, ROWS - 1), batch)

        @pl.when(swaps + sames == 0)
        def _():
            add_message(BATCH)

        @pl.when((swaps == 0) & (sames > 0))
        def _():
            add_message(1)

        @pl.when(swaps > 0)
        def _():
            for x, g in pair:
                for j in range(ROWS - 1):
                    row = recv[x, j : j + 1, :]
                    turned = pltpu.roll(row, PROF, 1)
                    for q in range(GROUP):
                        to = ids_s[j][q, x]
                        far = to >= GRID_ROWS
                        for at, what, mask in (
                            (jnp.where(far, 0, to), row, masks[q]),
                            (jnp.where(far, to - REGION, 0), turned, masks[(q + 1) % GROUP]),
                        ):
                            at = pl.ds(at, 1)
                            pltpu.store(g.at[at, :], g[at, :] + what, mask=mask)

        return 0

    lax.fori_loop(0, half, add_source, 0)

    im = 1.0 / in_lanes(lat_len)

    def power(n):
        return jnp.broadcast_to(jnp.exp(-im * n.astype(jnp.float32)), (8, 128))

    parity = lane_block & 1
    to_end = [power(BAND - 1 - 2 * n - parity) for n in range(PAIRS)]
    to_start = [power(2 * n + parity) for n in range(PAIRS)]
    out_copies = []
    for part in range(PARTS):

        def gather(r, _):
            row = part * (PLANE // PARTS) + r * 8
            at = [pl.ds(pl.multiple_of(PAD + n * PLANE + row, 8), 8) for n in range(PAIRS)]
            cells = [ga[a, :] + gb[a, :] for a in at]
            up = down = None
            for n, x in enumerate(cells):
                up = to_end[n] * x if n == 0 else up + to_end[n] * x
                down = to_start[n] * x if n == 0 else down + to_start[n] * x
            for a, x in zip(at, cells):
                ga[a, :] = x
            here = pl.ds(pl.multiple_of(row, 8), 8)
            ups[here, :] = up
            downs[here, :] = down
            return 0

        lax.fori_loop(0, PLANE // PARTS // 8, gather, 0)
        for n in range(PAIRS):
            first = n * PLANE + part * (PLANE // PARTS)
            out_copies.append(
                pltpu.make_async_copy(
                    ga.at[pl.ds(PAD + first, PLANE // PARTS), :],
                    pairs.at[pl.ds(first, PLANE // PARTS), :],
                    out_sem.at[part * PAIRS + n],
                )
            )
            out_copies[-1].start()

    blk = blocks_of((8, 128))
    even = (blk & 1) == 0
    lower = blk < 2

    def pack(k, _):
        done = []
        for u in range(16):
            p = k * 16 + u
            row = (p >> 5) * (STEP * 8) + (p & 31) * 8
            sums = []
            for h in (0, 1):
                at = pl.ds(pl.multiple_of(row + h * (STEP * 4), 8), 8)
                sums.append(fold_lanes(ups[at, :], downs[at, :], even, 32))
            done.append(fold_lanes(sums[0], sums[1], lower, 64))
        for u, x in enumerate(done):
            ends[pl.ds(pl.multiple_of((k * 16 + u) * 8, 8), 8), :] = x
        return 0

    lax.fori_loop(0, SEGV * (STEP // 2) // 16, pack, 0)
    for copy in out_copies:
        copy.wait()


def to_grid(recv, lat_len):
    vmem = pl.BlockSpec(memory_space=pltpu.VMEM)
    smem = pl.BlockSpec(memory_space=pltpu.SMEM)
    return pl.pallas_call(
        grid_kernel,
        out_shape=(
            jax.ShapeDtypeStruct((NLON // 2, 128), jnp.float32),
            jax.ShapeDtypeStruct((REGION, 128), jnp.float32),
            jax.ShapeDtypeStruct((1,), jnp.int32),
        ),
        in_specs=[vmem, smem],
        out_specs=(vmem, pl.BlockSpec(memory_space=pl.ANY), smem),
        scratch_shapes=[
            pltpu.VMEM((GRID_ROWS, 128), jnp.float32),
            pltpu.VMEM((GRID_ROWS, 128), jnp.float32),
            pltpu.VMEM((PLANE, 128), jnp.float32),
            pltpu.VMEM((PLANE, 128), jnp.float32),
            pltpu.VMEM((128, 128), jnp.int32),
            pltpu.SemaphoreType.DMA((ROWS,)),
            pltpu.SemaphoreType.DMA((PARTS * PAIRS,)),
        ]
        + [pltpu.SMEM((GROUP, 128), jnp.int32)] * ROWS,
        compiler_params=pltpu.CompilerParams(vmem_limit_bytes=VMEM_LIMIT),
        name="to_grid",
    )(recv, lat_len)


def circle_carry(last, fades, backward):
    il, seg_fade, fade8, fade16, whole, sub = fades
    run, tail = [], []
    for x in last:
        for m, by in enumerate((1, 2, 4)):
            x = x + seg_fade[m] * (shift_up if backward else shift_down)(x, by, sub)
        run.append(x)
        tail.append(x[0:1] if backward else x[7:8])
    entering = []
    for sv in range(SEGV):
        order = [tail[(sv + n) % 3] if backward else tail[(sv - n) % 3] for n in (1, 2, 3)]
        c = (order[0] + fade8 * order[1] + fade16 * order[2]) * whole
        if backward:
            entering.append(shift_up(run[sv], 1, sub) + jnp.exp(-il * (STEP * (7.0 - sub.astype(jnp.float32)))) * c)
        else:
            entering.append(shift_down(run[sv], 1, sub) + jnp.exp(-il * (STEP * sub.astype(jnp.float32))) * c)
    return entering


def circle_fades(il):
    sub = lax.broadcasted_iota(jnp.int32, (8, 128), 0)
    seg_fade = [jnp.broadcast_to(jnp.exp(-il * float(STEP * m)), (8, 128)) for m in (1, 2, 4)]
    fade8 = jnp.exp(-il * float(STEP * 8))
    fade16 = jnp.exp(-il * float(STEP * 16))
    whole = 1.0 / (1.0 - jnp.exp(-il * float(NLON)))
    return il, seg_fade, fade8, fade16, whole, sub


def total_gain(il, im):
    one_lon, one_lat = jnp.exp(-il), jnp.exp(-im)
    return (1.0 - one_lon) * (1.0 - one_lon) * ((1.0 - one_lat) / (1.0 + one_lat))


def smooth_kernel(pairs, lon_len, local, done, ramp, carry):
    il = 1.0 / in_lanes(lon_len)
    fade = jnp.broadcast_to(jnp.exp(-il), (8, 128))
    stepno = (lax.broadcasted_iota(jnp.int32, (STEP, 128), 0) + 1).astype(jnp.float32)
    ramp[...] = jnp.exp(-stepno * il)
    fades = circle_fades(il)
    lower = blocks_of((8, 128)) < 2
    vectors = [(i, sv) for i in range(SHARE) for sv in range(SEGV)]

    def at_row(i, sv, t):
        return pl.ds(pl.multiple_of(i * PLANE + sv * (STEP * 8) + t * 8, 8), 8)

    def forward(n, state):
        cells = []
        for u in range(4):
            cells.append(
                [
                    fold_lanes(
                        pairs[at_row(2 * i, sv, n * 4 + u), :], pairs[at_row(2 * i + 1, sv, n * 4 + u), :], lower, 64
                    )
                    for i, sv in vectors
                ]
            )
        for u in range(4):
            state = tuple(fade * y + x for y, x in zip(state, cells[u]))
            cells[u] = state
        for u in range(4):
            for (i, sv), y in zip(vectors, cells[u]):
                local[at_row(i, sv, n * 4 + u), :] = y
        return state

    blank = tuple(jnp.zeros((8, 128), jnp.float32) for _ in vectors)
    state = lax.fori_loop(0, STEP // 4, forward, blank)
    for i in range(SHARE):
        for sv, x in enumerate(circle_carry(state[i * SEGV : (i + 1) * SEGV], fades, False)):
            carry[i * SEGV + sv] = x

    def backward(n, state):
        cells = []
        for u in range(4):
            t = STEP - 1 - n * 4 - u
            r = jnp.broadcast_to(ramp[pl.ds(t, 1), :], (8, 128))
            cells.append([local[at_row(i, sv, t), :] + r * carry[k] for k, (i, sv) in enumerate(vectors)])
        for u in range(4):
            state = tuple(fade * y + x for y, x in zip(state, cells[u]))
            cells[u] = state
        for u in range(4):
            for (i, sv), y in zip(vectors, cells[u]):
                local[at_row(i, sv, STEP - 1 - n * 4 - u), :] = y
        return state

    state = lax.fori_loop(0, STEP // 4, backward, blank)
    for i in range(SHARE):
        for sv, x in enumerate(circle_carry(state[i * SEGV : (i + 1) * SEGV], fades, True)):
            carry[i * SEGV + sv] = x

    def finish(n, _):
        cells = []
        for u in range(4):
            r = jnp.broadcast_to(ramp[pl.ds(STEP - 1 - n * 4 - u, 1), :], (8, 128))
            cells.append([local[at_row(i, sv, n * 4 + u), :] + r * carry[k] for k, (i, sv) in enumerate(vectors)])
        for u in range(4):
            for (i, sv), y in zip(vectors, cells[u]):
                local[at_row(i, sv, n * 4 + u), :] = y
        return 0

    lax.fori_loop(0, STEP // 4, finish, 0)
    done[...] = fade


def smooth_band(pairs, lon_len):
    return pl.pallas_call(
        smooth_kernel,
        grid=(TILES // SHARE,),
        out_shape=(
            jax.ShapeDtypeStruct((TILES * PLANE, 128), jnp.float32),
            jax.ShapeDtypeStruct((8, 128), jnp.float32),
        ),
        in_specs=[
            pl.BlockSpec((2 * SHARE * PLANE, 128), lambda n: (n, 0)),
            pl.BlockSpec(memory_space=pltpu.SMEM),
        ],
        out_specs=(
            pl.BlockSpec((SHARE * PLANE, 128), lambda n: (n, 0)),
            pl.BlockSpec(memory_space=pltpu.VMEM),
        ),
        scratch_shapes=[
            pltpu.VMEM((STEP, 128), jnp.float32),
            pltpu.VMEM((SHARE * SEGV, 8, 128), jnp.float32),
        ],
        compiler_params=pltpu.CompilerParams(vmem_limit_bytes=VMEM_LIMIT),
        cost_estimate=pl.CostEstimate(flops=20_000_000, bytes_accessed=14_000_000, transcendentals=0),
        name="smooth_band",
    )(pairs, lon_len)


def bands_kernel(ends, lat_len, _, out):
    im = 1.0 / in_lanes(lat_len)
    shape = ends.shape[1:]
    hop = jnp.broadcast_to(jnp.exp(-im * float(BAND)), shape)
    is_up = (blocks_of(shape) & 1) == 1
    acc = jnp.zeros(shape, jnp.float32)
    south = []
    for b in range(BANDS):
        south.append(acc)
        acc = hop * acc + ends[b]
    total = pltpu.roll(acc, PROF, 1)
    acc = jnp.zeros(shape, jnp.float32)
    for b in range(BANDS - 1, -1, -1):
        edge = jnp.exp(-im * float(BAND * (BANDS - 1 - b) + 1))
        out[b] = jnp.where(is_up, acc - edge * total, south[b])
        acc = hop * acc + ends[b]


def join_bands(ends, lat_len, after):
    vmem = pl.BlockSpec(memory_space=pltpu.VMEM)
    return pl.pallas_call(
        bands_kernel,
        out_shape=jax.ShapeDtypeStruct(ends.shape, jnp.float32),
        in_specs=[vmem, pl.BlockSpec(memory_space=pltpu.SMEM), pl.BlockSpec(memory_space=pl.ANY)],
        out_specs=vmem,
        compiler_params=pltpu.CompilerParams(vmem_limit_bytes=VMEM_LIMIT),
        name="join_bands",
    )(ends, lat_len, after)


def turn_kernel(local, control, lon_len, lat_len, out, flipped):
    m = pl.program_id(0)
    for side in range(WIDE):
        sub = (m % (4 // WIDE) * WIDE + side) * 2
        for i in range(TILES):
            x = jnp.concatenate(
                [local[i, pl.ds(sub, STEP, stride=8), :], local[i, pl.ds(sub + 1, STEP, stride=8), :]], axis=0
            )
            flipped[side, i * 128 : (i + 1) * 128, :] = jnp.transpose(x)
    for o in range(0, PROF, 8):
        il = 1.0 / in_rows(lon_len, o)
        im = 1.0 / in_rows(lat_len, o)
        fade = jnp.exp(-im)
        gain = total_gain(il, im)
        for side in range(WIDE):
            x = [flipped[side, n * PROF + o : n * PROF + o + 8, :] for n in range(BAND)]
            south = [x[0]]
            for n in range(1, BAND):
                south.append(fade * south[-1] + x[n])
            north = jnp.zeros((8, 128), jnp.float32)
            for n in range(BAND - 1, -1, -1):
                north = fade * north
                flipped[side, n * PROF + o : n * PROF + o + 8, :] = (south[n] + north) * gain
                north = north + x[n]
    for v in range(PROF):
        for g in range(BAND // 8):
            for side in range(WIDE):
                x = flipped[side, pl.ds(v + 8 * PROF * g, 8, stride=PROF), :]
                f, k, lats, lanes = v // LEVQ, v % LEVQ, slice(8 * g, 8 * g + 8), slice(128 * side, 128 * side + 128)
                out[f, k, lats, lanes] = control[f, k, lats, lanes] + x


def add_control(local, control, lon_len, lat_len):
    block = pl.BlockSpec((F, LEVQ, BAND, 128 * WIDE), lambda m: (0, 0, 0, m))
    smem = pl.BlockSpec(memory_space=pltpu.SMEM)
    return pl.pallas_call(
        turn_kernel,
        grid=(NLON // 128 // WIDE,),
        out_shape=jax.ShapeDtypeStruct(control.shape, jnp.float32),
        in_specs=[
            pl.BlockSpec((TILES, STEP * 8, 128), lambda m: (0, m // (4 // WIDE), 0)),
            block,
            smem,
            smem,
        ],
        out_specs=block,
        scratch_shapes=[pltpu.VMEM((WIDE, BAND * PROF, 128), jnp.float32)],
        compiler_params=pltpu.CompilerParams(vmem_limit_bytes=VMEM_LIMIT),
        cost_estimate=pl.CostEstimate(flops=20_000_000, bytes_accessed=15_000_000, transcendentals=0),
        name="add_control",
    )(local.reshape(TILES, PLANE, 128), control, lon_len, lat_len)


def last_kernel(lat_len, lon_len, parts, joined, out, held, from_start, from_end, ys, south, north, sem):
    half = STEP // 2
    per = LEVQ // 4
    chunks = [(k // 4, pl.ds(k % 4 * per, per)) for k in range(F * 4)]
    fetches = [pltpu.make_async_copy(parts.at[c], held.at[c], sem.at[0, k]) for k, c in enumerate(chunks)]
    stores = [pltpu.make_async_copy(held.at[c], out.at[c], sem.at[1, k]) for k, c in enumerate(chunks)]
    for copy in fetches:
        copy.start()

    lat = lax.broadcasted_iota(jnp.int32, (BAND, 128), 0).astype(jnp.float32)
    for v in range(PROF):
        scale = lat_len[v // LEVQ, v % LEVQ]
        from_start[v] = jnp.exp(-(lat + 1.0) / scale)
        from_end[v] = jnp.exp(-(float(BAND) - lat) / scale)

    il = 1.0 / in_lanes(lon_len)
    im = 1.0 / in_lanes(lat_len)
    fade = jnp.broadcast_to(jnp.exp(-il), (8, 128))
    fades = circle_fades(il)
    half_fade = jnp.broadcast_to(jnp.exp(-il * float(half)), (8, 128))
    first = blocks_of((8, 128)) < 2
    gain = total_gain(il, im)

    def rows_at(sv, p):
        return slice(sv * (half * 8) + p * 8, sv * (half * 8) + p * 8 + 8)

    def enter(last, backward):
        other = [pltpu.roll(x, 64, 1) for x in last]
        early = jnp.logical_not(first) if backward else first
        full = [jnp.where(early, o + half_fade * x, x + half_fade * o) for x, o in zip(last, other)]
        into = circle_carry(full, fades, backward)
        return [jnp.where(early, c, o + half_fade * c) for c, o in zip(into, other)]

    y = [jnp.zeros((8, 128), jnp.float32)] * SEGV
    for p in range(half):
        for sv in range(SEGV):
            y[sv] = fade * y[sv] + joined[rows_at(sv, p), :]
            ys[rows_at(sv, p), :] = y[sv]
    into = enter(y, False)
    y = [jnp.zeros((8, 128), jnp.float32)] * SEGV
    for p in range(half - 1, -1, -1):
        r = jnp.exp(-il * float(p + 1))
        for sv in range(SEGV):
            y[sv] = fade * y[sv] + (ys[rows_at(sv, p), :] + r * into[sv])
            ys[rows_at(sv, p), :] = y[sv]
    into = enter(y, True)
    for p in range(half):
        r = jnp.exp(-il * float(half - p))
        for sv in range(SEGV):
            ys[rows_at(sv, p), :] = (ys[rows_at(sv, p), :] + r * into[sv]) * gain
    for m in range(NLON // 128):
        pieces = []
        for s in (0, 1):
            x = ys[pl.ds(m // 4 * (half * 8) + m % 4 * 2 + s, half, stride=8), :]
            pieces += [x, pltpu.roll(x, 64, 1)]
        x = jnp.transpose(jnp.concatenate(pieces, axis=0))
        south[m] = x[0:PROF]
        north[m] = x[PROF : 2 * PROF]

    for n, fetch in enumerate(fetches):
        fetch.wait()
        for k in range(per):
            v = n * per + k
            f, level = v // LEVQ, v % LEVQ
            up, down = from_start[v], from_end[v]
            for m in range(NLON // 128):
                lanes = slice(m * 128, (m + 1) * 128)
                held[f, level, :, lanes] = held[f, level, :, lanes] + (
                    up * south[m, v : v + 1, :] + down * north[m, v : v + 1, :]
                )
        stores[n].start()
    for copy in stores:
        copy.wait()


def add_bands(lat_len, lon_len, parts, joined):
    smem = pl.BlockSpec(memory_space=pltpu.SMEM)
    vmem = pl.BlockSpec(memory_space=pltpu.VMEM)
    hbm = pl.BlockSpec(memory_space=pl.ANY)
    return pl.pallas_call(
        last_kernel,
        out_shape=jax.ShapeDtypeStruct(parts.shape, jnp.float32),
        in_specs=[smem, smem, hbm, vmem],
        out_specs=hbm,
        scratch_shapes=[
            pltpu.VMEM(parts.shape, jnp.float32),
            pltpu.VMEM((PROF, BAND, 128), jnp.float32),
            pltpu.VMEM((PROF, BAND, 128), jnp.float32),
            pltpu.VMEM((NLON // 2, 128), jnp.float32),
            pltpu.VMEM((NLON // 128, PROF, 128), jnp.float32),
            pltpu.VMEM((NLON // 128, PROF, 128), jnp.float32),
            pltpu.SemaphoreType.DMA((2, F * 4)),
        ],
        compiler_params=pltpu.CompilerParams(vmem_limit_bytes=VMEM_LIMIT),
        name="add_bands",
    )(lat_len, lon_len, parts, joined)


def per_device(control, obs_values, obs_owner, obs_column, sigma, len_lon, len_lat, len_lev):
    owner = obs_owner.reshape(1, -1)
    column = obs_column.reshape(1, -1)
    sigma = sigma.reshape(F * NLEV, NLAT)
    def one_turn(turn):
        messages = make_messages(turn.reshape(1), obs_values, owner, column, sigma, len_lev)
        messages = messages.reshape(BANDS * LEVS, ROWS, 128)
        arrived = lax.all_to_all(messages, ("lat", "lev"), split_axis=0, concat_axis=0, tiled=True)
        ends, grid, most = to_grid(arrived, len_lat)
        return ends, grid, most[0]

    ends, grid, most = one_turn(jnp.int32(0))

    def more(state):
        return state[0] * CAP < most

    def next_turn(state):
        turn, ends, grid = state
        more_ends, more_grid, _ = one_turn(turn)
        return turn + 1, ends + more_ends, grid + more_grid

    _, ends, grid = lax.while_loop(more, next_turn, (jnp.int32(1), ends, grid))

    ends = ends.reshape(BANDS, -1, 128)
    ends = lax.all_to_all(ends, "lat", split_axis=0, concat_axis=0, tiled=True)
    local, done = smooth_band(grid, len_lon)
    joined = join_bands(ends, len_lat, done)
    joined = lax.all_to_all(joined, "lat", split_axis=0, concat_axis=0, tiled=True)
    parts = add_control(local, control, len_lon, len_lat)
    return add_bands(len_lat, len_lon, parts, joined.reshape(NLON // 2, 128))


def solution(mesh):
    placed = (
        P(None, "lev", "lat", None),
        P(("lat", "lev"), None),
        P(("lat", "lev"), None),
        P(("lat", "lev")),
        P(),
        P(None, "lev"),
        P(None, "lev"),
        P(),
    )
    return jax.shard_map(
        per_device,
        mesh=mesh,
        in_specs=placed,
        out_specs=P(None, "lev", "lat", None),
        check_vma=False,
    )
```

```python
import jax
import jax.numpy as jnp
from jax import lax
from jax.experimental import pallas as pl
from jax.experimental.pallas import tpu as pltpu
from jax.sharding import PartitionSpec as P

F = 4
NLEV = 32
NLAT = 768
NLON = 1536
BANDS = 32
LEVS = 4
BAND = NLAT // BANDS
LEVQ = NLEV // LEVS
PROF = F * LEVQ
GROUP = 128 // PROF
ROWS = 32
CAP = (ROWS - 1) * GROUP
COUNT_LANE = 124
MOST_LANE = 125
STEP = 64
SEGV = 3
TILES = BAND // GROUP
PLANE = NLON
VMEM_LIMIT = 58 * 1024 * 1024
PAD = 8
REGION = BAND // 2 * PLANE
GRID_ROWS = REGION + PAD
HALF_CAP = CAP // 2
SWAP_LANE = 126
SAME_LANE = 127
BATCH = 2
SHARE = 2
WIDE = 4
UNROLL = 8
PARTS = 3
PAIRS = BAND // 2


def third(x):
    return (x * 21846) >> 16


def blocks_of(shape):
    return lax.broadcasted_iota(jnp.int32, shape, len(shape) - 1) // PROF


def in_lanes(lengths):
    value = lax.broadcasted_iota(jnp.int32, (1, 128), 1) & (PROF - 1)
    x = jnp.ones((1, 128), jnp.float32)
    for v in range(PROF):
        x = jnp.where(value == v, lengths[v // LEVQ, v % LEVQ], x)
    return x


def in_rows(lengths, first):
    row = lax.broadcasted_iota(jnp.int32, (8, 128), 0)
    x = jnp.ones((8, 128), jnp.float32)
    for v in range(8):
        x = jnp.where(row == v, lengths[(first + v) // LEVQ, (first + v) % LEVQ], x)
    return x


def send_kernel(
    turn, vals_in, owner, column, sigma, len_lev, out, vals, held, heads, picks, work, lines, xs, places, sem, io_sem, *place_s
):
    rows = vals.shape[0]
    take = pltpu.make_async_copy(vals_in, vals, io_sem.at[0])
    take.start()
    tiles = rows // 128
    turn_no = turn[0]

    d = owner[...]
    c = column[...]
    c48 = third(c >> 4)
    lat = (d & 3) * 192 + c48
    lon = (d >> 2) * 48 + (c - c48 * 48)
    band = third(lat >> 3)
    seg = lon >> 6
    grid_row = ((seg >> 3) * STEP + (lon & (STEP - 1))) * 8 + (seg & 7)
    odd = lat & 1
    address = ((lat - band * BAND) >> 1) * PLANE + grid_row + PAD

    width = 256
    r0 = lax.broadcasted_iota(jnp.int32, (width, width), 0)
    r1 = lax.broadcasted_iota(jnp.int32, (width, width), 1)
    earlier = jnp.where(r0 < r1, 1.0, 0.0).astype(jnp.bfloat16)
    band_id = lax.broadcasted_iota(jnp.int32, (BANDS, width), 0)
    place_id = lax.broadcasted_iota(jnp.int32, (128, width), 0)
    base = jnp.zeros((BANDS, 1), jnp.float32)
    half_base = jnp.zeros((2 * BANDS, 1), jnp.float32)
    found = jnp.zeros((2 * BANDS, 128), jnp.float32)
    for k in range(rows // width):
        cut = slice(k * width, (k + 1) * width)
        hot = jnp.where(band[:, cut] == band_id, 1.0, 0.0)
        before = jnp.dot(hot.astype(jnp.bfloat16), earlier, preferred_element_type=jnp.float32) + base
        rank = jnp.sum(hot * before, axis=0, keepdims=True).astype(jnp.int32) - turn_no * CAP
        base = base + jnp.sum(hot, axis=1, keepdims=True)
        now = (rank >= 0) & (rank < CAP)
        parity = odd[:, cut]
        hot = jnp.where(now, hot, 0.0)
        sides = jnp.concatenate([jnp.where(parity == 0, hot, 0.0), jnp.where(parity == 1, hot, 0.0)], axis=0)
        before = jnp.dot(sides.astype(jnp.bfloat16), earlier, preferred_element_type=jnp.float32) + half_base
        rank = jnp.sum(sides * before, axis=0, keepdims=True).astype(jnp.int32)
        half_base = half_base + jnp.sum(sides, axis=1, keepdims=True)
        swapped = rank >= HALF_CAP
        pos = jnp.where(swapped, CAP - 1 - rank, rank)
        q = 2 * (pos & 1) + jnp.where(swapped, 1 - parity, parity)
        row = pos >> 1
        slot = jnp.where(now, q * (BANDS * ROWS) + band[:, cut] * ROWS + row, ROWS - 1)
        for g in range(width // 128):
            n = k * (width // 128) + g
            places[n : n + 1, :] = slot[:, g * 128 : (g + 1) * 128]
            places[tiles + n : tiles + n + 1, :] = lat[:, cut][:, g * 128 : (g + 1) * 128]
        a = address[:, cut] + jnp.where(swapped, REGION, 0)
        high = hot * (a >> 8).astype(jnp.float32)
        low = hot * (a & 255).astype(jnp.float32)
        both = jnp.concatenate([high, low], axis=0).astype(jnp.bfloat16)
        at_place = jnp.where(row * GROUP + q == place_id, 1.0, 0.0).astype(jnp.bfloat16)
        found = found + lax.dot_general(
            both, at_place, (((1,), (1,)), ((), ())), preferred_element_type=jnp.float32
        )
    copies = [
        pltpu.make_async_copy(places.at[pl.ds(n, 1), :], place_s[n], sem.at[n]) for n in range(tiles)
    ]
    for copy in copies:
        copy.start()
    headers = found[:BANDS] * 256.0 + found[BANDS:]
    lane = lax.broadcasted_iota(jnp.int32, (BANDS, 128), 1)
    most_side = jnp.maximum(half_base[:BANDS], half_base[BANDS:])
    left = jnp.minimum(2.0 * most_side, float(CAP))
    swaps = jnp.where(most_side > float(HALF_CAP), 1.0, 0.0)
    most = jnp.max(base, axis=0, keepdims=True)
    headers = jnp.where(lane < CAP, headers, 0.0)
    headers = jnp.where(lane == COUNT_LANE, left, headers)
    headers = jnp.where(lane == MOST_LANE, most, headers)
    heads[...] = jnp.where(lane == SWAP_LANE, swaps, headers)

    sig = sigma[...]
    sig_hi = sig.astype(jnp.bfloat16)
    picks[0:128, :] = sig_hi
    picks[128:256, :] = (sig - sig_hi.astype(jnp.float32)).astype(jnp.bfloat16)
    fade = jnp.exp(-1.0 / len_lev[...])
    fade = jnp.concatenate([fade, fade], axis=0)
    f_hi = fade.astype(jnp.bfloat16).astype(jnp.float32)
    f_mid = (fade - f_hi).astype(jnp.bfloat16).astype(jnp.float32)
    f_lo = fade - f_hi - f_mid
    picks[256:288, :] = jnp.concatenate([f_hi, f_mid, f_lo, jnp.zeros_like(fade)], axis=0).astype(jnp.bfloat16)
    lat_id = lax.broadcasted_iota(jnp.int32, (NLAT, width), 0)

    def smooth_levels(k, _):
        which = jnp.concatenate([places[pl.ds(tiles + 2 * k + g, 1), :] for g in (0, 1)], axis=1)
        at_lat = jnp.where(lat_id == which, 1.0, 0.0).astype(jnp.bfloat16)
        got = jnp.dot(picks[...], at_lat, preferred_element_type=jnp.float32)
        for g in (0, 1):
            lanes = slice(g * 128, (g + 1) * 128)
            at = pl.ds(pl.multiple_of(k * width + g * 128, 128), 128)
            side = work.at[g]
            side[0:128, :] = jnp.transpose(vals[at, :]) * (got[0:128, lanes] + got[128:256, lanes])
            a = got[256:260, lanes] + got[264:268, lanes] + got[272:276, lanes]
            y = [side[pl.ds(0, F, stride=NLEV), :]]
            for n in range(1, NLEV):
                y.append(a * y[-1] + side[pl.ds(n, F, stride=NLEV), :])
            gain = (1.0 - a) * (1.0 - a)
            w = y[-1]
            for n in range(NLEV - 1, -1, -1):
                if n < NLEV - 1:
                    w = a * w + y[n]
                side[pl.ds(128 + n // LEVQ * PROF + n % LEVQ, F, stride=LEVQ), :] = w * gain
            lines[at, :] = jnp.transpose(side[128:, :])
        return 0

    take.wait()
    lax.fori_loop(0, rows // width, smooth_levels, 0)

    zeros = jnp.zeros((128, 128), jnp.float32)

    def clear(i, _):
        xs[pl.ds(pl.multiple_of(i * 128, 128), 128), :] = zeros
        return 0

    lax.fori_loop(0, xs.shape[0] // 128, clear, 0)
    for copy in copies:
        copy.wait()

    def place(n, _):
        for u in range(4):
            r = n * 4 + u
            to = [place_s[g][0, r] for g in range(tiles)]
            for g in range(tiles):
                xs[pl.ds(to[g], 1), :] = lines[pl.ds(g * 128 + r, 1), :]
        return 0

    lax.fori_loop(0, 128 // 4, place, 0)

    blk = blocks_of((ROWS, 128))
    even = (blk & 1) == 0
    lower = blk < 2

    def first_swap(b):
        x = [xs[pl.ds(pl.multiple_of(q * (BANDS * ROWS) + b * ROWS, ROWS), ROWS), :] for q in range(GROUP)]
        first = [jnp.where(lower, x[q], pltpu.roll(x[q + 2], 64, 1)) for q in (0, 1)]
        last = [jnp.where(lower, pltpu.roll(x[q], 64, 1), x[q + 2]) for q in (0, 1)]
        return first, last

    sends = []
    for part in range(BANDS // 8):
        bands = range(part * 8, part * 8 + 8)
        ahead = first_swap(bands[0])
        for b in bands:
            now = ahead
            if b + 1 in bands:
                ahead = first_swap(b + 1)
            for l, (u, w) in ((0, now[0]), (2, now[1])):
                held[b, l] = jnp.where(even, u, pltpu.roll(w, 32, 1))
                held[b, l + 1] = jnp.where(even, pltpu.roll(u, 96, 1), w)
            for l in range(LEVS):
                held[b, l, ROWS - 1 : ROWS, :] = heads[b : b + 1, :]
        some = pl.ds(part * 8, 8)
        sends.append(pltpu.make_async_copy(held.at[some], out.at[some], io_sem.at[1 + part]))
        sends[-1].start()
    for copy in sends:
        copy.wait()


def make_messages(turn, vals, owner, column, sigma, len_lev):
    rows = vals.shape[0]
    vmem = pl.BlockSpec(memory_space=pltpu.VMEM)
    return pl.pallas_call(
        send_kernel,
        out_shape=jax.ShapeDtypeStruct((BANDS, LEVS, ROWS, 128), jnp.float32),
        in_specs=[pl.BlockSpec(memory_space=pltpu.SMEM), pl.BlockSpec(memory_space=pltpu.HBM)] + [vmem] * 4,
        out_specs=pl.BlockSpec(memory_space=pltpu.HBM),
        scratch_shapes=[
            pltpu.VMEM((rows, 128), jnp.float32),
            pltpu.VMEM((BANDS, LEVS, ROWS, 128), jnp.float32),
            pltpu.VMEM((BANDS, 128), jnp.float32),
            pltpu.VMEM((288, NLAT), jnp.bfloat16),
            pltpu.VMEM((2, 256, 128), jnp.float32),
            pltpu.VMEM((rows, 128), jnp.float32),
            pltpu.VMEM((GROUP * BANDS * ROWS, 128), jnp.float32),
            pltpu.VMEM((rows // 64, 128), jnp.int32),
            pltpu.SemaphoreType.DMA((rows // 128,)),
            pltpu.SemaphoreType.DMA((1 + BANDS // 8,)),
        ]
        + [pltpu.SMEM((1, 128), jnp.int32)] * (rows // 128),
        compiler_params=pltpu.CompilerParams(vmem_limit_bytes=VMEM_LIMIT),
        name="make_messages",
    )(turn, vals, owner, column, sigma, len_lev)


def fold_lanes(a, b, first, by):
    return jnp.where(first, a, b) + pltpu.roll(jnp.where(first, b, a), by, 1)


def shift_down(x, by, sub):
    return jnp.where(sub >= by, pltpu.roll(x, by, 0), 0.0)


def shift_up(x, by, sub):
    return jnp.where(sub < 8 - by, pltpu.roll(x, 8 - by, 0), 0.0)


def grid_kernel(recv, lat_len, ends, grid, most, ga, gb, ups, downs, ids_v, sem, out_sem, *ids_s):
    heads = recv[:, ROWS - 1, :]
    lane = lax.broadcasted_iota(jnp.int32, (128, 128), 1)
    heads = jnp.where(lane == MOST_LANE, jnp.max(heads, axis=0, keepdims=True), heads)
    ids = jnp.transpose(heads).astype(jnp.int32)
    same = jnp.zeros((8, 128), jnp.bool_)
    for m in range(0, 128, 16):
        a, b = ids[m : m + 8], ids[m + 8 : m + 16]
        turned = pltpu.roll(b, 4, 0)
        same = same | ((a >= PAD) & ((a == pltpu.roll(a, 4, 0)) | (a == b) | (a == turned)))
        same = same | ((b >= PAD) & (b == turned))
    same = jnp.max(jnp.where(same, 1, 0), axis=0, keepdims=True)
    ids_v[...] = ids
    ids_v[SAME_LANE : SAME_LANE + 1, :] = same
    copies = [
        pltpu.make_async_copy(ids_v.at[pl.ds(GROUP * j, GROUP), :], ids_s[j], sem.at[j]) for j in range(ROWS)
    ]
    for copy in copies:
        copy.start()
    zeros = jnp.zeros((256, 128), jnp.float32)

    def clear(i, _):
        at = pl.ds(pl.multiple_of(PAD + i * 256, 8), 256)
        ga[at, :] = zeros
        gb[at, :] = zeros
        return 0

    lax.fori_loop(0, REGION // 256, clear, 0)
    ga[:PAD, :] = zeros[:PAD]
    gb[:PAD, :] = zeros[:PAD]
    for copy in copies:
        copy.wait()
    tail = ids_s[ROWS - 1]
    most[0] = tail[MOST_LANE - CAP, 0]

    lane_block = blocks_of((1, 128))
    masks = [lane_block == q for q in range(GROUP)]
    half = recv.shape[0] // 2

    def add_source(s, _):
        pair = ((s, ga), (s + half, gb))
        n = jnp.maximum(tail[COUNT_LANE - CAP, s], tail[COUNT_LANE - CAP, s + half])
        swaps = tail[SWAP_LANE - CAP, s] + tail[SWAP_LANE - CAP, s + half]
        sames = tail[SAME_LANE - CAP, s] + tail[SAME_LANE - CAP, s + half]

        def add_rows(lo, hi, batch):
            items = [(range(j, min(j + batch, hi)), x, g) for j in range(lo, hi, batch) for x, g in pair]

            def read(item):
                js, x, g = item
                at = [[pl.ds(ids_s[j][q, x], 1) for q in range(GROUP)] for j in js]
                return at, [[g[a, :] for a in some] for some in at], [recv[x, j : j + 1, :] for j in js]

            ahead = read(items[0])
            for k, (_, _, g) in enumerate(items):
                at, held, row = ahead
                if k + 1 < len(items):
                    ahead = read(items[k + 1])
                for m in range(len(row)):
                    for q in range(GROUP):
                        pltpu.store(g.at[at[m][q], :], held[m][q] + row[m], mask=masks[q])

        def add_message(batch):
            add_rows(0, 12, batch)
            for lo in range(12, ROWS - 1, 4):

                @pl.when(n > GROUP * lo)
                def _():
                    add_rows(lo, min(lo + 4, ROWS - 1), batch)

        @pl.when(swaps + sames == 0)
        def _():
            add_message(BATCH)

        @pl.when((swaps == 0) & (sames > 0))
        def _():
            add_message(1)

        @pl.when(swaps > 0)
        def _():
            for x, g in pair:
                for j in range(ROWS - 1):
                    row = recv[x, j : j + 1, :]
                    turned = pltpu.roll(row, PROF, 1)
                    for q in range(GROUP):
                        to = ids_s[j][q, x]
                        far = to >= GRID_ROWS
                        for at, what, mask in (
                            (jnp.where(far, 0, to), row, masks[q]),
                            (jnp.where(far, to - REGION, 0), turned, masks[(q + 1) % GROUP]),
                        ):
                            at = pl.ds(at, 1)
                            pltpu.store(g.at[at, :], g[at, :] + what, mask=mask)

        return 0

    lax.fori_loop(0, half, add_source, 0)

    im = 1.0 / in_lanes(lat_len)

    def power(n):
        return jnp.broadcast_to(jnp.exp(-im * n.astype(jnp.float32)), (8, 128))

    to_end = [power(BAND - 1 - 4 * i - lane_block) for i in range(TILES)]
    to_start = [power(4 * i + lane_block) for i in range(TILES)]
    blk = blocks_of((8, 128))
    even = (blk & 1) == 0
    lower = blk < 2
    out_copies = []
    for part in range(PARTS):

        def gather(r, _):
            rows = [part * (PLANE // PARTS) + (r * UNROLL + u) * 8 for u in range(UNROLL)]

            def fold(row):
                at = [pl.ds(pl.multiple_of(PAD + n * PLANE + row, 8), 8) for n in range(PAIRS)]
                g = [ga[a, :] + gb[a, :] for a in at]
                return [fold_lanes(g[2 * i], g[2 * i + 1], lower, 64) for i in range(TILES)]

            def put(row, cells):
                up = down = None
                for i, x in enumerate(cells):
                    up = to_end[i] * x if i == 0 else up + to_end[i] * x
                    down = to_start[i] * x if i == 0 else down + to_start[i] * x
                for i, x in enumerate(cells):
                    ga[pl.ds(pl.multiple_of(PAD + i * PLANE + row, 8), 8), :] = x
                here = pl.ds(pl.multiple_of(row, 8), 8)
                ups[here, :] = up
                downs[here, :] = down

            ahead = [fold(rows[0]), fold(rows[1])]
            for u, row in enumerate(rows):
                if u + 2 < UNROLL:
                    ahead.append(fold(rows[u + 2]))
                put(row, ahead[u])
            return 0

        lax.fori_loop(0, PLANE // PARTS // 8 // UNROLL, gather, 0)
        for i in range(TILES):
            first = i * PLANE + part * (PLANE // PARTS)
            out_copies.append(
                pltpu.make_async_copy(
                    ga.at[pl.ds(PAD + first, PLANE // PARTS), :],
                    grid.at[pl.ds(first, PLANE // PARTS), :],
                    out_sem.at[part * TILES + i],
                )
            )
            out_copies[-1].start()

    def pack(k, _):
        done = []
        for u in range(16):
            p = k * 16 + u
            row = (p >> 5) * (STEP * 8) + (p & 31) * 8
            sums = []
            for h in (0, 1):
                at = pl.ds(pl.multiple_of(row + h * (STEP * 4), 8), 8)
                sums.append(fold_lanes(ups[at, :], downs[at, :], even, 32))
            done.append(fold_lanes(sums[0], sums[1], lower, 64))
        for u, x in enumerate(done):
            ends[pl.ds(pl.multiple_of((k * 16 + u) * 8, 8), 8), :] = x
        return 0

    lax.fori_loop(0, SEGV * (STEP // 2) // 16, pack, 0)
    for copy in out_copies:
        copy.wait()


def to_grid(recv, lat_len):
    vmem = pl.BlockSpec(memory_space=pltpu.VMEM)
    smem = pl.BlockSpec(memory_space=pltpu.SMEM)
    return pl.pallas_call(
        grid_kernel,
        out_shape=(
            jax.ShapeDtypeStruct((NLON // 2, 128), jnp.float32),
            jax.ShapeDtypeStruct((TILES * PLANE, 128), jnp.float32),
            jax.ShapeDtypeStruct((1,), jnp.int32),
        ),
        in_specs=[vmem, smem],
        out_specs=(vmem, pl.BlockSpec(memory_space=pltpu.HBM), smem),
        scratch_shapes=[
            pltpu.VMEM((GRID_ROWS, 128), jnp.float32),
            pltpu.VMEM((GRID_ROWS, 128), jnp.float32),
            pltpu.VMEM((PLANE, 128), jnp.float32),
            pltpu.VMEM((PLANE, 128), jnp.float32),
            pltpu.VMEM((128, 128), jnp.int32),
            pltpu.SemaphoreType.DMA((ROWS,)),
            pltpu.SemaphoreType.DMA((PARTS * TILES,)),
        ]
        + [pltpu.SMEM((GROUP, 128), jnp.int32)] * ROWS,
        compiler_params=pltpu.CompilerParams(vmem_limit_bytes=32 * 1024 * 1024),
        name="to_grid",
    )(recv, lat_len)


def circle_carry(last, fades, backward):
    il, seg_fade, fade8, fade16, whole, sub = fades
    run, tail = [], []
    for x in last:
        for m, by in enumerate((1, 2, 4)):
            x = x + seg_fade[m] * (shift_up if backward else shift_down)(x, by, sub)
        run.append(x)
        tail.append(x[0:1] if backward else x[7:8])
    entering = []
    for sv in range(SEGV):
        order = [tail[(sv + n) % 3] if backward else tail[(sv - n) % 3] for n in (1, 2, 3)]
        c = (order[0] + fade8 * order[1] + fade16 * order[2]) * whole
        if backward:
            entering.append(shift_up(run[sv], 1, sub) + jnp.exp(-il * (STEP * (7.0 - sub.astype(jnp.float32)))) * c)
        else:
            entering.append(shift_down(run[sv], 1, sub) + jnp.exp(-il * (STEP * sub.astype(jnp.float32))) * c)
    return entering


def circle_fades(il):
    sub = lax.broadcasted_iota(jnp.int32, (8, 128), 0)
    seg_fade = [jnp.broadcast_to(jnp.exp(-il * float(STEP * m)), (8, 128)) for m in (1, 2, 4)]
    fade8 = jnp.exp(-il * float(STEP * 8))
    fade16 = jnp.exp(-il * float(STEP * 16))
    whole = 1.0 / (1.0 - jnp.exp(-il * float(NLON)))
    return il, seg_fade, fade8, fade16, whole, sub


def total_gain(il, im):
    one_lon, one_lat = jnp.exp(-il), jnp.exp(-im)
    return (1.0 - one_lon) * (1.0 - one_lon) * ((1.0 - one_lat) / (1.0 + one_lat))


def smooth_kernel(grid, lon_len, local, done, ramp, carry):
    il = 1.0 / in_lanes(lon_len)
    fade = jnp.broadcast_to(jnp.exp(-il), (8, 128))
    stepno = (lax.broadcasted_iota(jnp.int32, (STEP, 128), 0) + 1).astype(jnp.float32)
    ramp[...] = jnp.exp(-stepno * il)
    fades = circle_fades(il)
    vectors = [(i, sv) for i in range(SHARE) for sv in range(SEGV)]

    def at_row(i, sv, t):
        return pl.ds(pl.multiple_of(i * PLANE + sv * (STEP * 8) + t * 8, 8), 8)

    def forward(n, state):
        cells = []
        for u in range(4):
            cells.append([grid[at_row(i, sv, n * 4 + u), :] for i, sv in vectors])
        for u in range(4):
            state = tuple(fade * y + x for y, x in zip(state, cells[u]))
            cells[u] = state
        for u in range(4):
            for (i, sv), y in zip(vectors, cells[u]):
                local[at_row(i, sv, n * 4 + u), :] = y
        return state

    blank = tuple(jnp.zeros((8, 128), jnp.float32) for _ in vectors)
    state = lax.fori_loop(0, STEP // 4, forward, blank)
    for i in range(SHARE):
        for sv, x in enumerate(circle_carry(state[i * SEGV : (i + 1) * SEGV], fades, False)):
            carry[i * SEGV + sv] = x

    def backward(n, state):
        cells = []
        for u in range(4):
            t = STEP - 1 - n * 4 - u
            r = jnp.broadcast_to(ramp[pl.ds(t, 1), :], (8, 128))
            cells.append([local[at_row(i, sv, t), :] + r * carry[k] for k, (i, sv) in enumerate(vectors)])
        for u in range(4):
            state = tuple(fade * y + x for y, x in zip(state, cells[u]))
            cells[u] = state
        for u in range(4):
            for (i, sv), y in zip(vectors, cells[u]):
                local[at_row(i, sv, STEP - 1 - n * 4 - u), :] = y
        return state

    state = lax.fori_loop(0, STEP // 4, backward, blank)
    for i in range(SHARE):
        for sv, x in enumerate(circle_carry(state[i * SEGV : (i + 1) * SEGV], fades, True)):
            carry[i * SEGV + sv] = x

    def finish(n, _):
        cells = []
        for u in range(4):
            r = jnp.broadcast_to(ramp[pl.ds(STEP - 1 - n * 4 - u, 1), :], (8, 128))
            cells.append([local[at_row(i, sv, n * 4 + u), :] + r * carry[k] for k, (i, sv) in enumerate(vectors)])
        for u in range(4):
            for (i, sv), y in zip(vectors, cells[u]):
                local[at_row(i, sv, n * 4 + u), :] = y
        return 0

    lax.fori_loop(0, STEP // 4, finish, 0)
    done[...] = fade


def smooth_band(grid, lon_len):
    return pl.pallas_call(
        smooth_kernel,
        grid=(TILES // SHARE,),
        out_shape=(
            jax.ShapeDtypeStruct((TILES * PLANE, 128), jnp.float32),
            jax.ShapeDtypeStruct((8, 128), jnp.float32),
        ),
        in_specs=[
            pl.BlockSpec((SHARE * PLANE, 128), lambda n: (n, 0)),
            pl.BlockSpec(memory_space=pltpu.SMEM),
        ],
        out_specs=(
            pl.BlockSpec((SHARE * PLANE, 128), lambda n: (n, 0)),
            pl.BlockSpec(memory_space=pltpu.VMEM),
        ),
        scratch_shapes=[
            pltpu.VMEM((STEP, 128), jnp.float32),
            pltpu.VMEM((SHARE * SEGV, 8, 128), jnp.float32),
        ],
        compiler_params=pltpu.CompilerParams(vmem_limit_bytes=VMEM_LIMIT),
        cost_estimate=pl.CostEstimate(flops=20_000_000, bytes_accessed=9_400_000, transcendentals=0),
        name="smooth_band",
    )(grid, lon_len)


def bands_kernel(ends, lat_len, _, out):
    im = 1.0 / in_lanes(lat_len)
    shape = ends.shape[1:]
    hop = jnp.broadcast_to(jnp.exp(-im * float(BAND)), shape)
    is_up = (blocks_of(shape) & 1) == 1
    acc = jnp.zeros(shape, jnp.float32)
    south = []
    for b in range(BANDS):
        south.append(acc)
        acc = hop * acc + ends[b]
    total = pltpu.roll(acc, PROF, 1)
    acc = jnp.zeros(shape, jnp.float32)
    for b in range(BANDS - 1, -1, -1):
        edge = jnp.exp(-im * float(BAND * (BANDS - 1 - b) + 1))
        out[b] = jnp.where(is_up, acc - edge * total, south[b])
        acc = hop * acc + ends[b]


def join_bands(ends, lat_len, after):
    vmem = pl.BlockSpec(memory_space=pltpu.VMEM)
    return pl.pallas_call(
        bands_kernel,
        out_shape=jax.ShapeDtypeStruct(ends.shape, jnp.float32),
        in_specs=[vmem, pl.BlockSpec(memory_space=pltpu.SMEM), pl.BlockSpec(memory_space=pltpu.HBM)],
        out_specs=vmem,
        compiler_params=pltpu.CompilerParams(vmem_limit_bytes=8 * 1024 * 1024),
        name="join_bands",
    )(ends, lat_len, after)


def turn_kernel(local, control, lon_len, lat_len, out, flipped):
    m = pl.program_id(0)
    for side in range(WIDE):
        sub = (m % (4 // WIDE) * WIDE + side) * 2
        for i in range(TILES):
            x = jnp.concatenate(
                [local[i, pl.ds(sub, STEP, stride=8), :], local[i, pl.ds(sub + 1, STEP, stride=8), :]], axis=0
            )
            flipped[side, i * 128 : (i + 1) * 128, :] = jnp.transpose(x)
    for o in range(0, PROF, 8):
        il = 1.0 / in_rows(lon_len, o)
        im = 1.0 / in_rows(lat_len, o)
        fade = jnp.exp(-im)
        gain = total_gain(il, im)
        for side in range(WIDE):
            x = [flipped[side, n * PROF + o : n * PROF + o + 8, :] for n in range(BAND)]
            south = [x[0]]
            for n in range(1, BAND):
                south.append(fade * south[-1] + x[n])
            north = jnp.zeros((8, 128), jnp.float32)
            for n in range(BAND - 1, -1, -1):
                north = fade * north
                flipped[side, n * PROF + o : n * PROF + o + 8, :] = (south[n] + north) * gain
                north = north + x[n]
    for v in range(PROF):
        for g in range(BAND // 8):
            for side in range(WIDE):
                x = flipped[side, pl.ds(v + 8 * PROF * g, 8, stride=PROF), :]
                f, k, lats, lanes = v // LEVQ, v % LEVQ, slice(8 * g, 8 * g + 8), slice(128 * side, 128 * side + 128)
                out[f, k, lats, lanes] = control[f, k, lats, lanes] + x


def add_control(local, control, lon_len, lat_len):
    block = pl.BlockSpec((F, LEVQ, BAND, 128 * WIDE), lambda m: (0, 0, 0, m))
    smem = pl.BlockSpec(memory_space=pltpu.SMEM)
    return pl.pallas_call(
        turn_kernel,
        grid=(NLON // 128 // WIDE,),
        out_shape=jax.ShapeDtypeStruct(control.shape, jnp.float32),
        in_specs=[
            pl.BlockSpec((TILES, STEP * 8, 128), lambda m: (0, m // (4 // WIDE), 0)),
            block,
            smem,
            smem,
        ],
        out_specs=block,
        scratch_shapes=[pltpu.VMEM((WIDE, BAND * PROF, 128), jnp.float32)],
        compiler_params=pltpu.CompilerParams(vmem_limit_bytes=VMEM_LIMIT),
        cost_estimate=pl.CostEstimate(flops=20_000_000, bytes_accessed=15_000_000, transcendentals=0),
        name="add_control",
    )(local.reshape(TILES, PLANE, 128), control, lon_len, lat_len)


def last_kernel(lat_len, lon_len, parts, joined, out, held, from_start, from_end, ys, south, north, sem):
    half = STEP // 2
    per = LEVQ // 4
    chunks = [(k // 4, pl.ds(k % 4 * per, per)) for k in range(F * 4)]
    fetches = [pltpu.make_async_copy(parts.at[c], held.at[c], sem.at[0, k]) for k, c in enumerate(chunks)]
    stores = [pltpu.make_async_copy(held.at[c], out.at[c], sem.at[1, k]) for k, c in enumerate(chunks)]
    for copy in fetches:
        copy.start()

    lat = lax.broadcasted_iota(jnp.int32, (BAND, 128), 0).astype(jnp.float32)
    for v in range(PROF):
        scale = lat_len[v // LEVQ, v % LEVQ]
        from_start[v] = jnp.exp(-(lat + 1.0) / scale)
        from_end[v] = jnp.exp(-(float(BAND) - lat) / scale)

    il = 1.0 / in_lanes(lon_len)
    im = 1.0 / in_lanes(lat_len)
    fade = jnp.broadcast_to(jnp.exp(-il), (8, 128))
    fades = circle_fades(il)
    half_fade = jnp.broadcast_to(jnp.exp(-il * float(half)), (8, 128))
    first = blocks_of((8, 128)) < 2
    gain = total_gain(il, im)

    def rows_at(sv, p):
        return slice(sv * (half * 8) + p * 8, sv * (half * 8) + p * 8 + 8)

    def enter(last, backward):
        other = [pltpu.roll(x, 64, 1) for x in last]
        early = jnp.logical_not(first) if backward else first
        full = [jnp.where(early, o + half_fade * x, x + half_fade * o) for x, o in zip(last, other)]
        into = circle_carry(full, fades, backward)
        return [jnp.where(early, c, o + half_fade * c) for c, o in zip(into, other)]

    y = [jnp.zeros((8, 128), jnp.float32)] * SEGV
    for p in range(half):
        for sv in range(SEGV):
            y[sv] = fade * y[sv] + joined[rows_at(sv, p), :]
            ys[rows_at(sv, p), :] = y[sv]
    into = enter(y, False)
    y = [jnp.zeros((8, 128), jnp.float32)] * SEGV
    for p in range(half - 1, -1, -1):
        r = jnp.exp(-il * float(p + 1))
        for sv in range(SEGV):
            y[sv] = fade * y[sv] + (ys[rows_at(sv, p), :] + r * into[sv])
            ys[rows_at(sv, p), :] = y[sv]
    into = enter(y, True)
    for p in range(half):
        r = jnp.exp(-il * float(half - p))
        for sv in range(SEGV):
            ys[rows_at(sv, p), :] = (ys[rows_at(sv, p), :] + r * into[sv]) * gain
    for m in range(NLON // 128):
        pieces = []
        for s in (0, 1):
            x = ys[pl.ds(m // 4 * (half * 8) + m % 4 * 2 + s, half, stride=8), :]
            pieces += [x, pltpu.roll(x, 64, 1)]
        x = jnp.transpose(jnp.concatenate(pieces, axis=0))
        south[m] = x[0:PROF]
        north[m] = x[PROF : 2 * PROF]

    for n, fetch in enumerate(fetches):
        fetch.wait()
        for k in range(per):
            v = n * per + k
            f, level = v // LEVQ, v % LEVQ
            up, down = from_start[v], from_end[v]
            for m in range(NLON // 128):
                lanes = slice(m * 128, (m + 1) * 128)
                held[f, level, :, lanes] = held[f, level, :, lanes] + (
                    up * south[m, v : v + 1, :] + down * north[m, v : v + 1, :]
                )
        stores[n].start()
    for copy in stores:
        copy.wait()


def add_bands(lat_len, lon_len, parts, joined):
    smem = pl.BlockSpec(memory_space=pltpu.SMEM)
    vmem = pl.BlockSpec(memory_space=pltpu.VMEM)
    hbm = pl.BlockSpec(memory_space=pltpu.HBM)
    return pl.pallas_call(
        last_kernel,
        out_shape=jax.ShapeDtypeStruct(parts.shape, jnp.float32),
        in_specs=[smem, smem, hbm, vmem],
        out_specs=hbm,
        scratch_shapes=[
            pltpu.VMEM(parts.shape, jnp.float32),
            pltpu.VMEM((PROF, BAND, 128), jnp.float32),
            pltpu.VMEM((PROF, BAND, 128), jnp.float32),
            pltpu.VMEM((NLON // 2, 128), jnp.float32),
            pltpu.VMEM((NLON // 128, PROF, 128), jnp.float32),
            pltpu.VMEM((NLON // 128, PROF, 128), jnp.float32),
            pltpu.SemaphoreType.DMA((2, F * 4)),
        ],
        compiler_params=pltpu.CompilerParams(vmem_limit_bytes=32 * 1024 * 1024),
        name="add_bands",
    )(lat_len, lon_len, parts, joined)


def per_device(control, obs_values, obs_owner, obs_column, sigma, len_lon, len_lat, len_lev):
    owner = obs_owner.reshape(1, -1)
    column = obs_column.reshape(1, -1)
    sigma = sigma.reshape(F * NLEV, NLAT)
    def one_turn(turn):
        messages = make_messages(turn.reshape(1), obs_values, owner, column, sigma, len_lev)
        messages = messages.reshape(BANDS * LEVS, ROWS, 128)
        arrived = lax.all_to_all(messages, ("lat", "lev"), split_axis=0, concat_axis=0, tiled=True)
        ends, grid, most = to_grid(arrived, len_lat)
        return ends, grid, most[0]

    ends, grid, most = one_turn(jnp.int32(0))

    def more(state):
        return state[0] * CAP < most

    def next_turn(state):
        turn, ends, grid = state
        more_ends, more_grid, _ = one_turn(turn)
        return turn + 1, ends + more_ends, grid + more_grid

    _, ends, grid = lax.while_loop(more, next_turn, (jnp.int32(1), ends, grid))

    ends = ends.reshape(BANDS, -1, 128)
    ends = lax.all_to_all(ends, "lat", split_axis=0, concat_axis=0, tiled=True)
    local, done = smooth_band(grid, len_lon)
    joined = join_bands(ends, len_lat, done)
    joined = lax.all_to_all(joined, "lat", split_axis=0, concat_axis=0, tiled=True)
    parts = add_control(local, control, len_lon, len_lat)
    return add_bands(len_lat, len_lon, parts, joined.reshape(NLON // 2, 128))


def solution(mesh):
    placed = (
        P(None, "lev", "lat", None),
        P(("lat", "lev"), None),
        P(("lat", "lev"), None),
        P(("lat", "lev")),
        P(),
        P(None, "lev"),
        P(None, "lev"),
        P(),
    )
    return jax.shard_map(
        per_device,
        mesh=mesh,
        in_specs=placed,
        out_specs=P(None, "lev", "lat", None),
        check_vma=False,
    )
```

```python
import jax
import jax.numpy as jnp
from jax import lax
from jax.experimental import pallas as pl
from jax.experimental.pallas import tpu as pltpu
from jax.sharding import PartitionSpec as P

F = 4
NLEV = 32
NLAT = 768
NLON = 1536
BANDS = 32
LEVS = 4
BAND = NLAT // BANDS
LEVQ = NLEV // LEVS
PROF = F * LEVQ
GROUP = 128 // PROF
ROWS = 32
CAP = (ROWS - 1) * GROUP
COUNT_LANE = 124
MOST_LANE = 125
STEP = 64
SEGV = 3
TILES = BAND // GROUP
PLANE = NLON
VMEM_LIMIT = 58 * 1024 * 1024
PAD = 8
REGION = BAND // 2 * PLANE
GRID_ROWS = REGION + PAD
HALF_CAP = CAP // 2
SWAP_LANE = 126
SAME_LANE = 127
BATCH = 3
SHARE = 2
WIDE = 4
UNROLL = 8
FIRST, NEXT = 18, 6
PARTS = 3
PAIRS = BAND // 2


def third(x):
    return (x * 21846) >> 16


def blocks_of(shape):
    return lax.broadcasted_iota(jnp.int32, shape, len(shape) - 1) // PROF


def in_lanes(lengths):
    value = lax.broadcasted_iota(jnp.int32, (1, 128), 1) & (PROF - 1)
    x = jnp.ones((1, 128), jnp.float32)
    for v in range(PROF):
        x = jnp.where(value == v, lengths[v // LEVQ, v % LEVQ], x)
    return x


def in_rows(lengths, first):
    row = lax.broadcasted_iota(jnp.int32, (8, 128), 0)
    x = jnp.ones((8, 128), jnp.float32)
    for v in range(8):
        x = jnp.where(row == v, lengths[(first + v) // LEVQ, (first + v) % LEVQ], x)
    return x


def send_kernel(
    turn, vals_in, owner, column, sigma, len_lev, out, vals, held, heads, picks, lines, xs, places, sem, io_sem, *more
):
    stage_a, stage_b, work_a, work_b, fades_a, fades_b = more[:6]
    place_s = more[6:]
    rows = vals.shape[0]
    take = pltpu.make_async_copy(vals_in, vals, io_sem.at[0])
    take.start()
    tiles = rows // 128
    turn_no = turn[0]

    d = owner[...]
    c = column[...]
    c48 = third(c >> 4)
    lat = (d & 3) * 192 + c48
    lon = (d >> 2) * 48 + (c - c48 * 48)
    band = third(lat >> 3)
    seg = lon >> 6
    grid_row = ((seg >> 3) * STEP + (lon & (STEP - 1))) * 8 + (seg & 7)
    odd = lat & 1
    address = ((lat - band * BAND) >> 1) * PLANE + grid_row + PAD

    width = 256
    r0 = lax.broadcasted_iota(jnp.int32, (width, width), 0)
    r1 = lax.broadcasted_iota(jnp.int32, (width, width), 1)
    earlier = jnp.where(r0 < r1, 1.0, 0.0).astype(jnp.bfloat16)
    band_id = lax.broadcasted_iota(jnp.int32, (BANDS, width), 0)
    place_id = lax.broadcasted_iota(jnp.int32, (128, width), 0)
    base = jnp.zeros((BANDS, 1), jnp.float32)
    half_base = jnp.zeros((2 * BANDS, 1), jnp.float32)
    found = jnp.zeros((2 * BANDS, 128), jnp.float32)
    for k in range(rows // width):
        cut = slice(k * width, (k + 1) * width)
        hot = jnp.where(band[:, cut] == band_id, 1.0, 0.0)
        before = jnp.dot(hot.astype(jnp.bfloat16), earlier, preferred_element_type=jnp.float32) + base
        rank = jnp.sum(hot * before, axis=0, keepdims=True).astype(jnp.int32) - turn_no * CAP
        base = base + jnp.sum(hot, axis=1, keepdims=True)
        now = (rank >= 0) & (rank < CAP)
        parity = odd[:, cut]
        hot = jnp.where(now, hot, 0.0)
        sides = jnp.concatenate([jnp.where(parity == 0, hot, 0.0), jnp.where(parity == 1, hot, 0.0)], axis=0)
        before = jnp.dot(sides.astype(jnp.bfloat16), earlier, preferred_element_type=jnp.float32) + half_base
        rank = jnp.sum(sides * before, axis=0, keepdims=True).astype(jnp.int32)
        half_base = half_base + jnp.sum(sides, axis=1, keepdims=True)
        swapped = rank >= HALF_CAP
        pos = jnp.where(swapped, CAP - 1 - rank, rank)
        q = 2 * (pos & 1) + jnp.where(swapped, 1 - parity, parity)
        row = pos >> 1
        slot = jnp.where(now, q * (BANDS * ROWS) + band[:, cut] * ROWS + row, ROWS - 1)
        for g in range(width // 128):
            n = k * (width // 128) + g
            places[n : n + 1, :] = slot[:, g * 128 : (g + 1) * 128]
            places[tiles + n : tiles + n + 1, :] = lat[:, cut][:, g * 128 : (g + 1) * 128]
        a = address[:, cut] + jnp.where(swapped, REGION, 0)
        high = hot * (a >> 8).astype(jnp.float32)
        low = hot * (a & 255).astype(jnp.float32)
        both = jnp.concatenate([high, low], axis=0).astype(jnp.bfloat16)
        at_place = jnp.where(row * GROUP + q == place_id, 1.0, 0.0).astype(jnp.bfloat16)
        found = found + lax.dot_general(
            both, at_place, (((1,), (1,)), ((), ())), preferred_element_type=jnp.float32
        )
    copies = [
        pltpu.make_async_copy(places.at[pl.ds(n, 1), :], place_s[n], sem.at[n]) for n in range(tiles)
    ]
    for copy in copies:
        copy.start()
    headers = found[:BANDS] * 256.0 + found[BANDS:]
    lane = lax.broadcasted_iota(jnp.int32, (BANDS, 128), 1)
    most_side = jnp.maximum(half_base[:BANDS], half_base[BANDS:])
    left = jnp.minimum(2.0 * most_side, float(CAP))
    swaps = jnp.where(most_side > float(HALF_CAP), 1.0, 0.0)
    most = jnp.max(base, axis=0, keepdims=True)
    headers = jnp.where(lane < CAP, headers, 0.0)
    headers = jnp.where(lane == COUNT_LANE, left, headers)
    headers = jnp.where(lane == MOST_LANE, most, headers)
    headers = jnp.where(lane == SWAP_LANE, swaps, headers)
    heads[0] = headers
    place_no = jnp.where(lane < CAP, lane & 3, 1)
    headers = jnp.where(place_no == 2, pltpu.roll(headers, 2, 1), jnp.where(place_no == 0, pltpu.roll(headers, 126, 1), headers))
    heads[1] = headers

    sig = sigma[...]
    sig_hi = sig.astype(jnp.bfloat16)
    picks[0:128, :] = sig_hi
    picks[128:256, :] = (sig - sig_hi.astype(jnp.float32)).astype(jnp.bfloat16)
    fade = jnp.exp(-1.0 / len_lev[...])
    fade = jnp.concatenate([fade, fade], axis=0)
    f_hi = fade.astype(jnp.bfloat16).astype(jnp.float32)
    f_mid = (fade - f_hi).astype(jnp.bfloat16).astype(jnp.float32)
    f_lo = fade - f_hi - f_mid
    picks[256:288, :] = jnp.concatenate([f_hi, f_mid, f_lo, jnp.zeros_like(fade)], axis=0).astype(jnp.bfloat16)
    lat_id = lax.broadcasted_iota(jnp.int32, (NLAT, width), 0)

    def pick(k, stage, fades):
        which = jnp.concatenate([places[pl.ds(tiles + 2 * k + g, 1), :] for g in (0, 1)], axis=1)
        at_lat = jnp.where(lat_id == which, 1.0, 0.0).astype(jnp.bfloat16)
        got = jnp.dot(picks[...], at_lat, preferred_element_type=jnp.float32)
        for g in (0, 1):
            lanes = slice(g * 128, (g + 1) * 128)
            at = pl.ds(pl.multiple_of(k * width + g * 128, 128), 128)
            stage[g] = jnp.transpose(vals[at, :]) * (got[0:128, lanes] + got[128:256, lanes])
        fades[...] = got[256:264, :] + got[264:272, :] + got[272:280, :]

    def smooth_levels(k, stage, fades, work):
        for g in (0, 1):
            side = work.at[g]
            a = fades[0:F, g * 128 : (g + 1) * 128]
            y = [stage[g, pl.ds(0, F, stride=NLEV), :]]
            for n in range(1, NLEV):
                y.append(a * y[-1] + stage[g, pl.ds(n, F, stride=NLEV), :])
            gain = (1.0 - a) * (1.0 - a)
            w = y[-1]
            for n in range(NLEV - 1, -1, -1):
                if n < NLEV - 1:
                    w = a * w + y[n]
                side[pl.ds(n // LEVQ * PROF + n % LEVQ, F, stride=LEVQ), :] = w * gain
        for g in (0, 1):
            lines[pl.ds(pl.multiple_of(k * width + g * 128, 128), 128), :] = jnp.transpose(work[g])

    def two_blocks(n, _):
        pick(2 * n + 1, stage_b, fades_b)
        smooth_levels(2 * n, stage_a, fades_a, work_a)
        pick(jnp.minimum(2 * n + 2, rows // width - 1), stage_a, fades_a)
        smooth_levels(2 * n + 1, stage_b, fades_b, work_b)
        return 0

    take.wait()
    pick(0, stage_a, fades_a)
    lax.fori_loop(0, rows // width // 2, two_blocks, 0)

    zeros = jnp.zeros((128, 128), jnp.float32)

    def clear(i, _):
        xs[pl.ds(pl.multiple_of(i * 128, 128), 128), :] = zeros
        return 0

    lax.fori_loop(0, xs.shape[0] // 128, clear, 0)
    for copy in copies:
        copy.wait()

    def place(n, _):
        for u in range(4):
            r = n * 4 + u
            to = [place_s[g][0, r] for g in range(tiles)]
            for g in range(tiles):
                xs[pl.ds(to[g], 1), :] = lines[pl.ds(g * 128 + r, 1), :]
        return 0

    lax.fori_loop(0, 128 // 4, place, 0)

    blk = blocks_of((ROWS, 128))
    even = (blk & 1) == 0
    lower = blk < 2

    def swap(a, b, keep, by):
        turned = pltpu.roll(jnp.where(keep, b, a), by, 1)
        return jnp.where(keep, a, turned), jnp.where(keep, turned, b)

    def first_swap(b):
        x = [xs[pl.ds(pl.multiple_of(q * (BANDS * ROWS) + b * ROWS, ROWS), ROWS), :] for q in range(GROUP)]
        pairs = [swap(x[q], x[q + 2], lower, 64) for q in (0, 1)]
        return [p[0] for p in pairs], [p[1] for p in pairs]

    sends = []
    for part in range(BANDS // 8):
        bands = range(part * 8, part * 8 + 8)
        ahead = first_swap(bands[0])
        for b in bands:
            now = ahead
            if b + 1 in bands:
                ahead = first_swap(b + 1)
            for l, (u, w) in ((0, now[0]), (2, now[1])):
                held[b, l], held[b, l + 1] = swap(u, w, even, 32)
            for l in range(LEVS):
                held[b, l, ROWS - 1 : ROWS, :] = heads[l % 2, b : b + 1, :]
        some = pl.ds(part * 8, 8)
        sends.append(pltpu.make_async_copy(held.at[some], out.at[some], io_sem.at[1 + part]))
        sends[-1].start()
    for copy in sends:
        copy.wait()


def make_messages(turn, vals, owner, column, sigma, len_lev):
    rows = vals.shape[0]
    vmem = pl.BlockSpec(memory_space=pltpu.VMEM)
    return pl.pallas_call(
        send_kernel,
        out_shape=jax.ShapeDtypeStruct((BANDS, LEVS, ROWS, 128), jnp.float32),
        in_specs=[pl.BlockSpec(memory_space=pltpu.SMEM), pl.BlockSpec(memory_space=pltpu.HBM)] + [vmem] * 4,
        out_specs=pl.BlockSpec(memory_space=pltpu.HBM),
        scratch_shapes=[
            pltpu.VMEM((rows, 128), jnp.float32),
            pltpu.VMEM((BANDS, LEVS, ROWS, 128), jnp.float32),
            pltpu.VMEM((2, BANDS, 128), jnp.float32),
            pltpu.VMEM((288, NLAT), jnp.bfloat16),
            pltpu.VMEM((rows, 128), jnp.float32),
            pltpu.VMEM((GROUP * BANDS * ROWS, 128), jnp.float32),
            pltpu.VMEM((rows // 64, 128), jnp.int32),
            pltpu.SemaphoreType.DMA((rows // 128,)),
            pltpu.SemaphoreType.DMA((1 + BANDS // 8,)),
        ]
        + [pltpu.VMEM((2, 128, 128), jnp.float32)] * 4
        + [pltpu.VMEM((8, 256), jnp.float32)] * 2
        + [pltpu.SMEM((1, 128), jnp.int32)] * (rows // 128),
        compiler_params=pltpu.CompilerParams(vmem_limit_bytes=VMEM_LIMIT),
        name="make_messages",
    )(turn, vals, owner, column, sigma, len_lev)


def fold_lanes(a, b, first, by):
    return jnp.where(first, a, b) + pltpu.roll(jnp.where(first, b, a), by, 1)


def shift_down(x, by, sub):
    return jnp.where(sub >= by, pltpu.roll(x, by, 0), 0.0)


def shift_up(x, by, sub):
    return jnp.where(sub < 8 - by, pltpu.roll(x, 8 - by, 0), 0.0)


def grid_kernel(recv, lat_len, ends, grid, most, ga, gb, ups, downs, ids_v, sem, out_sem, *ids_s):
    heads = recv[:, ROWS - 1, :]
    lane = lax.broadcasted_iota(jnp.int32, (128, 128), 1)
    heads = jnp.where(lane == MOST_LANE, jnp.max(heads, axis=0, keepdims=True), heads)
    ids = jnp.transpose(heads).astype(jnp.int32)
    same = jnp.zeros((8, 128), jnp.bool_)
    for m in range(0, 128, 8):
        a = ids[m : m + 8]
        again = a == pltpu.roll(a, 4, 0)
        if m < 120:
            b = ids[m + 8 : m + 16]
            again = again | (a == b) | (a == pltpu.roll(b, 4, 0))
        same = same | ((a >= PAD) & again)
    same = jnp.max(jnp.where(same, 1, 0), axis=0, keepdims=True)
    ids_v[...] = ids
    ids_v[SAME_LANE : SAME_LANE + 1, :] = same
    copies = [
        pltpu.make_async_copy(ids_v.at[pl.ds(GROUP * j, GROUP), :], ids_s[j], sem.at[j]) for j in range(ROWS)
    ]
    for copy in copies:
        copy.start()
    zeros = jnp.zeros((256, 128), jnp.float32)

    def clear(i, _):
        at = pl.ds(pl.multiple_of(PAD + i * 256, 8), 256)
        ga[at, :] = zeros
        gb[at, :] = zeros
        return 0

    lax.fori_loop(0, REGION // 256, clear, 0)
    ga[:PAD, :] = zeros[:PAD]
    gb[:PAD, :] = zeros[:PAD]
    for copy in copies:
        copy.wait()
    tail = ids_s[ROWS - 1]
    most[0] = tail[MOST_LANE - CAP, 0]

    lane_block = blocks_of((1, 128))
    masks = [lane_block == q for q in range(GROUP)]
    half = recv.shape[0] // 2

    def add_source(s, _):
        pair = ((s, ga), (s + half, gb))
        n = jnp.maximum(tail[COUNT_LANE - CAP, s], tail[COUNT_LANE - CAP, s + half])
        swaps = tail[SWAP_LANE - CAP, s] + tail[SWAP_LANE - CAP, s + half]
        sames = tail[SAME_LANE - CAP, s] + tail[SAME_LANE - CAP, s + half]

        def add_rows(lo, hi, batch):
            items = [(range(j, min(j + batch, hi)), x, g) for j in range(lo, hi, batch) for x, g in pair]

            def read(item):
                js, x, g = item
                at = [[pl.ds(ids_s[j][q, x], 1) for q in range(GROUP)] for j in js]
                return at, [[g[a, :] for a in some] for some in at], [recv[x, j : j + 1, :] for j in js]

            ahead = read(items[0])
            for k, (_, _, g) in enumerate(items):
                at, held, row = ahead
                if k + 1 < len(items):
                    ahead = read(items[k + 1])
                for m in range(len(row)):
                    for q in range(GROUP):
                        pltpu.store(g.at[at[m][q], :], held[m][q] + row[m], mask=masks[q])

        def add_message(batch):
            add_rows(0, FIRST, batch)
            for lo in range(FIRST, ROWS - 1, NEXT):

                @pl.when(n > GROUP * lo)
                def _():
                    add_rows(lo, min(lo + NEXT, ROWS - 1), batch)

        @pl.when(swaps + sames == 0)
        def _():
            add_message(BATCH)

        @pl.when((swaps == 0) & (sames > 0))
        def _():
            add_message(1)

        @pl.when(swaps > 0)
        def _():
            for x, g in pair:
                for j in range(ROWS - 1):
                    row = recv[x, j : j + 1, :]
                    turned = pltpu.roll(row, PROF, 1)
                    for q in range(GROUP):
                        to = ids_s[j][q, x]
                        far = to >= GRID_ROWS
                        for at, what, mask in (
                            (jnp.where(far, 0, to), row, masks[q]),
                            (jnp.where(far, to - REGION, 0), turned, masks[(q + 1) % GROUP]),
                        ):
                            at = pl.ds(at, 1)
                            pltpu.store(g.at[at, :], g[at, :] + what, mask=mask)

        return 0

    lax.fori_loop(0, half, add_source, 0)

    im = 1.0 / in_lanes(lat_len)

    def power(n):
        return jnp.broadcast_to(jnp.exp(-im * n.astype(jnp.float32)), (8, 128))

    to_end = [power(BAND - 1 - 4 * i - lane_block) for i in range(TILES)]
    to_start = [power(4 * i + lane_block) for i in range(TILES)]
    blk = blocks_of((8, 128))
    even = (blk & 1) == 0
    lower = blk < 2
    out_copies = []
    for part in range(PARTS):

        def gather(r, _):
            rows = [part * (PLANE // PARTS) + (r * UNROLL + u) * 8 for u in range(UNROLL)]

            def fold(row):
                at = [pl.ds(pl.multiple_of(PAD + n * PLANE + row, 8), 8) for n in range(PAIRS)]
                g = [ga[a, :] + gb[a, :] for a in at]
                return [fold_lanes(g[2 * i], g[2 * i + 1], lower, 64) for i in range(TILES)]

            def put(row, cells):
                up = down = None
                for i, x in enumerate(cells):
                    up = to_end[i] * x if i == 0 else up + to_end[i] * x
                    down = to_start[i] * x if i == 0 else down + to_start[i] * x
                for i, x in enumerate(cells):
                    ga[pl.ds(pl.multiple_of(PAD + i * PLANE + row, 8), 8), :] = x
                here = pl.ds(pl.multiple_of(row, 8), 8)
                ups[here, :] = up
                downs[here, :] = down

            ahead = [fold(rows[0]), fold(rows[1])]
            for u, row in enumerate(rows):
                if u + 2 < UNROLL:
                    ahead.append(fold(rows[u + 2]))
                put(row, ahead[u])
            return 0

        lax.fori_loop(0, PLANE // PARTS // 8 // UNROLL, gather, 0)
        for i in range(TILES):
            first = i * PLANE + part * (PLANE // PARTS)
            out_copies.append(
                pltpu.make_async_copy(
                    ga.at[pl.ds(PAD + first, PLANE // PARTS), :],
                    grid.at[pl.ds(first, PLANE // PARTS), :],
                    out_sem.at[part * TILES + i],
                )
            )
            out_copies[-1].start()

    def pack(k, _):
        done = []
        for u in range(16):
            p = k * 16 + u
            row = (p >> 5) * (STEP * 8) + (p & 31) * 8
            sums = []
            for h in (0, 1):
                at = pl.ds(pl.multiple_of(row + h * (STEP * 4), 8), 8)
                sums.append(fold_lanes(ups[at, :], downs[at, :], even, 32))
            done.append(fold_lanes(sums[0], sums[1], lower, 64))
        for u, x in enumerate(done):
            ends[pl.ds(pl.multiple_of((k * 16 + u) * 8, 8), 8), :] = x
        return 0

    lax.fori_loop(0, SEGV * (STEP // 2) // 16, pack, 0)
    for copy in out_copies:
        copy.wait()


def to_grid(recv, lat_len):
    vmem = pl.BlockSpec(memory_space=pltpu.VMEM)
    smem = pl.BlockSpec(memory_space=pltpu.SMEM)
    return pl.pallas_call(
        grid_kernel,
        out_shape=(
            jax.ShapeDtypeStruct((NLON // 2, 128), jnp.float32),
            jax.ShapeDtypeStruct((TILES * PLANE, 128), jnp.float32),
            jax.ShapeDtypeStruct((1,), jnp.int32),
        ),
        in_specs=[vmem, smem],
        out_specs=(vmem, pl.BlockSpec(memory_space=pltpu.HBM), smem),
        scratch_shapes=[
            pltpu.VMEM((GRID_ROWS, 128), jnp.float32),
            pltpu.VMEM((GRID_ROWS, 128), jnp.float32),
            pltpu.VMEM((PLANE, 128), jnp.float32),
            pltpu.VMEM((PLANE, 128), jnp.float32),
            pltpu.VMEM((128, 128), jnp.int32),
            pltpu.SemaphoreType.DMA((ROWS,)),
            pltpu.SemaphoreType.DMA((PARTS * TILES,)),
        ]
        + [pltpu.SMEM((GROUP, 128), jnp.int32)] * ROWS,
        compiler_params=pltpu.CompilerParams(vmem_limit_bytes=32 * 1024 * 1024),
        name="to_grid",
    )(recv, lat_len)


def circle_carry(last, fades, backward):
    il, seg_fade, fade8, fade16, whole, sub = fades
    run, tail = [], []
    for x in last:
        for m, by in enumerate((1, 2, 4)):
            x = x + seg_fade[m] * (shift_up if backward else shift_down)(x, by, sub)
        run.append(x)
        tail.append(x[0:1] if backward else x[7:8])
    entering = []
    for sv in range(SEGV):
        order = [tail[(sv + n) % 3] if backward else tail[(sv - n) % 3] for n in (1, 2, 3)]
        c = (order[0] + fade8 * order[1] + fade16 * order[2]) * whole
        if backward:
            entering.append(shift_up(run[sv], 1, sub) + jnp.exp(-il * (STEP * (7.0 - sub.astype(jnp.float32)))) * c)
        else:
            entering.append(shift_down(run[sv], 1, sub) + jnp.exp(-il * (STEP * sub.astype(jnp.float32))) * c)
    return entering


def circle_fades(il):
    sub = lax.broadcasted_iota(jnp.int32, (8, 128), 0)
    seg_fade = [jnp.broadcast_to(jnp.exp(-il * float(STEP * m)), (8, 128)) for m in (1, 2, 4)]
    fade8 = jnp.exp(-il * float(STEP * 8))
    fade16 = jnp.exp(-il * float(STEP * 16))
    whole = 1.0 / (1.0 - jnp.exp(-il * float(NLON)))
    return il, seg_fade, fade8, fade16, whole, sub


def total_gain(il, im):
    one_lon, one_lat = jnp.exp(-il), jnp.exp(-im)
    return (1.0 - one_lon) * (1.0 - one_lon) * ((1.0 - one_lat) / (1.0 + one_lat))


def smooth_kernel(grid, lon_len, local, done, ramp, carry):
    done[0] = 1
    il = 1.0 / in_lanes(lon_len)
    fade = jnp.broadcast_to(jnp.exp(-il), (8, 128))
    stepno = (lax.broadcasted_iota(jnp.int32, (STEP, 128), 0) + 1).astype(jnp.float32)
    ramp[...] = jnp.exp(-stepno * il)
    fades = circle_fades(il)
    vectors = [(i, sv) for i in range(SHARE) for sv in range(SEGV)]

    def at_row(i, sv, t):
        return pl.ds(pl.multiple_of(i * PLANE + sv * (STEP * 8) + t * 8, 8), 8)

    def forward(n, state):
        cells = []
        for u in range(4):
            cells.append([grid[at_row(i, sv, n * 4 + u), :] for i, sv in vectors])
        for u in range(4):
            state = tuple(fade * y + x for y, x in zip(state, cells[u]))
            cells[u] = state
        for u in range(4):
            for (i, sv), y in zip(vectors, cells[u]):
                local[at_row(i, sv, n * 4 + u), :] = y
        return state

    blank = tuple(jnp.zeros((8, 128), jnp.float32) for _ in vectors)
    state = lax.fori_loop(0, STEP // 4, forward, blank)
    for i in range(SHARE):
        for sv, x in enumerate(circle_carry(state[i * SEGV : (i + 1) * SEGV], fades, False)):
            carry[i * SEGV + sv] = x

    def backward(n, state):
        cells = []
        for u in range(4):
            t = STEP - 1 - n * 4 - u
            r = jnp.broadcast_to(ramp[pl.ds(t, 1), :], (8, 128))
            cells.append([local[at_row(i, sv, t), :] + r * carry[k] for k, (i, sv) in enumerate(vectors)])
        for u in range(4):
            state = tuple(fade * y + x for y, x in zip(state, cells[u]))
            cells[u] = state
        for u in range(4):
            for (i, sv), y in zip(vectors, cells[u]):
                local[at_row(i, sv, STEP - 1 - n * 4 - u), :] = y
        return state

    state = lax.fori_loop(0, STEP // 4, backward, blank)
    for i in range(SHARE):
        for sv, x in enumerate(circle_carry(state[i * SEGV : (i + 1) * SEGV], fades, True)):
            carry[i * SEGV + sv] = x

    def finish(n, _):
        cells = []
        for u in range(4):
            r = jnp.broadcast_to(ramp[pl.ds(STEP - 1 - n * 4 - u, 1), :], (8, 128))
            cells.append([local[at_row(i, sv, n * 4 + u), :] + r * carry[k] for k, (i, sv) in enumerate(vectors)])
        for u in range(4):
            for (i, sv), y in zip(vectors, cells[u]):
                local[at_row(i, sv, n * 4 + u), :] = y
        return 0

    lax.fori_loop(0, STEP // 4, finish, 0)


def smooth_band(grid, lon_len):
    return pl.pallas_call(
        smooth_kernel,
        grid=(TILES // SHARE,),
        out_shape=(
            jax.ShapeDtypeStruct((TILES * PLANE, 128), jnp.float32),
            jax.ShapeDtypeStruct((1,), jnp.int32),
        ),
        in_specs=[
            pl.BlockSpec((SHARE * PLANE, 128), lambda n: (n, 0)),
            pl.BlockSpec(memory_space=pltpu.SMEM),
        ],
        out_specs=(
            pl.BlockSpec((SHARE * PLANE, 128), lambda n: (n, 0)),
            pl.BlockSpec(memory_space=pltpu.SMEM),
        ),
        scratch_shapes=[
            pltpu.VMEM((STEP, 128), jnp.float32),
            pltpu.VMEM((SHARE * SEGV, 8, 128), jnp.float32),
        ],
        compiler_params=pltpu.CompilerParams(vmem_limit_bytes=VMEM_LIMIT),
        cost_estimate=pl.CostEstimate(flops=20_000_000, bytes_accessed=9_400_000, transcendentals=0),
        name="smooth_band",
    )(grid, lon_len)


def bands_kernel(ends, lat_len, _, out):
    im = 1.0 / in_lanes(lat_len)
    shape = ends.shape[1:]
    hop = jnp.broadcast_to(jnp.exp(-im * float(BAND)), shape)
    is_up = (blocks_of(shape) & 1) == 1
    acc = jnp.zeros(shape, jnp.float32)
    south = []
    for b in range(BANDS):
        south.append(acc)
        acc = hop * acc + ends[b]
    total = pltpu.roll(acc, PROF, 1)
    acc = jnp.zeros(shape, jnp.float32)
    for b in range(BANDS - 1, -1, -1):
        edge = jnp.exp(-im * float(BAND * (BANDS - 1 - b) + 1))
        out[b] = jnp.where(is_up, acc - edge * total, south[b])
        acc = hop * acc + ends[b]


def join_bands(ends, lat_len, after):
    vmem = pl.BlockSpec(memory_space=pltpu.VMEM)
    return pl.pallas_call(
        bands_kernel,
        out_shape=jax.ShapeDtypeStruct(ends.shape, jnp.float32),
        in_specs=[vmem] + [pl.BlockSpec(memory_space=pltpu.SMEM)] * 2,
        out_specs=vmem,
        compiler_params=pltpu.CompilerParams(vmem_limit_bytes=8 * 1024 * 1024),
        name="join_bands",
    )(ends, lat_len, after)


def turn_kernel(local, control, lon_len, lat_len, out, flipped):
    m = pl.program_id(0)
    for side in range(WIDE):
        sub = (m % (4 // WIDE) * WIDE + side) * 2
        for i in range(TILES):
            x = jnp.concatenate(
                [local[i, pl.ds(sub, STEP, stride=8), :], local[i, pl.ds(sub + 1, STEP, stride=8), :]], axis=0
            )
            flipped[side, i * 128 : (i + 1) * 128, :] = jnp.transpose(x)
    for o in range(0, PROF, 8):
        il = 1.0 / in_rows(lon_len, o)
        im = 1.0 / in_rows(lat_len, o)
        fade = jnp.exp(-im)
        gain = total_gain(il, im)
        for side in range(WIDE):
            x = [flipped[side, n * PROF + o : n * PROF + o + 8, :] for n in range(BAND)]
            south = [x[0]]
            for n in range(1, BAND):
                south.append(fade * south[-1] + x[n])
            north = jnp.zeros((8, 128), jnp.float32)
            for n in range(BAND - 1, -1, -1):
                north = fade * north
                flipped[side, n * PROF + o : n * PROF + o + 8, :] = (south[n] + north) * gain
                north = north + x[n]
    for v in range(PROF):
        for g in range(BAND // 8):
            for side in range(WIDE):
                x = flipped[side, pl.ds(v + 8 * PROF * g, 8, stride=PROF), :]
                f, k, lats, lanes = v // LEVQ, v % LEVQ, slice(8 * g, 8 * g + 8), slice(128 * side, 128 * side + 128)
                out[f, k, lats, lanes] = control[f, k, lats, lanes] + x


def add_control(local, control, lon_len, lat_len):
    block = pl.BlockSpec((F, LEVQ, BAND, 128 * WIDE), lambda m: (0, 0, 0, m))
    smem = pl.BlockSpec(memory_space=pltpu.SMEM)
    return pl.pallas_call(
        turn_kernel,
        grid=(NLON // 128 // WIDE,),
        out_shape=jax.ShapeDtypeStruct(control.shape, jnp.float32),
        in_specs=[
            pl.BlockSpec((TILES, STEP * 8, 128), lambda m: (0, m // (4 // WIDE), 0)),
            block,
            smem,
            smem,
        ],
        out_specs=block,
        scratch_shapes=[pltpu.VMEM((WIDE, BAND * PROF, 128), jnp.float32)],
        compiler_params=pltpu.CompilerParams(vmem_limit_bytes=VMEM_LIMIT),
        cost_estimate=pl.CostEstimate(flops=20_000_000, bytes_accessed=15_000_000, transcendentals=0),
        name="add_control",
    )(local.reshape(TILES, PLANE, 128), control, lon_len, lat_len)


def last_kernel(lat_len, lon_len, parts, joined, out, held, from_start, from_end, ys, south, north, sem):
    half = STEP // 2
    per = LEVQ // 4
    chunks = [(k // 4, pl.ds(k % 4 * per, per)) for k in range(F * 4)]
    fetches = [pltpu.make_async_copy(parts.at[c], held.at[c], sem.at[0, k]) for k, c in enumerate(chunks)]
    stores = [pltpu.make_async_copy(held.at[c], out.at[c], sem.at[1, k]) for k, c in enumerate(chunks)]
    for copy in fetches:
        copy.start()

    lat = lax.broadcasted_iota(jnp.int32, (BAND, 128), 0).astype(jnp.float32)
    for v in range(PROF):
        scale = lat_len[v // LEVQ, v % LEVQ]
        from_start[v] = jnp.exp(-(lat + 1.0) / scale)
        from_end[v] = jnp.exp(-(float(BAND) - lat) / scale)

    il = 1.0 / in_lanes(lon_len)
    im = 1.0 / in_lanes(lat_len)
    fade = jnp.broadcast_to(jnp.exp(-il), (8, 128))
    fades = circle_fades(il)
    half_fade = jnp.broadcast_to(jnp.exp(-il * float(half)), (8, 128))
    first = blocks_of((8, 128)) < 2
    gain = total_gain(il, im)

    def rows_at(sv, p):
        return slice(sv * (half * 8) + p * 8, sv * (half * 8) + p * 8 + 8)

    def enter(last, backward):
        other = [pltpu.roll(x, 64, 1) for x in last]
        early = jnp.logical_not(first) if backward else first
        full = [jnp.where(early, o + half_fade * x, x + half_fade * o) for x, o in zip(last, other)]
        into = circle_carry(full, fades, backward)
        return [jnp.where(early, c, o + half_fade * c) for c, o in zip(into, other)]

    y = [jnp.zeros((8, 128), jnp.float32)] * SEGV
    for p in range(half):
        for sv in range(SEGV):
            y[sv] = fade * y[sv] + joined[rows_at(sv, p), :]
            ys[rows_at(sv, p), :] = y[sv]
    into = enter(y, False)
    y = [jnp.zeros((8, 128), jnp.float32)] * SEGV
    for p in range(half - 1, -1, -1):
        r = jnp.exp(-il * float(p + 1))
        for sv in range(SEGV):
            y[sv] = fade * y[sv] + (ys[rows_at(sv, p), :] + r * into[sv])
            ys[rows_at(sv, p), :] = y[sv]
    into = enter(y, True)
    for p in range(half):
        r = jnp.exp(-il * float(half - p))
        for sv in range(SEGV):
            ys[rows_at(sv, p), :] = (ys[rows_at(sv, p), :] + r * into[sv]) * gain
    for m in range(NLON // 128):
        pieces = []
        for s in (0, 1):
            x = ys[pl.ds(m // 4 * (half * 8) + m % 4 * 2 + s, half, stride=8), :]
            pieces += [x, pltpu.roll(x, 64, 1)]
        x = jnp.transpose(jnp.concatenate(pieces, axis=0))
        south[m] = x[0:PROF]
        north[m] = x[PROF : 2 * PROF]

    for n, fetch in enumerate(fetches):
        fetch.wait()
        for k in range(per):
            v = n * per + k
            f, level = v // LEVQ, v % LEVQ
            up, down = from_start[v], from_end[v]
            for m in range(NLON // 128):
                lanes = slice(m * 128, (m + 1) * 128)
                held[f, level, :, lanes] = held[f, level, :, lanes] + (
                    up * south[m, v : v + 1, :] + down * north[m, v : v + 1, :]
                )
        stores[n].start()
    for copy in stores:
        copy.wait()


def add_bands(lat_len, lon_len, parts, joined):
    smem = pl.BlockSpec(memory_space=pltpu.SMEM)
    vmem = pl.BlockSpec(memory_space=pltpu.VMEM)
    hbm = pl.BlockSpec(memory_space=pltpu.HBM)
    return pl.pallas_call(
        last_kernel,
        out_shape=jax.ShapeDtypeStruct(parts.shape, jnp.float32),
        in_specs=[smem, smem, hbm, vmem],
        out_specs=hbm,
        scratch_shapes=[
            pltpu.VMEM(parts.shape, jnp.float32),
            pltpu.VMEM((PROF, BAND, 128), jnp.float32),
            pltpu.VMEM((PROF, BAND, 128), jnp.float32),
            pltpu.VMEM((NLON // 2, 128), jnp.float32),
            pltpu.VMEM((NLON // 128, PROF, 128), jnp.float32),
            pltpu.VMEM((NLON // 128, PROF, 128), jnp.float32),
            pltpu.SemaphoreType.DMA((2, F * 4)),
        ],
        compiler_params=pltpu.CompilerParams(vmem_limit_bytes=24 * 1024 * 1024),
        input_output_aliases={2: 0},
        name="add_bands",
    )(lat_len, lon_len, parts, joined)


def per_device(control, obs_values, obs_owner, obs_column, sigma, len_lon, len_lat, len_lev):
    owner = obs_owner.reshape(1, -1)
    column = obs_column.reshape(1, -1)
    sigma = sigma.reshape(F * NLEV, NLAT)
    def one_turn(turn):
        messages = make_messages(turn.reshape(1), obs_values, owner, column, sigma, len_lev)
        messages = messages.reshape(BANDS * LEVS, ROWS, 128)
        arrived = lax.all_to_all(messages, ("lat", "lev"), split_axis=0, concat_axis=0, tiled=True)
        ends, grid, most = to_grid(arrived, len_lat)
        return ends, grid, most[0]

    ends, grid, most = one_turn(jnp.int32(0))

    def more(state):
        return state[0] * CAP < most

    def next_turn(state):
        turn, ends, grid = state
        more_ends, more_grid, _ = one_turn(turn)
        return turn + 1, ends + more_ends, grid + more_grid

    _, ends, grid = lax.while_loop(more, next_turn, (jnp.int32(1), ends, grid))

    ends = ends.reshape(BANDS, -1, 128)
    ends = lax.all_to_all(ends, "lat", split_axis=0, concat_axis=0, tiled=True)
    local, done = smooth_band(grid, len_lon)
    joined = join_bands(ends, len_lat, done)
    joined = lax.all_to_all(joined, "lat", split_axis=0, concat_axis=0, tiled=True)
    parts = add_control(local, control, len_lon, len_lat)
    return add_bands(len_lat, len_lon, parts, joined.reshape(NLON // 2, 128))


def solution(mesh):
    placed = (
        P(None, "lev", "lat", None),
        P(("lat", "lev"), None),
        P(("lat", "lev"), None),
        P(("lat", "lev")),
        P(),
        P(None, "lev"),
        P(None, "lev"),
        P(),
    )
    return jax.shard_map(
        per_device,
        mesh=mesh,
        in_specs=placed,
        out_specs=P(None, "lev", "lat", None),
        check_vma=False,
    )
```

```python
import jax
import jax.numpy as jnp
from jax import lax
from jax.experimental import pallas as pl
from jax.experimental.pallas import tpu as pltpu
from jax.sharding import PartitionSpec as P

F = 4
NLEV = 32
NLAT = 768
NLON = 1536
BANDS = 32
LEVS = 4
BAND = NLAT // BANDS
LEVQ = NLEV // LEVS
PROF = F * LEVQ
GROUP = 128 // PROF
ROWS = 32
CAP = (ROWS - 1) * GROUP
COUNT_LANE = 124
MOST_LANE = 125
STEP = 64
SEGV = 3
TILES = BAND // GROUP
PLANE = NLON
VMEM_LIMIT = 58 * 1024 * 1024
PAD = 8
REGION = BAND // 2 * PLANE
GRID_ROWS = REGION + PAD
HALF_CAP = CAP // 2
SWAP_LANE = 126
SAME_LANE = 127
BATCH = 3
SHARE = 2
WIDE = 4
UNROLL = 16
FIRST, NEXT = 18, 6
PARTS = 3
PAIRS = BAND // 2


def third(x):
    return (x * 21846) >> 16


def blocks_of(shape):
    return lax.broadcasted_iota(jnp.int32, shape, len(shape) - 1) // PROF


def in_lanes(lengths):
    value = lax.broadcasted_iota(jnp.int32, (1, 128), 1) & (PROF - 1)
    x = jnp.ones((1, 128), jnp.float32)
    for v in range(PROF):
        x = jnp.where(value == v, lengths[v // LEVQ, v % LEVQ], x)
    return x


def in_rows(lengths, first):
    row = lax.broadcasted_iota(jnp.int32, (8, 128), 0)
    x = jnp.ones((8, 128), jnp.float32)
    for v in range(8):
        x = jnp.where(row == v, lengths[(first + v) // LEVQ, (first + v) % LEVQ], x)
    return x


def send_kernel(
    turn, vals_in, owner, column, sigma_in, len_lev, out, vals, sigma, held, heads, picks, lines, xs, places, sem, io_sem, *more
):
    stage_a, stage_b, work_a, work_b, fades_a, fades_b = more[:6]
    place_s = more[6:]
    rows = vals.shape[0]
    take = pltpu.make_async_copy(vals_in, vals, io_sem.at[0])
    take.start()
    take_sigma = pltpu.make_async_copy(sigma_in, sigma, io_sem.at[1 + BANDS // 8])
    take_sigma.start()
    tiles = rows // 128
    turn_no = turn[0]

    d = owner[...]
    c = column[...]
    c48 = third(c >> 4)
    lat = (d & 3) * 192 + c48
    lon = (d >> 2) * 48 + (c - c48 * 48)
    band = third(lat >> 3)
    seg = lon >> 6
    grid_row = ((seg >> 3) * STEP + (lon & (STEP - 1))) * 8 + (seg & 7)
    odd = lat & 1
    address = ((lat - band * BAND) >> 1) * PLANE + grid_row + PAD

    width = 256
    r0 = lax.broadcasted_iota(jnp.int32, (width, width), 0)
    r1 = lax.broadcasted_iota(jnp.int32, (width, width), 1)
    earlier = jnp.where(r0 < r1, 1.0, 0.0).astype(jnp.bfloat16)
    band_id = lax.broadcasted_iota(jnp.int32, (BANDS, width), 0)
    place_id = lax.broadcasted_iota(jnp.int32, (128, width), 0)
    base = jnp.zeros((BANDS, 1), jnp.float32)
    half_base = jnp.zeros((2 * BANDS, 1), jnp.float32)
    found = jnp.zeros((2 * BANDS, 128), jnp.float32)
    for k in range(rows // width):
        cut = slice(k * width, (k + 1) * width)
        hot = jnp.where(band[:, cut] == band_id, 1.0, 0.0)
        before = jnp.dot(hot.astype(jnp.bfloat16), earlier, preferred_element_type=jnp.float32) + base
        rank = jnp.sum(hot * before, axis=0, keepdims=True).astype(jnp.int32) - turn_no * CAP
        base = base + jnp.sum(hot, axis=1, keepdims=True)
        now = (rank >= 0) & (rank < CAP)
        parity = odd[:, cut]
        hot = jnp.where(now, hot, 0.0)
        sides = jnp.concatenate([jnp.where(parity == 0, hot, 0.0), jnp.where(parity == 1, hot, 0.0)], axis=0)
        before = jnp.dot(sides.astype(jnp.bfloat16), earlier, preferred_element_type=jnp.float32) + half_base
        rank = jnp.sum(sides * before, axis=0, keepdims=True).astype(jnp.int32)
        half_base = half_base + jnp.sum(sides, axis=1, keepdims=True)
        swapped = rank >= HALF_CAP
        pos = jnp.where(swapped, CAP - 1 - rank, rank)
        q = 2 * (pos & 1) + jnp.where(swapped, 1 - parity, parity)
        row = pos >> 1
        slot = jnp.where(now, q * (BANDS * ROWS) + band[:, cut] * ROWS + row, ROWS - 1)
        for g in range(width // 128):
            n = k * (width // 128) + g
            places[n : n + 1, :] = slot[:, g * 128 : (g + 1) * 128]
            places[tiles + n : tiles + n + 1, :] = lat[:, cut][:, g * 128 : (g + 1) * 128]
        a = address[:, cut] + jnp.where(swapped, REGION, 0)
        high = hot * (a >> 8).astype(jnp.float32)
        low = hot * (a & 255).astype(jnp.float32)
        both = jnp.concatenate([high, low], axis=0).astype(jnp.bfloat16)
        at_place = jnp.where(row * GROUP + q == place_id, 1.0, 0.0).astype(jnp.bfloat16)
        found = found + lax.dot_general(
            both, at_place, (((1,), (1,)), ((), ())), preferred_element_type=jnp.float32
        )
    copies = [
        pltpu.make_async_copy(places.at[pl.ds(n, 1), :], place_s[n], sem.at[n]) for n in range(tiles)
    ]
    for copy in copies:
        copy.start()
    headers = found[:BANDS] * 256.0 + found[BANDS:]
    lane = lax.broadcasted_iota(jnp.int32, (BANDS, 128), 1)
    most_side = jnp.maximum(half_base[:BANDS], half_base[BANDS:])
    left = jnp.minimum(2.0 * most_side, float(CAP))
    swaps = jnp.where(most_side > float(HALF_CAP), 1.0, 0.0)
    most = jnp.max(base, axis=0, keepdims=True)
    headers = jnp.where(lane < CAP, headers, 0.0)
    headers = jnp.where(lane == COUNT_LANE, left, headers)
    headers = jnp.where(lane == MOST_LANE, most, headers)
    headers = jnp.where(lane == SWAP_LANE, swaps, headers)
    heads[0] = headers
    place_no = jnp.where(lane < CAP, lane & 3, 1)
    headers = jnp.where(place_no == 2, pltpu.roll(headers, 2, 1), jnp.where(place_no == 0, pltpu.roll(headers, 126, 1), headers))
    heads[1] = headers

    take_sigma.wait()
    sig = sigma[...]
    sig_hi = sig.astype(jnp.bfloat16)
    picks[0:128, :] = sig_hi
    picks[128:256, :] = (sig - sig_hi.astype(jnp.float32)).astype(jnp.bfloat16)
    fade = jnp.exp(-1.0 / len_lev[...])
    fade = jnp.concatenate([fade, fade], axis=0)
    f_hi = fade.astype(jnp.bfloat16).astype(jnp.float32)
    f_mid = (fade - f_hi).astype(jnp.bfloat16).astype(jnp.float32)
    f_lo = fade - f_hi - f_mid
    picks[256:288, :] = jnp.concatenate([f_hi, f_mid, f_lo, jnp.zeros_like(fade)], axis=0).astype(jnp.bfloat16)
    lat_id = lax.broadcasted_iota(jnp.int32, (NLAT, width), 0)

    def pick(k, stage, fades):
        which = jnp.concatenate([places[pl.ds(tiles + 2 * k + g, 1), :] for g in (0, 1)], axis=1)
        at_lat = jnp.where(lat_id == which, 1.0, 0.0).astype(jnp.bfloat16)
        got = jnp.dot(picks[...], at_lat, preferred_element_type=jnp.float32)
        for g in (0, 1):
            lanes = slice(g * 128, (g + 1) * 128)
            at = pl.ds(pl.multiple_of(k * width + g * 128, 128), 128)
            stage[g] = jnp.transpose(vals[at, :]) * (got[0:128, lanes] + got[128:256, lanes])
        fades[...] = got[256:264, :] + got[264:272, :] + got[272:280, :]

    def smooth_levels(k, stage, fades, work):
        for g in (0, 1):
            side = work.at[g]
            a = fades[0:F, g * 128 : (g + 1) * 128]
            y = [stage[g, pl.ds(0, F, stride=NLEV), :]]
            for n in range(1, NLEV):
                y.append(a * y[-1] + stage[g, pl.ds(n, F, stride=NLEV), :])
            gain = (1.0 - a) * (1.0 - a)
            w = y[-1]
            for n in range(NLEV - 1, -1, -1):
                if n < NLEV - 1:
                    w = a * w + y[n]
                side[pl.ds(n // LEVQ * PROF + n % LEVQ, F, stride=LEVQ), :] = w * gain
        for g in (0, 1):
            lines[pl.ds(pl.multiple_of(k * width + g * 128, 128), 128), :] = jnp.transpose(work[g])

    def two_blocks(n, _):
        pick(2 * n + 1, stage_b, fades_b)
        smooth_levels(2 * n, stage_a, fades_a, work_a)
        pick(jnp.minimum(2 * n + 2, rows // width - 1), stage_a, fades_a)
        smooth_levels(2 * n + 1, stage_b, fades_b, work_b)
        return 0

    take.wait()
    pick(0, stage_a, fades_a)
    lax.fori_loop(0, rows // width // 2, two_blocks, 0)

    zeros = jnp.zeros((128, 128), jnp.float32)

    def clear(i, _):
        xs[pl.ds(pl.multiple_of(i * 128, 128), 128), :] = zeros
        return 0

    lax.fori_loop(0, xs.shape[0] // 128, clear, 0)
    for copy in copies:
        copy.wait()

    def place(n, _):
        for u in range(4):
            r = n * 4 + u
            to = [place_s[g][0, r] for g in range(tiles)]
            for g in range(tiles):
                xs[pl.ds(to[g], 1), :] = lines[pl.ds(g * 128 + r, 1), :]
        return 0

    lax.fori_loop(0, 128 // 4, place, 0)

    blk = blocks_of((ROWS, 128))
    even = (blk & 1) == 0
    lower = blk < 2

    def swap(a, b, keep, by):
        turned = pltpu.roll(jnp.where(keep, b, a), by, 1)
        return jnp.where(keep, a, turned), jnp.where(keep, turned, b)

    def first_swap(b):
        x = [xs[pl.ds(pl.multiple_of(q * (BANDS * ROWS) + b * ROWS, ROWS), ROWS), :] for q in range(GROUP)]
        pairs = [swap(x[q], x[q + 2], lower, 64) for q in (0, 1)]
        return [p[0] for p in pairs], [p[1] for p in pairs]

    sends = []
    for part in range(BANDS // 8):
        bands = range(part * 8, part * 8 + 8)
        ahead = first_swap(bands[0])
        for b in bands:
            now = ahead
            if b + 1 in bands:
                ahead = first_swap(b + 1)
            for l, (u, w) in ((0, now[0]), (2, now[1])):
                held[b, l], held[b, l + 1] = swap(u, w, even, 32)
            for l in range(LEVS):
                held[b, l, ROWS - 1 : ROWS, :] = heads[l % 2, b : b + 1, :]
        some = pl.ds(part * 8, 8)
        sends.append(pltpu.make_async_copy(held.at[some], out.at[some], io_sem.at[1 + part]))
        sends[-1].start()
    for copy in sends:
        copy.wait()


def make_messages(turn, vals, owner, column, sigma, len_lev):
    rows = vals.shape[0]
    vmem = pl.BlockSpec(memory_space=pltpu.VMEM)
    hbm = pl.BlockSpec(memory_space=pltpu.HBM)
    return pl.pallas_call(
        send_kernel,
        out_shape=jax.ShapeDtypeStruct((BANDS, LEVS, ROWS, 128), jnp.float32),
        in_specs=[pl.BlockSpec(memory_space=pltpu.SMEM), hbm, vmem, vmem, hbm, vmem],
        out_specs=pl.BlockSpec(memory_space=pltpu.HBM),
        scratch_shapes=[
            pltpu.VMEM((rows, 128), jnp.float32),
            pltpu.VMEM((F * NLEV, NLAT), jnp.float32),
            pltpu.VMEM((BANDS, LEVS, ROWS, 128), jnp.float32),
            pltpu.VMEM((2, BANDS, 128), jnp.float32),
            pltpu.VMEM((288, NLAT), jnp.bfloat16),
            pltpu.VMEM((rows, 128), jnp.float32),
            pltpu.VMEM((GROUP * BANDS * ROWS, 128), jnp.float32),
            pltpu.VMEM((rows // 64, 128), jnp.int32),
            pltpu.SemaphoreType.DMA((rows // 128,)),
            pltpu.SemaphoreType.DMA((2 + BANDS // 8,)),
        ]
        + [pltpu.VMEM((2, 128, 128), jnp.float32)] * 4
        + [pltpu.VMEM((8, 256), jnp.float32)] * 2
        + [pltpu.SMEM((1, 128), jnp.int32)] * (rows // 128),
        compiler_params=pltpu.CompilerParams(vmem_limit_bytes=VMEM_LIMIT),
        name="make_messages",
    )(turn, vals, owner, column, sigma, len_lev)


def fold_lanes(a, b, first, by):
    return jnp.where(first, a, b) + pltpu.roll(jnp.where(first, b, a), by, 1)


def shift_down(x, by, sub):
    return jnp.where(sub >= by, pltpu.roll(x, by, 0), 0.0)


def shift_up(x, by, sub):
    return jnp.where(sub < 8 - by, pltpu.roll(x, 8 - by, 0), 0.0)


def grid_kernel(recv, lat_len, ends, grid, most, ga, gb, ups, downs, ids_v, sem, out_sem, *ids_s):
    heads = recv[:, ROWS - 1, :]
    lane = lax.broadcasted_iota(jnp.int32, (128, 128), 1)
    heads = jnp.where(lane == MOST_LANE, jnp.max(heads, axis=0, keepdims=True), heads)
    ids = jnp.transpose(heads).astype(jnp.int32)
    same = jnp.zeros((8, 128), jnp.bool_)
    for m in range(0, 128, 8):
        a = ids[m : m + 8]
        again = a == pltpu.roll(a, 4, 0)
        if m < 120:
            b = ids[m + 8 : m + 16]
            again = again | (a == b) | (a == pltpu.roll(b, 4, 0))
        same = same | ((a >= PAD) & again)
    same = jnp.max(jnp.where(same, 1, 0), axis=0, keepdims=True)
    ids_v[...] = ids
    count = ids[COUNT_LANE : COUNT_LANE + 1, :]
    ids_v[COUNT_LANE : COUNT_LANE + 1, :] = jnp.maximum(count, pltpu.roll(count, 64, 1))
    care = same + 2 * ids[SWAP_LANE : SWAP_LANE + 1, :]
    ids_v[SAME_LANE : SAME_LANE + 1, :] = jnp.maximum(care, pltpu.roll(care, 64, 1))
    copies = [
        pltpu.make_async_copy(ids_v.at[pl.ds(GROUP * j, GROUP), :], ids_s[j], sem.at[j]) for j in range(ROWS)
    ]
    for copy in copies:
        copy.start()
    zeros = jnp.zeros((256, 128), jnp.float32)

    def clear(i, _):
        at = pl.ds(pl.multiple_of(PAD + i * 256, 8), 256)
        ga[at, :] = zeros
        gb[at, :] = zeros
        return 0

    lax.fori_loop(0, REGION // 256, clear, 0)
    ga[:PAD, :] = zeros[:PAD]
    gb[:PAD, :] = zeros[:PAD]
    for copy in copies:
        copy.wait()
    tail = ids_s[ROWS - 1]
    most[0] = tail[MOST_LANE - CAP, 0]

    lane_block = blocks_of((1, 128))
    masks = [lane_block == q for q in range(GROUP)]
    half = recv.shape[0] // 2

    def add_source(s, _):
        pair = ((s, ga), (s + half, gb))
        n = tail[COUNT_LANE - CAP, s]
        care = tail[SAME_LANE - CAP, s]

        def add_rows(lo, hi, batch):
            items = [(range(j, min(j + batch, hi)), x, g) for j in range(lo, hi, batch) for x, g in pair]

            def read(item):
                js, x, g = item
                at = [[pl.ds(ids_s[j][q, x], 1) for q in range(GROUP)] for j in js]
                return at, [[g[a, :] for a in some] for some in at], [recv[x, j : j + 1, :] for j in js]

            ahead = read(items[0])
            for k, (_, _, g) in enumerate(items):
                at, held, row = ahead
                if k + 1 < len(items):
                    ahead = read(items[k + 1])
                for m in range(len(row)):
                    for q in range(GROUP):
                        pltpu.store(g.at[at[m][q], :], held[m][q] + row[m], mask=masks[q])

        def add_message(batch):
            add_rows(0, FIRST, batch)
            for lo in range(FIRST, ROWS - 1, NEXT):

                @pl.when(n > GROUP * lo)
                def _():
                    add_rows(lo, min(lo + NEXT, ROWS - 1), batch)

        @pl.when(care == 0)
        def _():
            add_message(BATCH)

        @pl.when(care == 1)
        def _():
            add_message(1)

        @pl.when(care > 1)
        def _():
            for x, g in pair:
                for j in range(ROWS - 1):
                    row = recv[x, j : j + 1, :]
                    turned = pltpu.roll(row, PROF, 1)
                    for q in range(GROUP):
                        to = ids_s[j][q, x]
                        far = to >= GRID_ROWS
                        for at, what, mask in (
                            (jnp.where(far, 0, to), row, masks[q]),
                            (jnp.where(far, to - REGION, 0), turned, masks[(q + 1) % GROUP]),
                        ):
                            at = pl.ds(at, 1)
                            pltpu.store(g.at[at, :], g[at, :] + what, mask=mask)

        return 0

    lax.fori_loop(0, half, add_source, 0)

    im = 1.0 / in_lanes(lat_len)

    def power(n):
        return jnp.broadcast_to(jnp.exp(-im * n.astype(jnp.float32)), (8, 128))

    to_end = [power(BAND - 1 - 4 * i - lane_block) for i in range(TILES)]
    to_start = [power(4 * i + lane_block) for i in range(TILES)]
    blk = blocks_of((8, 128))
    even = (blk & 1) == 0
    lower = blk < 2
    out_copies = []
    for part in range(PARTS):

        def gather(r, _):
            rows = [part * (PLANE // PARTS) + (r * UNROLL + u) * 8 for u in range(UNROLL)]

            def fold(row):
                at = [pl.ds(pl.multiple_of(PAD + n * PLANE + row, 8), 8) for n in range(PAIRS)]
                g = [ga[a, :] + gb[a, :] for a in at]
                return [fold_lanes(g[2 * i], g[2 * i + 1], lower, 64) for i in range(TILES)]

            def put(row, cells):
                up = down = None
                for i, x in enumerate(cells):
                    up = to_end[i] * x if i == 0 else up + to_end[i] * x
                    down = to_start[i] * x if i == 0 else down + to_start[i] * x
                for i, x in enumerate(cells):
                    ga[pl.ds(pl.multiple_of(PAD + i * PLANE + row, 8), 8), :] = x
                here = pl.ds(pl.multiple_of(row, 8), 8)
                ups[here, :] = up
                downs[here, :] = down

            ahead = [fold(rows[0]), fold(rows[1])]
            for u, row in enumerate(rows):
                if u + 2 < UNROLL:
                    ahead.append(fold(rows[u + 2]))
                put(row, ahead[u])
            return 0

        lax.fori_loop(0, PLANE // PARTS // 8 // UNROLL, gather, 0)
        for i in range(TILES):
            first = i * PLANE + part * (PLANE // PARTS)
            out_copies.append(
                pltpu.make_async_copy(
                    ga.at[pl.ds(PAD + first, PLANE // PARTS), :],
                    grid.at[pl.ds(first, PLANE // PARTS), :],
                    out_sem.at[part * TILES + i],
                )
            )
            out_copies[-1].start()

    def pack(k, _):
        done = []
        for u in range(16):
            p = k * 16 + u
            row = (p >> 5) * (STEP * 8) + (p & 31) * 8
            sums = []
            for h in (0, 1):
                at = pl.ds(pl.multiple_of(row + h * (STEP * 4), 8), 8)
                sums.append(fold_lanes(ups[at, :], downs[at, :], even, 32))
            done.append(fold_lanes(sums[0], sums[1], lower, 64))
        for u, x in enumerate(done):
            ends[pl.ds(pl.multiple_of((k * 16 + u) * 8, 8), 8), :] = x
        return 0

    lax.fori_loop(0, SEGV * (STEP // 2) // 16, pack, 0)
    for copy in out_copies:
        copy.wait()


def to_grid(recv, lat_len):
    vmem = pl.BlockSpec(memory_space=pltpu.VMEM)
    smem = pl.BlockSpec(memory_space=pltpu.SMEM)
    return pl.pallas_call(
        grid_kernel,
        out_shape=(
            jax.ShapeDtypeStruct((NLON // 2, 128), jnp.float32),
            jax.ShapeDtypeStruct((TILES * PLANE, 128), jnp.float32),
            jax.ShapeDtypeStruct((1,), jnp.int32),
        ),
        in_specs=[vmem, smem],
        out_specs=(vmem, pl.BlockSpec(memory_space=pltpu.HBM), smem),
        scratch_shapes=[
            pltpu.VMEM((GRID_ROWS, 128), jnp.float32),
            pltpu.VMEM((GRID_ROWS, 128), jnp.float32),
            pltpu.VMEM((PLANE, 128), jnp.float32),
            pltpu.VMEM((PLANE, 128), jnp.float32),
            pltpu.VMEM((128, 128), jnp.int32),
            pltpu.SemaphoreType.DMA((ROWS,)),
            pltpu.SemaphoreType.DMA((PARTS * TILES,)),
        ]
        + [pltpu.SMEM((GROUP, 128), jnp.int32)] * ROWS,
        compiler_params=pltpu.CompilerParams(vmem_limit_bytes=32 * 1024 * 1024),
        name="to_grid",
    )(recv, lat_len)


def circle_carry(last, fades, backward):
    il, seg_fade, fade8, fade16, whole, sub = fades
    run, tail = [], []
    for x in last:
        for m, by in enumerate((1, 2, 4)):
            x = x + seg_fade[m] * (shift_up if backward else shift_down)(x, by, sub)
        run.append(x)
        tail.append(x[0:1] if backward else x[7:8])
    entering = []
    for sv in range(SEGV):
        order = [tail[(sv + n) % 3] if backward else tail[(sv - n) % 3] for n in (1, 2, 3)]
        c = (order[0] + fade8 * order[1] + fade16 * order[2]) * whole
        if backward:
            entering.append(shift_up(run[sv], 1, sub) + jnp.exp(-il * (STEP * (7.0 - sub.astype(jnp.float32)))) * c)
        else:
            entering.append(shift_down(run[sv], 1, sub) + jnp.exp(-il * (STEP * sub.astype(jnp.float32))) * c)
    return entering


def circle_fades(il):
    sub = lax.broadcasted_iota(jnp.int32, (8, 128), 0)
    seg_fade = [jnp.broadcast_to(jnp.exp(-il * float(STEP * m)), (8, 128)) for m in (1, 2, 4)]
    fade8 = jnp.exp(-il * float(STEP * 8))
    fade16 = jnp.exp(-il * float(STEP * 16))
    whole = 1.0 / (1.0 - jnp.exp(-il * float(NLON)))
    return il, seg_fade, fade8, fade16, whole, sub


def total_gain(il, im):
    one_lon, one_lat = jnp.exp(-il), jnp.exp(-im)
    return (1.0 - one_lon) * (1.0 - one_lon) * ((1.0 - one_lat) / (1.0 + one_lat))


def smooth_kernel(grid, lon_len, lat_len, local, handed_on, ramp, carry):
    for v in range(PROF):
        handed_on[v // LEVQ, v % LEVQ] = lat_len[v // LEVQ, v % LEVQ]
    il = 1.0 / in_lanes(lon_len)
    fade = jnp.broadcast_to(jnp.exp(-il), (8, 128))
    stepno = (lax.broadcasted_iota(jnp.int32, (STEP, 128), 0) + 1).astype(jnp.float32)
    ramp[...] = jnp.exp(-stepno * il)
    fades = circle_fades(il)
    vectors = [(i, sv) for i in range(SHARE) for sv in range(SEGV)]

    def at_row(i, sv, t):
        return pl.ds(pl.multiple_of(i * PLANE + sv * (STEP * 8) + t * 8, 8), 8)

    def forward(n, state):
        cells = []
        for u in range(4):
            cells.append([grid[at_row(i, sv, n * 4 + u), :] for i, sv in vectors])
        for u in range(4):
            state = tuple(fade * y + x for y, x in zip(state, cells[u]))
            cells[u] = state
        for u in range(4):
            for (i, sv), y in zip(vectors, cells[u]):
                local[at_row(i, sv, n * 4 + u), :] = y
        return state

    blank = tuple(jnp.zeros((8, 128), jnp.float32) for _ in vectors)
    state = lax.fori_loop(0, STEP // 4, forward, blank)
    for i in range(SHARE):
        for sv, x in enumerate(circle_carry(state[i * SEGV : (i + 1) * SEGV], fades, False)):
            carry[i * SEGV + sv] = x

    def backward(n, state):
        cells = []
        for u in range(4):
            t = STEP - 1 - n * 4 - u
            r = jnp.broadcast_to(ramp[pl.ds(t, 1), :], (8, 128))
            cells.append([local[at_row(i, sv, t), :] + r * carry[k] for k, (i, sv) in enumerate(vectors)])
        for u in range(4):
            state = tuple(fade * y + x for y, x in zip(state, cells[u]))
            cells[u] = state
        for u in range(4):
            for (i, sv), y in zip(vectors, cells[u]):
                local[at_row(i, sv, STEP - 1 - n * 4 - u), :] = y
        return state

    state = lax.fori_loop(0, STEP // 4, backward, blank)
    for i in range(SHARE):
        for sv, x in enumerate(circle_carry(state[i * SEGV : (i + 1) * SEGV], fades, True)):
            carry[i * SEGV + sv] = x

    def finish(n, _):
        cells = []
        for u in range(4):
            r = jnp.broadcast_to(ramp[pl.ds(STEP - 1 - n * 4 - u, 1), :], (8, 128))
            cells.append([local[at_row(i, sv, n * 4 + u), :] + r * carry[k] for k, (i, sv) in enumerate(vectors)])
        for u in range(4):
            for (i, sv), y in zip(vectors, cells[u]):
                local[at_row(i, sv, n * 4 + u), :] = y
        return 0

    lax.fori_loop(0, STEP // 4, finish, 0)


def smooth_band(grid, lon_len, lat_len):
    return pl.pallas_call(
        smooth_kernel,
        grid=(TILES // SHARE,),
        out_shape=(
            jax.ShapeDtypeStruct((TILES * PLANE, 128), jnp.float32),
            jax.ShapeDtypeStruct((F, LEVQ), jnp.float32),
        ),
        in_specs=[
            pl.BlockSpec((SHARE * PLANE, 128), lambda n: (n, 0)),
            pl.BlockSpec(memory_space=pltpu.SMEM),
            pl.BlockSpec(memory_space=pltpu.SMEM),
        ],
        out_specs=(
            pl.BlockSpec((SHARE * PLANE, 128), lambda n: (n, 0)),
            pl.BlockSpec(memory_space=pltpu.SMEM),
        ),
        scratch_shapes=[
            pltpu.VMEM((STEP, 128), jnp.float32),
            pltpu.VMEM((SHARE * SEGV, 8, 128), jnp.float32),
        ],
        compiler_params=pltpu.CompilerParams(vmem_limit_bytes=VMEM_LIMIT),
        cost_estimate=pl.CostEstimate(flops=20_000_000, bytes_accessed=9_400_000, transcendentals=0),
        name="smooth_band",
    )(grid, lon_len, lat_len)


def bands_kernel(ends, lat_len, out):
    im = 1.0 / in_lanes(lat_len)
    shape = ends.shape[1:]
    hop = jnp.broadcast_to(jnp.exp(-im * float(BAND)), shape)
    is_up = (blocks_of(shape) & 1) == 1
    acc = jnp.zeros(shape, jnp.float32)
    south = []
    for b in range(BANDS):
        south.append(acc)
        acc = hop * acc + ends[b]
    total = pltpu.roll(acc, PROF, 1)
    acc = jnp.zeros(shape, jnp.float32)
    for b in range(BANDS - 1, -1, -1):
        edge = jnp.exp(-im * float(BAND * (BANDS - 1 - b) + 1))
        out[b] = jnp.where(is_up, acc - edge * total, south[b])
        acc = hop * acc + ends[b]


def join_bands(ends, lat_len):
    vmem = pl.BlockSpec(memory_space=pltpu.VMEM)
    return pl.pallas_call(
        bands_kernel,
        out_shape=jax.ShapeDtypeStruct(ends.shape, jnp.float32),
        in_specs=[vmem, pl.BlockSpec(memory_space=pltpu.SMEM)],
        out_specs=vmem,
        compiler_params=pltpu.CompilerParams(vmem_limit_bytes=8 * 1024 * 1024),
        name="join_bands",
    )(ends, lat_len)


def turn_kernel(local, control, lon_len, lat_len, out, flipped):
    m = pl.program_id(0)
    for side in range(WIDE):
        sub = (m % (4 // WIDE) * WIDE + side) * 2
        for i in range(TILES):
            x = jnp.concatenate(
                [local[i, pl.ds(sub, STEP, stride=8), :], local[i, pl.ds(sub + 1, STEP, stride=8), :]], axis=0
            )
            flipped[side, i * 128 : (i + 1) * 128, :] = jnp.transpose(x)
    for o in range(0, PROF, 8):
        il = 1.0 / in_rows(lon_len, o)
        im = 1.0 / in_rows(lat_len, o)
        fade = jnp.exp(-im)
        gain = total_gain(il, im)
        for side in range(WIDE):
            x = [flipped[side, n * PROF + o : n * PROF + o + 8, :] for n in range(BAND)]
            south = [x[0]]
            for n in range(1, BAND):
                south.append(fade * south[-1] + x[n])
            north = jnp.zeros((8, 128), jnp.float32)
            for n in range(BAND - 1, -1, -1):
                north = fade * north
                flipped[side, n * PROF + o : n * PROF + o + 8, :] = (south[n] + north) * gain
                north = north + x[n]
    for v in range(PROF):
        for g in range(BAND // 8):
            for side in range(WIDE):
                x = flipped[side, pl.ds(v + 8 * PROF * g, 8, stride=PROF), :]
                f, k, lats, lanes = v // LEVQ, v % LEVQ, slice(8 * g, 8 * g + 8), slice(128 * side, 128 * side + 128)
                out[f, k, lats, lanes] = control[f, k, lats, lanes] + x


def add_control(local, control, lon_len, lat_len):
    block = pl.BlockSpec((F, LEVQ, BAND, 128 * WIDE), lambda m: (0, 0, 0, m))
    smem = pl.BlockSpec(memory_space=pltpu.SMEM)
    return pl.pallas_call(
        turn_kernel,
        grid=(NLON // 128 // WIDE,),
        out_shape=jax.ShapeDtypeStruct(control.shape, jnp.float32),
        in_specs=[
            pl.BlockSpec((TILES, STEP * 8, 128), lambda m: (0, m // (4 // WIDE), 0)),
            block,
            smem,
            smem,
        ],
        out_specs=block,
        scratch_shapes=[pltpu.VMEM((WIDE, BAND * PROF, 128), jnp.float32)],
        compiler_params=pltpu.CompilerParams(vmem_limit_bytes=VMEM_LIMIT),
        cost_estimate=pl.CostEstimate(flops=20_000_000, bytes_accessed=15_000_000, transcendentals=0),
        name="add_control",
    )(local.reshape(TILES, PLANE, 128), control, lon_len, lat_len)


def last_kernel(lat_len, lon_len, parts, joined, out, held, from_start, from_end, ys, south, north, sem):
    half = STEP // 2
    per = LEVQ // 4
    chunks = [(k // 4, pl.ds(k % 4 * per, per)) for k in range(F * 4)]
    fetches = [pltpu.make_async_copy(parts.at[c], held.at[c], sem.at[0, k]) for k, c in enumerate(chunks)]
    stores = [pltpu.make_async_copy(held.at[c], out.at[c], sem.at[1, k]) for k, c in enumerate(chunks)]
    for copy in fetches:
        copy.start()

    lat = lax.broadcasted_iota(jnp.int32, (BAND, 128), 0).astype(jnp.float32)
    for v in range(PROF):
        scale = lat_len[v // LEVQ, v % LEVQ]
        from_start[v] = jnp.exp(-(lat + 1.0) / scale)
        from_end[v] = jnp.exp(-(float(BAND) - lat) / scale)

    il = 1.0 / in_lanes(lon_len)
    im = 1.0 / in_lanes(lat_len)
    fade = jnp.broadcast_to(jnp.exp(-il), (8, 128))
    fades = circle_fades(il)
    half_fade = jnp.broadcast_to(jnp.exp(-il * float(half)), (8, 128))
    first = blocks_of((8, 128)) < 2
    gain = total_gain(il, im)

    def rows_at(sv, p):
        return slice(sv * (half * 8) + p * 8, sv * (half * 8) + p * 8 + 8)

    def enter(last, backward):
        other = [pltpu.roll(x, 64, 1) for x in last]
        early = jnp.logical_not(first) if backward else first
        full = [jnp.where(early, o + half_fade * x, x + half_fade * o) for x, o in zip(last, other)]
        into = circle_carry(full, fades, backward)
        return [jnp.where(early, c, o + half_fade * c) for c, o in zip(into, other)]

    y = [jnp.zeros((8, 128), jnp.float32)] * SEGV
    for p in range(half):
        for sv in range(SEGV):
            y[sv] = fade * y[sv] + joined[rows_at(sv, p), :]
            ys[rows_at(sv, p), :] = y[sv]
    into = enter(y, False)
    y = [jnp.zeros((8, 128), jnp.float32)] * SEGV
    for p in range(half - 1, -1, -1):
        r = jnp.exp(-il * float(p + 1))
        for sv in range(SEGV):
            y[sv] = fade * y[sv] + (ys[rows_at(sv, p), :] + r * into[sv])
            ys[rows_at(sv, p), :] = y[sv]
    into = enter(y, True)
    for p in range(half):
        r = jnp.exp(-il * float(half - p))
        for sv in range(SEGV):
            ys[rows_at(sv, p), :] = (ys[rows_at(sv, p), :] + r * into[sv]) * gain
    for m in range(NLON // 128):
        pieces = []
        for s in (0, 1):
            x = ys[pl.ds(m // 4 * (half * 8) + m % 4 * 2 + s, half, stride=8), :]
            pieces += [x, pltpu.roll(x, 64, 1)]
        x = jnp.transpose(jnp.concatenate(pieces, axis=0))
        south[m] = x[0:PROF]
        north[m] = x[PROF : 2 * PROF]

    for n, fetch in enumerate(fetches):
        fetch.wait()
        for k in range(per):
            v = n * per + k
            f, level = v // LEVQ, v % LEVQ
            up, down = from_start[v], from_end[v]
            for m in range(NLON // 128):
                lanes = slice(m * 128, (m + 1) * 128)
                held[f, level, :, lanes] = held[f, level, :, lanes] + (
                    up * south[m, v : v + 1, :] + down * north[m, v : v + 1, :]
                )
        stores[n].start()
    for copy in stores:
        copy.wait()


def add_bands(lat_len, lon_len, parts, joined):
    smem = pl.BlockSpec(memory_space=pltpu.SMEM)
    vmem = pl.BlockSpec(memory_space=pltpu.VMEM)
    hbm = pl.BlockSpec(memory_space=pltpu.HBM)
    return pl.pallas_call(
        last_kernel,
        out_shape=jax.ShapeDtypeStruct(parts.shape, jnp.float32),
        in_specs=[smem, smem, hbm, vmem],
        out_specs=hbm,
        scratch_shapes=[
            pltpu.VMEM(parts.shape, jnp.float32),
            pltpu.VMEM((PROF, BAND, 128), jnp.float32),
            pltpu.VMEM((PROF, BAND, 128), jnp.float32),
            pltpu.VMEM((NLON // 2, 128), jnp.float32),
            pltpu.VMEM((NLON // 128, PROF, 128), jnp.float32),
            pltpu.VMEM((NLON // 128, PROF, 128), jnp.float32),
            pltpu.SemaphoreType.DMA((2, F * 4)),
        ],
        compiler_params=pltpu.CompilerParams(vmem_limit_bytes=24 * 1024 * 1024),
        input_output_aliases={2: 0},
        name="add_bands",
    )(lat_len, lon_len, parts, joined)


def per_device(control, obs_values, obs_owner, obs_column, sigma, len_lon, len_lat, len_lev):
    owner = obs_owner.reshape(1, -1)
    column = obs_column.reshape(1, -1)
    sigma = sigma.reshape(F * NLEV, NLAT)
    def one_turn(turn):
        messages = make_messages(turn.reshape(1), obs_values, owner, column, sigma, len_lev)
        messages = messages.reshape(BANDS * LEVS, ROWS, 128)
        arrived = lax.all_to_all(messages, ("lat", "lev"), split_axis=0, concat_axis=0, tiled=True)
        ends, grid, most = to_grid(arrived, len_lat)
        return ends, grid, most[0]

    ends, grid, most = one_turn(jnp.int32(0))

    def more(state):
        return state[0] * CAP < most

    def next_turn(state):
        turn, ends, grid = state
        more_ends, more_grid, _ = one_turn(turn)
        return turn + 1, ends + more_ends, grid + more_grid

    _, ends, grid = lax.while_loop(more, next_turn, (jnp.int32(1), ends, grid))

    ends = ends.reshape(BANDS, -1, 128)
    ends = lax.all_to_all(ends, "lat", split_axis=0, concat_axis=0, tiled=True)
    local, lengths = smooth_band(grid, len_lon, len_lat)
    joined = join_bands(ends, lengths)
    joined = lax.all_to_all(joined, "lat", split_axis=0, concat_axis=0, tiled=True)
    parts = add_control(local, control, len_lon, len_lat)
    return add_bands(len_lat, len_lon, parts, joined.reshape(NLON // 2, 128))


def solution(mesh):
    placed = (
        P(None, "lev", "lat", None),
        P(("lat", "lev"), None),
        P(("lat", "lev"), None),
        P(("lat", "lev")),
        P(),
        P(None, "lev"),
        P(None, "lev"),
        P(),
    )
    return jax.shard_map(
        per_device,
        mesh=mesh,
        in_specs=placed,
        out_specs=P(None, "lev", "lat", None),
        check_vma=False,
    )
```

```python
import jax
import jax.numpy as jnp
from jax import lax
from jax.experimental import pallas as pl
from jax.experimental.pallas import tpu as pltpu
from jax.sharding import PartitionSpec as P

F = 4
NLEV = 32
NLAT = 768
NLON = 1536
BANDS = 32
LEVS = 4
BAND = NLAT // BANDS
LEVQ = NLEV // LEVS
PROF = F * LEVQ
GROUP = 128 // PROF
ROWS = 32
CAP = (ROWS - 1) * GROUP
COUNT_LANE = 124
MOST_LANE = 125
STEP = 64
SEGV = 3
TILES = BAND // GROUP
PLANE = NLON
VMEM_LIMIT = 58 * 1024 * 1024
PAD = 8
REGION = BAND // 2 * PLANE
GRID_ROWS = REGION + PAD
HALF_CAP = CAP // 2
SWAP_LANE = 126
SAME_LANE = 127
BATCH = 3
SHARE = 2
WIDE = 4
UNROLL = 32
FIRST, NEXT = 18, 6
PARTS = 3
PAIRS = BAND // 2


def third(x):
    return (x * 21846) >> 16


def blocks_of(shape):
    return lax.broadcasted_iota(jnp.int32, shape, len(shape) - 1) // PROF


def in_lanes(lengths):
    value = lax.broadcasted_iota(jnp.int32, (1, 128), 1) & (PROF - 1)
    x = jnp.ones((1, 128), jnp.float32)
    for v in range(PROF):
        x = jnp.where(value == v, lengths[v // LEVQ, v % LEVQ], x)
    return x


def in_rows(lengths, first):
    row = lax.broadcasted_iota(jnp.int32, (8, 128), 0)
    x = jnp.ones((8, 128), jnp.float32)
    for v in range(8):
        x = jnp.where(row == v, lengths[(first + v) // LEVQ, (first + v) % LEVQ], x)
    return x


def send_kernel(
    turn, vals_in, owner, column, sigma_in, len_lev, out, vals, sigma, held, heads, picks, lines, xs, places, sem, io_sem, *more
):
    stage_a, stage_b, work_a, work_b, fades_a, fades_b = more[:6]
    place_s = more[6:]
    rows = vals.shape[0]
    take = pltpu.make_async_copy(vals_in, vals, io_sem.at[0])
    take.start()
    take_sigma = pltpu.make_async_copy(sigma_in, sigma, io_sem.at[1 + BANDS // 8])
    take_sigma.start()
    tiles = rows // 128
    turn_no = turn[0]

    d = owner[...]
    c = column[...]
    c48 = third(c >> 4)
    lat = (d & 3) * 192 + c48
    lon = (d >> 2) * 48 + (c - c48 * 48)
    band = third(lat >> 3)
    seg = lon >> 6
    grid_row = ((seg >> 3) * STEP + (lon & (STEP - 1))) * 8 + (seg & 7)
    odd = lat & 1
    address = ((lat - band * BAND) >> 1) * PLANE + grid_row + PAD

    width = 256
    r0 = lax.broadcasted_iota(jnp.int32, (width, width), 0)
    r1 = lax.broadcasted_iota(jnp.int32, (width, width), 1)
    earlier = jnp.where(r0 < r1, 1.0, 0.0).astype(jnp.bfloat16)
    band_id = lax.broadcasted_iota(jnp.int32, (BANDS, width), 0)
    place_id = lax.broadcasted_iota(jnp.int32, (128, width), 0)
    base = jnp.zeros((BANDS, 1), jnp.float32)
    half_base = jnp.zeros((2 * BANDS, 1), jnp.float32)
    found = jnp.zeros((2 * BANDS, 128), jnp.float32)
    for k in range(rows // width):
        cut = slice(k * width, (k + 1) * width)
        hot = jnp.where(band[:, cut] == band_id, 1.0, 0.0)
        before = jnp.dot(hot.astype(jnp.bfloat16), earlier, preferred_element_type=jnp.float32) + base
        rank = jnp.sum(hot * before, axis=0, keepdims=True).astype(jnp.int32) - turn_no * CAP
        base = base + jnp.sum(hot, axis=1, keepdims=True)
        now = (rank >= 0) & (rank < CAP)
        parity = odd[:, cut]
        hot = jnp.where(now, hot, 0.0)
        sides = jnp.concatenate([jnp.where(parity == 0, hot, 0.0), jnp.where(parity == 1, hot, 0.0)], axis=0)
        before = jnp.dot(sides.astype(jnp.bfloat16), earlier, preferred_element_type=jnp.float32) + half_base
        rank = jnp.sum(sides * before, axis=0, keepdims=True).astype(jnp.int32)
        half_base = half_base + jnp.sum(sides, axis=1, keepdims=True)
        swapped = rank >= HALF_CAP
        pos = jnp.where(swapped, CAP - 1 - rank, rank)
        q = 2 * (pos & 1) + jnp.where(swapped, 1 - parity, parity)
        row = pos >> 1
        slot = jnp.where(now, q * (BANDS * ROWS) + band[:, cut] * ROWS + row, ROWS - 1)
        for g in range(width // 128):
            n = k * (width // 128) + g
            places[n : n + 1, :] = slot[:, g * 128 : (g + 1) * 128]
            places[tiles + n : tiles + n + 1, :] = lat[:, cut][:, g * 128 : (g + 1) * 128]
        a = address[:, cut] + jnp.where(swapped, REGION, 0)
        high = hot * (a >> 8).astype(jnp.float32)
        low = hot * (a & 255).astype(jnp.float32)
        both = jnp.concatenate([high, low], axis=0).astype(jnp.bfloat16)
        at_place = jnp.where(row * GROUP + q == place_id, 1.0, 0.0).astype(jnp.bfloat16)
        found = found + lax.dot_general(
            both, at_place, (((1,), (1,)), ((), ())), preferred_element_type=jnp.float32
        )
    copies = [
        pltpu.make_async_copy(places.at[pl.ds(n, 1), :], place_s[n], sem.at[n]) for n in range(tiles)
    ]
    for copy in copies:
        copy.start()
    headers = found[:BANDS] * 256.0 + found[BANDS:]
    lane = lax.broadcasted_iota(jnp.int32, (BANDS, 128), 1)
    most_side = jnp.maximum(half_base[:BANDS], half_base[BANDS:])
    left = jnp.minimum(2.0 * most_side, float(CAP))
    swaps = jnp.where(most_side > float(HALF_CAP), 1.0, 0.0)
    most = jnp.max(base, axis=0, keepdims=True)
    headers = jnp.where(lane < CAP, headers, 0.0)
    headers = jnp.where(lane == COUNT_LANE, left, headers)
    headers = jnp.where(lane == MOST_LANE, most, headers)
    headers = jnp.where(lane == SWAP_LANE, swaps, headers)
    heads[0] = headers
    place_no = jnp.where(lane < CAP, lane & 3, 1)
    headers = jnp.where(place_no == 2, pltpu.roll(headers, 2, 1), jnp.where(place_no == 0, pltpu.roll(headers, 126, 1), headers))
    heads[1] = headers

    take_sigma.wait()
    sig = sigma[...]
    sig_hi = sig.astype(jnp.bfloat16)
    picks[0:128, :] = sig_hi
    picks[128:256, :] = (sig - sig_hi.astype(jnp.float32)).astype(jnp.bfloat16)
    fade = jnp.exp(-1.0 / len_lev[...])
    fade = jnp.concatenate([fade, fade], axis=0)
    f_hi = fade.astype(jnp.bfloat16).astype(jnp.float32)
    f_mid = (fade - f_hi).astype(jnp.bfloat16).astype(jnp.float32)
    f_lo = fade - f_hi - f_mid
    picks[256:288, :] = jnp.concatenate([f_hi, f_mid, f_lo, jnp.zeros_like(fade)], axis=0).astype(jnp.bfloat16)
    lat_id = lax.broadcasted_iota(jnp.int32, (NLAT, width), 0)

    def pick(k, stage, fades):
        which = jnp.concatenate([places[pl.ds(tiles + 2 * k + g, 1), :] for g in (0, 1)], axis=1)
        at_lat = jnp.where(lat_id == which, 1.0, 0.0).astype(jnp.bfloat16)
        got = jnp.dot(picks[...], at_lat, preferred_element_type=jnp.float32)
        for g in (0, 1):
            lanes = slice(g * 128, (g + 1) * 128)
            at = pl.ds(pl.multiple_of(k * width + g * 128, 128), 128)
            stage[g] = jnp.transpose(vals[at, :]) * (got[0:128, lanes] + got[128:256, lanes])
        fades[...] = got[256:264, :] + got[264:272, :] + got[272:280, :]

    def smooth_levels(k, stage, fades, work):
        for g in (0, 1):
            side = work.at[g]
            a = fades[0:F, g * 128 : (g + 1) * 128]
            y = [stage[g, pl.ds(0, F, stride=NLEV), :]]
            for n in range(1, NLEV):
                y.append(a * y[-1] + stage[g, pl.ds(n, F, stride=NLEV), :])
            gain = (1.0 - a) * (1.0 - a)
            w = y[-1]
            for n in range(NLEV - 1, -1, -1):
                if n < NLEV - 1:
                    w = a * w + y[n]
                side[pl.ds(n // LEVQ * PROF + n % LEVQ, F, stride=LEVQ), :] = w * gain
        for g in (0, 1):
            lines[pl.ds(pl.multiple_of(k * width + g * 128, 128), 128), :] = jnp.transpose(work[g])

    def two_blocks(n, _):
        pick(2 * n + 1, stage_b, fades_b)
        smooth_levels(2 * n, stage_a, fades_a, work_a)
        pick(jnp.minimum(2 * n + 2, rows // width - 1), stage_a, fades_a)
        smooth_levels(2 * n + 1, stage_b, fades_b, work_b)
        return 0

    take.wait()
    pick(0, stage_a, fades_a)
    lax.fori_loop(0, rows // width // 2, two_blocks, 0)

    zeros = jnp.zeros((128, 128), jnp.float32)

    def clear(i, _):
        xs[pl.ds(pl.multiple_of(i * 128, 128), 128), :] = zeros
        return 0

    lax.fori_loop(0, xs.shape[0] // 128, clear, 0)
    for copy in copies:
        copy.wait()

    def place(n, _):
        for u in range(4):
            r = n * 4 + u
            to = [place_s[g][0, r] for g in range(tiles)]
            for g in range(tiles):
                xs[pl.ds(to[g], 1), :] = lines[pl.ds(g * 128 + r, 1), :]
        return 0

    lax.fori_loop(0, 128 // 4, place, 0)

    blk = blocks_of((ROWS, 128))
    even = (blk & 1) == 0
    lower = blk < 2

    def swap(a, b, keep, by):
        turned = pltpu.roll(jnp.where(keep, b, a), by, 1)
        return jnp.where(keep, a, turned), jnp.where(keep, turned, b)

    def first_swap(b):
        x = [xs[pl.ds(pl.multiple_of(q * (BANDS * ROWS) + b * ROWS, ROWS), ROWS), :] for q in range(GROUP)]
        pairs = [swap(x[q], x[q + 2], lower, 64) for q in (0, 1)]
        return [p[0] for p in pairs], [p[1] for p in pairs]

    sends = []
    for part in range(BANDS // 8):
        bands = range(part * 8, part * 8 + 8)
        ahead = first_swap(bands[0])
        for b in bands:
            now = ahead
            if b + 1 in bands:
                ahead = first_swap(b + 1)
            for l, (u, w) in ((0, now[0]), (2, now[1])):
                held[b, l], held[b, l + 1] = swap(u, w, even, 32)
            for l in range(LEVS):
                held[b, l, ROWS - 1 : ROWS, :] = heads[l % 2, b : b + 1, :]
        some = pl.ds(part * 8, 8)
        sends.append(pltpu.make_async_copy(held.at[some], out.at[some], io_sem.at[1 + part]))
        sends[-1].start()
    for copy in sends:
        copy.wait()


def make_messages(turn, vals, owner, column, sigma, len_lev):
    rows = vals.shape[0]
    vmem = pl.BlockSpec(memory_space=pltpu.VMEM)
    hbm = pl.BlockSpec(memory_space=pltpu.HBM)
    return pl.pallas_call(
        send_kernel,
        out_shape=jax.ShapeDtypeStruct((BANDS, LEVS, ROWS, 128), jnp.float32),
        in_specs=[pl.BlockSpec(memory_space=pltpu.SMEM), hbm, vmem, vmem, hbm, vmem],
        out_specs=pl.BlockSpec(memory_space=pltpu.HBM),
        scratch_shapes=[
            pltpu.VMEM((rows, 128), jnp.float32),
            pltpu.VMEM((F * NLEV, NLAT), jnp.float32),
            pltpu.VMEM((BANDS, LEVS, ROWS, 128), jnp.float32),
            pltpu.VMEM((2, BANDS, 128), jnp.float32),
            pltpu.VMEM((288, NLAT), jnp.bfloat16),
            pltpu.VMEM((rows, 128), jnp.float32),
            pltpu.VMEM((GROUP * BANDS * ROWS, 128), jnp.float32),
            pltpu.VMEM((rows // 64, 128), jnp.int32),
            pltpu.SemaphoreType.DMA((rows // 128,)),
            pltpu.SemaphoreType.DMA((2 + BANDS // 8,)),
        ]
        + [pltpu.VMEM((2, 128, 128), jnp.float32)] * 4
        + [pltpu.VMEM((8, 256), jnp.float32)] * 2
        + [pltpu.SMEM((1, 128), jnp.int32)] * (rows // 128),
        compiler_params=pltpu.CompilerParams(vmem_limit_bytes=VMEM_LIMIT),
        name="make_messages",
    )(turn, vals, owner, column, sigma, len_lev)


def fold_lanes(a, b, first, by):
    return jnp.where(first, a, b) + pltpu.roll(jnp.where(first, b, a), by, 1)


def shift_down(x, by, sub):
    return jnp.where(sub >= by, pltpu.roll(x, by, 0), 0.0)


def shift_up(x, by, sub):
    return jnp.where(sub < 8 - by, pltpu.roll(x, 8 - by, 0), 0.0)


def grid_kernel(recv, lat_len, ends, grid, most, ga, gb, ups, downs, ids_v, sem, out_sem, *ids_s):
    heads = recv[:, ROWS - 1, :]
    lane = lax.broadcasted_iota(jnp.int32, (128, 128), 1)
    heads = jnp.where(lane == MOST_LANE, jnp.max(heads, axis=0, keepdims=True), heads)
    ids = jnp.transpose(heads).astype(jnp.int32)
    same = jnp.zeros((8, 128), jnp.bool_)
    for m in range(0, 128, 8):
        a = ids[m : m + 8]
        again = a == pltpu.roll(a, 4, 0)
        if m < 120:
            b = ids[m + 8 : m + 16]
            again = again | (a == b) | (a == pltpu.roll(b, 4, 0))
        same = same | ((a >= PAD) & again)
    same = jnp.max(jnp.where(same, 1, 0), axis=0, keepdims=True)
    ids_v[...] = ids
    count = ids[COUNT_LANE : COUNT_LANE + 1, :]
    ids_v[COUNT_LANE : COUNT_LANE + 1, :] = jnp.maximum(count, pltpu.roll(count, 64, 1))
    care = same + 2 * ids[SWAP_LANE : SWAP_LANE + 1, :]
    ids_v[SAME_LANE : SAME_LANE + 1, :] = jnp.maximum(care, pltpu.roll(care, 64, 1))
    copies = [
        pltpu.make_async_copy(ids_v.at[pl.ds(GROUP * j, GROUP), :], ids_s[j], sem.at[j]) for j in range(ROWS)
    ]
    for copy in copies:
        copy.start()
    zeros = jnp.zeros((256, 128), jnp.float32)

    def clear(i, _):
        at = pl.ds(pl.multiple_of(PAD + i * 256, 8), 256)
        ga[at, :] = zeros
        gb[at, :] = zeros
        return 0

    lax.fori_loop(0, REGION // 256, clear, 0)
    ga[:PAD, :] = zeros[:PAD]
    gb[:PAD, :] = zeros[:PAD]
    for copy in copies:
        copy.wait()
    tail = ids_s[ROWS - 1]
    most[0] = tail[MOST_LANE - CAP, 0]

    lane_block = blocks_of((1, 128))
    masks = [lane_block == q for q in range(GROUP)]
    half = recv.shape[0] // 2

    def add_source(s, _):
        pair = ((s, ga), (s + half, gb))
        n = tail[COUNT_LANE - CAP, s]
        care = tail[SAME_LANE - CAP, s]

        def add_rows(lo, hi, batch):
            items = [(range(j, min(j + batch, hi)), x, g) for j in range(lo, hi, batch) for x, g in pair]

            def read(item):
                js, x, g = item
                at = [[pl.ds(ids_s[j][q, x], 1) for q in range(GROUP)] for j in js]
                return at, [[g[a, :] for a in some] for some in at], [recv[x, j : j + 1, :] for j in js]

            ahead = read(items[0])
            for k, (_, _, g) in enumerate(items):
                at, held, row = ahead
                if k + 1 < len(items):
                    ahead = read(items[k + 1])
                for m in range(len(row)):
                    for q in range(GROUP):
                        pltpu.store(g.at[at[m][q], :], held[m][q] + row[m], mask=masks[q])

        def add_message(batch):
            add_rows(0, FIRST, batch)
            for lo in range(FIRST, ROWS - 1, NEXT):

                @pl.when(n > GROUP * lo)
                def _():
                    add_rows(lo, min(lo + NEXT, ROWS - 1), batch)

        @pl.when(care == 0)
        def _():
            add_message(BATCH)

        @pl.when(care == 1)
        def _():
            add_message(1)

        @pl.when(care > 1)
        def _():
            for x, g in pair:
                for j in range(ROWS - 1):
                    row = recv[x, j : j + 1, :]
                    turned = pltpu.roll(row, PROF, 1)
                    for q in range(GROUP):
                        to = ids_s[j][q, x]
                        far = to >= GRID_ROWS
                        for at, what, mask in (
                            (jnp.where(far, 0, to), row, masks[q]),
                            (jnp.where(far, to - REGION, 0), turned, masks[(q + 1) % GROUP]),
                        ):
                            at = pl.ds(at, 1)
                            pltpu.store(g.at[at, :], g[at, :] + what, mask=mask)

        return 0

    lax.fori_loop(0, half, add_source, 0)

    im = 1.0 / in_lanes(lat_len)

    def power(n):
        return jnp.broadcast_to(jnp.exp(-im * n.astype(jnp.float32)), (8, 128))

    to_end = [power(BAND - 1 - 4 * i - lane_block) for i in range(TILES)]
    to_start = [power(4 * i + lane_block) for i in range(TILES)]
    blk = blocks_of((8, 128))
    even = (blk & 1) == 0
    lower = blk < 2
    out_copies = []
    for part in range(PARTS):

        def gather(r, _):
            rows = [part * (PLANE // PARTS) + (r * UNROLL + u) * 8 for u in range(UNROLL)]

            def fold(row):
                at = [pl.ds(pl.multiple_of(PAD + n * PLANE + row, 8), 8) for n in range(PAIRS)]
                g = [ga[a, :] + gb[a, :] for a in at]
                return [fold_lanes(g[2 * i], g[2 * i + 1], lower, 64) for i in range(TILES)]

            def put(row, cells):
                up = down = None
                for i, x in enumerate(cells):
                    up = to_end[i] * x if i == 0 else up + to_end[i] * x
                    down = to_start[i] * x if i == 0 else down + to_start[i] * x
                for i, x in enumerate(cells):
                    ga[pl.ds(pl.multiple_of(PAD + i * PLANE + row, 8), 8), :] = x
                here = pl.ds(pl.multiple_of(row, 8), 8)
                ups[here, :] = up
                downs[here, :] = down

            ahead = [fold(rows[0]), fold(rows[1])]
            for u, row in enumerate(rows):
                if u + 2 < UNROLL:
                    ahead.append(fold(rows[u + 2]))
                put(row, ahead[u])
            return 0

        lax.fori_loop(0, PLANE // PARTS // 8 // UNROLL, gather, 0)
        for i in range(TILES):
            first = i * PLANE + part * (PLANE // PARTS)
            out_copies.append(
                pltpu.make_async_copy(
                    ga.at[pl.ds(PAD + first, PLANE // PARTS), :],
                    grid.at[pl.ds(first, PLANE // PARTS), :],
                    out_sem.at[part * TILES + i],
                )
            )
            out_copies[-1].start()

    def pack(k, _):
        done = []
        for u in range(16):
            p = k * 16 + u
            row = (p >> 5) * (STEP * 8) + (p & 31) * 8
            sums = []
            for h in (0, 1):
                at = pl.ds(pl.multiple_of(row + h * (STEP * 4), 8), 8)
                sums.append(fold_lanes(ups[at, :], downs[at, :], even, 32))
            done.append(fold_lanes(sums[0], sums[1], lower, 64))
        for u, x in enumerate(done):
            ends[pl.ds(pl.multiple_of((k * 16 + u) * 8, 8), 8), :] = x
        return 0

    lax.fori_loop(0, SEGV * (STEP // 2) // 16, pack, 0)
    for copy in out_copies:
        copy.wait()


def to_grid(recv, lat_len):
    vmem = pl.BlockSpec(memory_space=pltpu.VMEM)
    smem = pl.BlockSpec(memory_space=pltpu.SMEM)
    return pl.pallas_call(
        grid_kernel,
        out_shape=(
            jax.ShapeDtypeStruct((NLON // 2, 128), jnp.float32),
            jax.ShapeDtypeStruct((TILES * PLANE, 128), jnp.float32),
            jax.ShapeDtypeStruct((1,), jnp.int32),
        ),
        in_specs=[vmem, smem],
        out_specs=(vmem, pl.BlockSpec(memory_space=pltpu.HBM), smem),
        scratch_shapes=[
            pltpu.VMEM((GRID_ROWS, 128), jnp.float32),
            pltpu.VMEM((GRID_ROWS, 128), jnp.float32),
            pltpu.VMEM((PLANE, 128), jnp.float32),
            pltpu.VMEM((PLANE, 128), jnp.float32),
            pltpu.VMEM((128, 128), jnp.int32),
            pltpu.SemaphoreType.DMA((ROWS,)),
            pltpu.SemaphoreType.DMA((PARTS * TILES,)),
        ]
        + [pltpu.SMEM((GROUP, 128), jnp.int32)] * ROWS,
        compiler_params=pltpu.CompilerParams(vmem_limit_bytes=32 * 1024 * 1024),
        name="to_grid",
    )(recv, lat_len)


def circle_carry(last, fades, backward):
    il, seg_fade, fade8, fade16, whole, sub = fades
    run, tail = [], []
    for x in last:
        for m, by in enumerate((1, 2, 4)):
            x = x + seg_fade[m] * (shift_up if backward else shift_down)(x, by, sub)
        run.append(x)
        tail.append(x[0:1] if backward else x[7:8])
    entering = []
    for sv in range(SEGV):
        order = [tail[(sv + n) % 3] if backward else tail[(sv - n) % 3] for n in (1, 2, 3)]
        c = (order[0] + fade8 * order[1] + fade16 * order[2]) * whole
        if backward:
            entering.append(shift_up(run[sv], 1, sub) + jnp.exp(-il * (STEP * (7.0 - sub.astype(jnp.float32)))) * c)
        else:
            entering.append(shift_down(run[sv], 1, sub) + jnp.exp(-il * (STEP * sub.astype(jnp.float32))) * c)
    return entering


def circle_fades(il):
    sub = lax.broadcasted_iota(jnp.int32, (8, 128), 0)
    seg_fade = [jnp.broadcast_to(jnp.exp(-il * float(STEP * m)), (8, 128)) for m in (1, 2, 4)]
    fade8 = jnp.exp(-il * float(STEP * 8))
    fade16 = jnp.exp(-il * float(STEP * 16))
    whole = 1.0 / (1.0 - jnp.exp(-il * float(NLON)))
    return il, seg_fade, fade8, fade16, whole, sub


def total_gain(il, im):
    one_lon, one_lat = jnp.exp(-il), jnp.exp(-im)
    return (1.0 - one_lon) * (1.0 - one_lon) * ((1.0 - one_lat) / (1.0 + one_lat))


def smooth_kernel(grid, lon_len, lat_len, local, handed_on, ramp, carry):
    for v in range(PROF):
        handed_on[v // LEVQ, v % LEVQ] = lat_len[v // LEVQ, v % LEVQ]
    il = 1.0 / in_lanes(lon_len)
    fade = jnp.broadcast_to(jnp.exp(-il), (8, 128))
    stepno = (lax.broadcasted_iota(jnp.int32, (STEP, 128), 0) + 1).astype(jnp.float32)
    ramp[...] = jnp.exp(-stepno * il)
    fades = circle_fades(il)
    vectors = [(i, sv) for i in range(SHARE) for sv in range(SEGV)]

    def at_row(i, sv, t):
        return pl.ds(pl.multiple_of(i * PLANE + sv * (STEP * 8) + t * 8, 8), 8)

    def forward(n, state):
        cells = []
        for u in range(4):
            cells.append([grid[at_row(i, sv, n * 4 + u), :] for i, sv in vectors])
        for u in range(4):
            state = tuple(fade * y + x for y, x in zip(state, cells[u]))
            cells[u] = state
        for u in range(4):
            for (i, sv), y in zip(vectors, cells[u]):
                local[at_row(i, sv, n * 4 + u), :] = y
        return state

    blank = tuple(jnp.zeros((8, 128), jnp.float32) for _ in vectors)
    state = lax.fori_loop(0, STEP // 4, forward, blank)
    for i in range(SHARE):
        for sv, x in enumerate(circle_carry(state[i * SEGV : (i + 1) * SEGV], fades, False)):
            carry[i * SEGV + sv] = x

    def backward(n, state):
        cells = []
        for u in range(4):
            t = STEP - 1 - n * 4 - u
            r = jnp.broadcast_to(ramp[pl.ds(t, 1), :], (8, 128))
            cells.append([local[at_row(i, sv, t), :] + r * carry[k] for k, (i, sv) in enumerate(vectors)])
        for u in range(4):
            state = tuple(fade * y + x for y, x in zip(state, cells[u]))
            cells[u] = state
        for u in range(4):
            for (i, sv), y in zip(vectors, cells[u]):
                local[at_row(i, sv, STEP - 1 - n * 4 - u), :] = y
        return state

    state = lax.fori_loop(0, STEP // 4, backward, blank)
    for i in range(SHARE):
        for sv, x in enumerate(circle_carry(state[i * SEGV : (i + 1) * SEGV], fades, True)):
            carry[i * SEGV + sv] = x

    def finish(n, _):
        cells = []
        for u in range(4):
            r = jnp.broadcast_to(ramp[pl.ds(STEP - 1 - n * 4 - u, 1), :], (8, 128))
            cells.append([local[at_row(i, sv, n * 4 + u), :] + r * carry[k] for k, (i, sv) in enumerate(vectors)])
        for u in range(4):
            for (i, sv), y in zip(vectors, cells[u]):
                local[at_row(i, sv, n * 4 + u), :] = y
        return 0

    lax.fori_loop(0, STEP // 4, finish, 0)


def smooth_band(grid, lon_len, lat_len):
    return pl.pallas_call(
        smooth_kernel,
        grid=(TILES // SHARE,),
        out_shape=(
            jax.ShapeDtypeStruct((TILES * PLANE, 128), jnp.float32),
            jax.ShapeDtypeStruct((F, LEVQ), jnp.float32),
        ),
        in_specs=[
            pl.BlockSpec((SHARE * PLANE, 128), lambda n: (n, 0)),
            pl.BlockSpec(memory_space=pltpu.SMEM),
            pl.BlockSpec(memory_space=pltpu.SMEM),
        ],
        out_specs=(
            pl.BlockSpec((SHARE * PLANE, 128), lambda n: (n, 0)),
            pl.BlockSpec(memory_space=pltpu.SMEM),
        ),
        scratch_shapes=[
            pltpu.VMEM((STEP, 128), jnp.float32),
            pltpu.VMEM((SHARE * SEGV, 8, 128), jnp.float32),
        ],
        compiler_params=pltpu.CompilerParams(vmem_limit_bytes=VMEM_LIMIT),
        cost_estimate=pl.CostEstimate(flops=20_000_000, bytes_accessed=9_400_000, transcendentals=0),
        name="smooth_band",
    )(grid, lon_len, lat_len)


def bands_kernel(ends, lat_len, out):
    im = 1.0 / in_lanes(lat_len)
    shape = ends.shape[1:]
    hop = jnp.broadcast_to(jnp.exp(-im * float(BAND)), shape)
    is_up = (blocks_of(shape) & 1) == 1
    acc = jnp.zeros(shape, jnp.float32)
    south = []
    for b in range(BANDS):
        south.append(acc)
        acc = hop * acc + ends[b]
    total = pltpu.roll(acc, PROF, 1)
    acc = jnp.zeros(shape, jnp.float32)
    for b in range(BANDS - 1, -1, -1):
        edge = jnp.exp(-im * float(BAND * (BANDS - 1 - b) + 1))
        out[b] = jnp.where(is_up, acc - edge * total, south[b])
        acc = hop * acc + ends[b]


def join_bands(ends, lat_len):
    vmem = pl.BlockSpec(memory_space=pltpu.VMEM)
    return pl.pallas_call(
        bands_kernel,
        out_shape=jax.ShapeDtypeStruct(ends.shape, jnp.float32),
        in_specs=[vmem, pl.BlockSpec(memory_space=pltpu.SMEM)],
        out_specs=vmem,
        compiler_params=pltpu.CompilerParams(vmem_limit_bytes=8 * 1024 * 1024),
        name="join_bands",
    )(ends, lat_len)


def turn_kernel(local, control, lon_len, lat_len, out, flipped):
    m = pl.program_id(0)
    for side in range(WIDE):
        sub = (m % (4 // WIDE) * WIDE + side) * 2
        for i in range(TILES):
            x = jnp.concatenate(
                [local[i, pl.ds(sub, STEP, stride=8), :], local[i, pl.ds(sub + 1, STEP, stride=8), :]], axis=0
            )
            flipped[side, i * 128 : (i + 1) * 128, :] = jnp.transpose(x)
    for o in range(0, PROF, 8):
        il = 1.0 / in_rows(lon_len, o)
        im = 1.0 / in_rows(lat_len, o)
        fade = jnp.exp(-im)
        gain = total_gain(il, im)
        for side in range(WIDE):
            x = [flipped[side, n * PROF + o : n * PROF + o + 8, :] for n in range(BAND)]
            south = [x[0]]
            for n in range(1, BAND):
                south.append(fade * south[-1] + x[n])
            north = jnp.zeros((8, 128), jnp.float32)
            for n in range(BAND - 1, -1, -1):
                north = fade * north
                flipped[side, n * PROF + o : n * PROF + o + 8, :] = (south[n] + north) * gain
                north = north + x[n]
    for v in range(PROF):
        for g in range(BAND // 8):
            for side in range(WIDE):
                x = flipped[side, pl.ds(v + 8 * PROF * g, 8, stride=PROF), :]
                f, k, lats, lanes = v // LEVQ, v % LEVQ, slice(8 * g, 8 * g + 8), slice(128 * side, 128 * side + 128)
                out[f, k, lats, lanes] = control[f, k, lats, lanes] + x


def add_control(local, control, lon_len, lat_len):
    block = pl.BlockSpec((F, LEVQ, BAND, 128 * WIDE), lambda m: (0, 0, 0, m))
    smem = pl.BlockSpec(memory_space=pltpu.SMEM)
    return pl.pallas_call(
        turn_kernel,
        grid=(NLON // 128 // WIDE,),
        out_shape=jax.ShapeDtypeStruct(control.shape, jnp.float32),
        in_specs=[
            pl.BlockSpec((TILES, STEP * 8, 128), lambda m: (0, m // (4 // WIDE), 0)),
            block,
            smem,
            smem,
        ],
        out_specs=block,
        scratch_shapes=[pltpu.VMEM((WIDE, BAND * PROF, 128), jnp.float32)],
        compiler_params=pltpu.CompilerParams(vmem_limit_bytes=VMEM_LIMIT),
        cost_estimate=pl.CostEstimate(flops=20_000_000, bytes_accessed=15_000_000, transcendentals=0),
        name="add_control",
    )(local.reshape(TILES, PLANE, 128), control, lon_len, lat_len)


def last_kernel(lat_len, lon_len, parts, joined, out, held, from_start, from_end, ys, south, north, sem):
    half = STEP // 2
    per = LEVQ // 2
    chunks = [(k // 2, pl.ds(k % 2 * per, per)) for k in range(F * 2)]
    fetches = [pltpu.make_async_copy(parts.at[c], held.at[c], sem.at[0, k]) for k, c in enumerate(chunks)]
    stores = [pltpu.make_async_copy(held.at[c], out.at[c], sem.at[1, k]) for k, c in enumerate(chunks)]
    for copy in fetches:
        copy.start()

    lat = lax.broadcasted_iota(jnp.int32, (BAND, 128), 0).astype(jnp.float32)
    for v in range(PROF):
        scale = lat_len[v // LEVQ, v % LEVQ]
        from_start[v] = jnp.exp(-(lat + 1.0) / scale)
        from_end[v] = jnp.exp(-(float(BAND) - lat) / scale)

    il = 1.0 / in_lanes(lon_len)
    im = 1.0 / in_lanes(lat_len)
    fade = jnp.broadcast_to(jnp.exp(-il), (8, 128))
    fades = circle_fades(il)
    half_fade = jnp.broadcast_to(jnp.exp(-il * float(half)), (8, 128))
    first = blocks_of((8, 128)) < 2
    gain = total_gain(il, im)

    def rows_at(sv, p):
        return slice(sv * (half * 8) + p * 8, sv * (half * 8) + p * 8 + 8)

    def enter(last, backward):
        other = [pltpu.roll(x, 64, 1) for x in last]
        early = jnp.logical_not(first) if backward else first
        full = [jnp.where(early, o + half_fade * x, x + half_fade * o) for x, o in zip(last, other)]
        into = circle_carry(full, fades, backward)
        return [jnp.where(early, c, o + half_fade * c) for c, o in zip(into, other)]

    y = [jnp.zeros((8, 128), jnp.float32)] * SEGV
    for p in range(half):
        for sv in range(SEGV):
            y[sv] = fade * y[sv] + joined[rows_at(sv, p), :]
            ys[rows_at(sv, p), :] = y[sv]
    into = enter(y, False)
    y = [jnp.zeros((8, 128), jnp.float32)] * SEGV
    for p in range(half - 1, -1, -1):
        r = jnp.exp(-il * float(p + 1))
        for sv in range(SEGV):
            y[sv] = fade * y[sv] + (ys[rows_at(sv, p), :] + r * into[sv])
            ys[rows_at(sv, p), :] = y[sv]
    into = enter(y, True)
    for p in range(half):
        r = jnp.exp(-il * float(half - p))
        for sv in range(SEGV):
            ys[rows_at(sv, p), :] = (ys[rows_at(sv, p), :] + r * into[sv]) * gain
    for m in range(NLON // 128):
        pieces = []
        for s in (0, 1):
            x = ys[pl.ds(m // 4 * (half * 8) + m % 4 * 2 + s, half, stride=8), :]
            pieces += [x, pltpu.roll(x, 64, 1)]
        x = jnp.transpose(jnp.concatenate(pieces, axis=0))
        south[m] = x[0:PROF]
        north[m] = x[PROF : 2 * PROF]

    for n, fetch in enumerate(fetches):
        fetch.wait()
        for k in range(per):
            v = n * per + k
            f, level = v // LEVQ, v % LEVQ
            up, down = from_start[v], from_end[v]
            for m in range(NLON // 128):
                lanes = slice(m * 128, (m + 1) * 128)
                held[f, level, :, lanes] = held[f, level, :, lanes] + (
                    up * south[m, v : v + 1, :] + down * north[m, v : v + 1, :]
                )
        stores[n].start()
    for copy in stores:
        copy.wait()


def add_bands(lat_len, lon_len, parts, joined):
    smem = pl.BlockSpec(memory_space=pltpu.SMEM)
    vmem = pl.BlockSpec(memory_space=pltpu.VMEM)
    hbm = pl.BlockSpec(memory_space=pltpu.HBM)
    return pl.pallas_call(
        last_kernel,
        out_shape=jax.ShapeDtypeStruct(parts.shape, jnp.float32),
        in_specs=[smem, smem, hbm, vmem],
        out_specs=hbm,
        scratch_shapes=[
            pltpu.VMEM(parts.shape, jnp.float32),
            pltpu.VMEM((PROF, BAND, 128), jnp.float32),
            pltpu.VMEM((PROF, BAND, 128), jnp.float32),
            pltpu.VMEM((NLON // 2, 128), jnp.float32),
            pltpu.VMEM((NLON // 128, PROF, 128), jnp.float32),
            pltpu.VMEM((NLON // 128, PROF, 128), jnp.float32),
            pltpu.SemaphoreType.DMA((2, F * 2)),
        ],
        compiler_params=pltpu.CompilerParams(vmem_limit_bytes=24 * 1024 * 1024),
        input_output_aliases={2: 0},
        name="add_bands",
    )(lat_len, lon_len, parts, joined)


def per_device(control, obs_values, obs_owner, obs_column, sigma, len_lon, len_lat, len_lev):
    owner = obs_owner.reshape(1, -1)
    column = obs_column.reshape(1, -1)
    sigma = sigma.reshape(F * NLEV, NLAT)
    def one_turn(turn):
        messages = make_messages(turn.reshape(1), obs_values, owner, column, sigma, len_lev)
        messages = messages.reshape(BANDS * LEVS, ROWS, 128)
        arrived = lax.all_to_all(messages, ("lat", "lev"), split_axis=0, concat_axis=0, tiled=True)
        ends, grid, most = to_grid(arrived, len_lat)
        return ends, grid, most[0]

    ends, grid, most = one_turn(jnp.int32(0))

    def more(state):
        return state[0] * CAP < most

    def next_turn(state):
        turn, ends, grid = state
        more_ends, more_grid, _ = one_turn(turn)
        return turn + 1, ends + more_ends, grid + more_grid

    _, ends, grid = lax.while_loop(more, next_turn, (jnp.int32(1), ends, grid))

    ends = ends.reshape(BANDS, -1, 128)
    ends = lax.all_to_all(ends, "lat", split_axis=0, concat_axis=0, tiled=True)
    local, lengths = smooth_band(grid, len_lon, len_lat)
    joined = join_bands(ends, lengths)
    joined = lax.all_to_all(joined, "lat", split_axis=0, concat_axis=0, tiled=True)
    parts = add_control(local, control, len_lon, len_lat)
    return add_bands(len_lat, len_lon, parts, joined.reshape(NLON // 2, 128))


def solution(mesh):
    placed = (
        P(None, "lev", "lat", None),
        P(("lat", "lev"), None),
        P(("lat", "lev"), None),
        P(("lat", "lev")),
        P(),
        P(None, "lev"),
        P(None, "lev"),
        P(),
    )
    return jax.shard_map(
        per_device,
        mesh=mesh,
        in_specs=placed,
        out_specs=P(None, "lev", "lat", None),
        check_vma=False,
    )
```
